256 devices in a mesh: story: 32 (over x, z_lo, core), plan: 8 (over z_hi, y).
Axes of the slice: x: 4, y: 4, z: 8 (z_hi: 2, z_lo: 4; z = z_hi * 4 + z_lo), core: 2. Of those that a mesh axis runs over, the one named last changes fastest.
Arguments:
- u_now: float32 [3, 512, 128, 256], P(None, 'story', 'plan'), may hold values from -6 to 6
- u_prev: float32 [3, 512, 128, 256], P(None, 'story', 'plan'), may hold values from -6 to 6
- occupancy: int32 [32, 8, 16], P('story', 'plan'), may hold values 0 or 1
- materials: int32 [32, 8, 16], P('story', 'plan'), may hold values from 0 to 7
- shear_table: float32 [8], replicated, may hold values from 0.5 to 1.5
- lame_table: float32 [8], replicated, may hold values from 0.3 to 1.5
- density_table: float32 [8], replicated, may hold values from 0.8 to 1.2
Outputs:
- u_final: float32 [3, 512, 128, 256], P(None, 'story', 'plan')
The draws below stay inside these ranges and needn't reach their ends.
All inputs are finite; a program needn't handle non-finite values. No bound on the sum of `occupancy` on one device may be relied on, other than what follows from the above.
Results may differ from the reference program's by a relative error of at most 0.0003.
Values sent between devices are 32-bit elements; how exact they have to be, the bound alone decides.
No kernel may reach another device: no remote copies, remote signals or barrier semaphores. Data moves between devices by JAX's collectives and lax.ppermute only.
A program may use at most 128 MiB of HBM per device.

```python
import math
import jax
import jax.numpy as jnp
from jax import lax

BLOCK = 16
BY = 16
MATS = 8
STEPS = 2
NZB = 32
NXB = 8
NZ = 512
NX = 128
NY = 256


def touch_ends(drawn, own_key, least, largest):
    longest = drawn.shape.index(max(drawn.shape))
    spots = []
    for shift in (0, 1):
        where = [jax.random.randint(jax.random.fold_in(own_key, axis), (), 0, length) for axis, length in enumerate(drawn.shape)]
        where[longest] = (where[longest] + shift) % drawn.shape[longest]
        spots.append(tuple(where))
    return drawn.at[spots[0]].set(least).at[spots[1]].set(largest)


def steps_of(key, dims, split, least, high):
    def one(dim, parts):
        draws = jax.random.uniform(jax.random.fold_in(jax.random.fold_in(key, 6), dim), (parts,), jnp.float32, least / len(split), high / len(split))
        return jnp.repeat(jnp.exp(draws), dims[dim] // parts).reshape((-1,) + (1,) * (len(dims) - dim - 1))

    factor_of = one(*split[0])
    for cut in split[1:]:
        factor_of = factor_of * one(*cut)
    return factor_of


def normal_values(own_key, extent, scale, bound, pieces=(), kind=jnp.bfloat16):
    loudness = steps_of(own_key, extent, pieces, -0.22, 0.18) if pieces else 1.0
    array = jax.random.normal(own_key, extent, jnp.float32) * scale * loudness
    return jnp.minimum(jnp.maximum(array, -bound), bound).astype(kind)


def setup_inputs(seed: int = 0) -> dict:
    key_list = jax.random.split(jax.random.key(seed), 8)
    u_now = normal_values(key_list[0], (3, NZ, NX, NY), 1.0, 6.0, ((1, 32), (2, 8)), jnp.float32)
    u_prev = normal_values(key_list[1], (3, NZ, NX, NY), 1.0, 6.0, ((1, 32), (2, 8)), jnp.float32)
    occupancy = touch_ends((jax.random.randint(key_list[2], (NZB, NXB, BY), 0, 4) < 3).astype(jnp.int32), jax.random.fold_in(key_list[2], 1), 0, 1)
    materials = touch_ends(jax.random.randint(key_list[3], (NZB, NXB, BY), 0, MATS), jax.random.fold_in(key_list[3], 1), 0, MATS - 1).astype(jnp.int32)
    shear_table = jnp.clip(jnp.exp(jax.random.uniform(key_list[4], (MATS,), jnp.float32, math.log(0.5), math.log(1.5))), 0.5, 1.5)
    lame_table = jnp.clip(jax.random.uniform(key_list[5], (MATS,), jnp.float32, 0.3, 1.5), 0.3, 1.5)
    density_table = jnp.clip(jax.random.uniform(key_list[6], (MATS,), jnp.float32, 0.8, 1.2), 0.8, 1.2)
    return dict(u_now=u_now, u_prev=u_prev, occupancy=occupancy, materials=materials, shear_table=shear_table, lame_table=lame_table, density_table=density_table)


def filter_axis(values, axis, kind):
    count = values.shape[axis] - 2
    lower = lax.slice_in_dim(values, 0, count, axis=axis)
    middle = lax.slice_in_dim(values, 1, count + 1, axis=axis)
    upper = lax.slice_in_dim(values, 2, count + 2, axis=axis)
    if kind == "second":
        return lower - 2.0 * middle + upper
    if kind == "first":
        return (upper - lower) * 0.5
    return (lower + 4.0 * middle + upper) / 6.0


def derivatives(field):
    z_smooth = filter_axis(field, 0, "smooth")
    z_second = filter_axis(field, 0, "second")
    z_first = filter_axis(field, 0, "first")
    zs_xs = filter_axis(z_smooth, 1, "smooth")
    zs_xsecond = filter_axis(z_smooth, 1, "second")
    zs_xfirst = filter_axis(z_smooth, 1, "first")
    zsecond_xs = filter_axis(z_second, 1, "smooth")
    zfirst_xs = filter_axis(z_first, 1, "smooth")
    zfirst_xfirst = filter_axis(z_first, 1, "first")
    d_zz = filter_axis(zsecond_xs, 2, "smooth")
    d_xx = filter_axis(zs_xsecond, 2, "smooth")
    d_yy = filter_axis(zs_xs, 2, "second")
    d_zx = filter_axis(zfirst_xfirst, 2, "smooth")
    d_zy = filter_axis(zfirst_xs, 2, "first")
    d_xy = filter_axis(zs_xfirst, 2, "first")
    return ((d_zz, d_zx, d_zy), (d_zx, d_xx, d_xy), (d_zy, d_xy, d_yy))


def stiffness(padded, shear, lame, faces_load):
    tables = [derivatives(padded[index]) for index in range(3)]
    forces = []
    for comp_i in range(3):
        own = tables[comp_i]
        laplace = own[0][0] + own[1][1] + own[2][2]
        coupled = tables[0][comp_i][0] + tables[1][comp_i][1] + tables[2][comp_i][2]
        centre = padded[comp_i][:, 1:-1, 1:-1]
        upper_diff = centre[2:] - centre[1:-1]
        lower_diff = centre[1:-1] - centre[:-2]
        geometric = faces_load[1:] * upper_diff - faces_load[:-1] * lower_diff
        forces.append(shear * laplace + (lame + shear) * coupled - geometric)
    return jnp.stack(forces)


def expand(values, width):
    zcount, xcount, ycount = values.shape
    spread = jnp.broadcast_to(values[:, None, :, None, :, None], (zcount, width, xcount, width, ycount, width))
    return spread.reshape(zcount * width, xcount * width, ycount * width)


def lookup(materials, table):
    onehot = (materials[..., None] == jnp.arange(table.shape[0], dtype=jnp.int32)).astype(jnp.float32)
    return jnp.sum(onehot * table.astype(jnp.float32), -1)


def reference(u_now, u_prev, occupancy, materials, shear_table, lame_table, density_table):
    occupied = expand(occupancy.astype(jnp.float32), BLOCK)
    shear = expand(lookup(materials, shear_table), BLOCK)
    lame = expand(lookup(materials, lame_table), BLOCK)
    density = expand(lookup(materials, density_table), BLOCK)
    mass = density * occupied
    above = jnp.cumsum(mass[::-1], axis=0)[::-1]
    faces_load = (0.8 / NZ) * jnp.concatenate([above, jnp.zeros((1, NX, NY), jnp.float32)], 0)
    earlier = occupied * u_prev
    current = occupied * u_now
    for section in range(STEPS):
        padded = jnp.pad(current, ((0, 0), (1, 1), (1, 1), (1, 1)))

        def slab(index):
            start = (index * BLOCK).astype(jnp.int32)
            piece = lax.dynamic_slice_in_dim(padded, start, BLOCK + 2, 1)
            shear_part = lax.dynamic_slice_in_dim(shear, start, BLOCK, 0)
            lame_part = lax.dynamic_slice_in_dim(lame, start, BLOCK, 0)
            load_part = lax.dynamic_slice_in_dim(faces_load, start, BLOCK + 1, 0)
            return stiffness(piece, shear_part, lame_part, load_part)

        forces = lax.map(slab, jnp.arange(NZ // BLOCK, dtype=jnp.int32))
        forces = jnp.transpose(forces, (1, 0, 2, 3, 4)).reshape(3, NZ, NX, NY)
        following = occupied * (2.0 * current - earlier + 0.1 * forces / density)
        earlier = current
        current = following
    return current
```

```python
import functools

import jax
import jax.numpy as jnp
from jax import lax
from jax.experimental import pallas as pl
from jax.experimental.pallas import tpu as pltpu
from jax.sharding import PartitionSpec as P

BLOCK = 16
WIDE = 256
PAD = 24
F32 = jnp.float32


def swap(values, axis, first):
    pairs = []
    for low in range(first, lax.axis_size(axis) - 1, 2):
        pairs += [(low, low + 1), (low + 1, low)]
    return lax.ppermute(values, axis, pairs)


def row_shift(v):
    rows = v.shape[0]
    return pltpu.roll(v, 1, 0), pltpu.roll(v, rows - 1, 0)


def lane_shift(v):
    lane = lax.broadcasted_iota(jnp.int32, v.shape, 1)
    lower = jnp.where(lane == 0, 0.0, pltpu.roll(v, 1, 1))
    upper = jnp.where(lane == WIDE - 1, 0.0, pltpu.roll(v, WIDE - 1, 1))
    return lower, upper


def lane_smooth(v):
    lower, upper = lane_shift(v)
    return lower + upper + 4.0 * v


def lane_first(v):
    lower, upper = lane_shift(v)
    return upper - lower


def stencil(below, here, above, sign=None):
    zs = [lo + up + 4.0 * mid for lo, mid, up in zip(below, here, above)]
    zf = [up - lo for lo, up in zip(below, above)]
    if sign is not None:
        zf = [sign * v for v in zf]
    zs_sh = [row_shift(v) for v in zs]
    zf_sh = [row_shift(v) for v in zf]
    mid_sh = [row_shift(v) for v in here]
    s_zs = [lo + up + 4.0 * v for (lo, up), v in zip(zs_sh, zs)]
    s_mid = [lo + up + 4.0 * v for (lo, up), v in zip(mid_sh, here)]
    lap = []
    for j in range(3):
        inner = s_zs[j] - 2.0 * (s_mid[j] + zs[j])
        lap.append(lane_smooth(inner) - 2.0 * s_zs[j])
    f_zf0 = zf_sh[0][1] - zf_sh[0][0]
    f_zf1 = zf_sh[1][1] - zf_sh[1][0]
    s_zf0 = zf_sh[0][0] + zf_sh[0][1] + 4.0 * zf[0]
    s_zf2 = zf_sh[2][0] + zf_sh[2][1] + 4.0 * zf[2]
    f_zs1 = zs_sh[1][1] - zs_sh[1][0]
    f_zs2 = zs_sh[2][1] - zs_sh[2][0]
    c0 = lane_smooth(2.0 * s_zs[0] - 12.0 * s_mid[0] + 3.0 * f_zf1) + lane_first(3.0 * s_zf2)
    c1 = lane_smooth(2.0 * s_zs[1] - 12.0 * zs[1] + 3.0 * f_zf0) + lane_first(3.0 * f_zs2)
    c2 = lane_first(3.0 * (s_zf0 + f_zs1)) + 2.0 * lane_smooth(s_zs[2]) - 12.0 * s_zs[2]
    return lap, [c0, c1, c2]


def coefficients(own, over, under, carried):
    z = lax.broadcasted_iota(jnp.int32, (PAD, WIDE), 0) - 4
    zf = z.astype(F32)

    def pick(k):
        return jnp.where(z < 0, under[k], jnp.where(z > 15, over[k], own[k]))

    a, b, g = pick(0), pick(1), pick(2)
    mass, mass_over, mass_under = own[3], over[3], under[3]
    upper = jnp.where(z > 15, carried - mass_over, carried + mass * (15.0 - zf))
    lower = jnp.where(z < 0, carried + 16.0 * mass + mass_under, carried + mass * (16.0 - zf))
    return a, b, g * upper, g * lower


def prep_kernel(place, occ, mat, shear_t, lame_t, dens_t, now, prev, se, so, masses, consts, held_now, held_prev, sems, *, factor):
    top_first = place[0] % 2 == 0
    copies = []
    for k in range(2):
        top = jnp.logical_xor(top_first, k == 1)
        copies.append(pltpu.make_async_copy(now.at[:, pl.ds(jnp.where(top, 14, 0), 2)], held_now.at[k], sems.at[2 * k]))
        copies.append(pltpu.make_async_copy(prev.at[:, pl.ds(jnp.where(top, 15, 0), 1)], held_prev.at[k], sems.at[2 * k + 1]))
    for copy in copies:
        copy.start()
    block = lax.broadcasted_iota(jnp.int32, (1, WIDE), 1) // BLOCK
    zero = jnp.zeros((1, WIDE), F32)
    occupied, shear, lame, dens = zero, zero, zero, zero
    for j in range(BLOCK):
        at = block == j
        which = mat[j]
        occupied = jnp.where(at, occ[j].astype(F32), occupied)
        shear = jnp.where(at, shear_t[which], shear)
        lame = jnp.where(at, lame_t[which], lame)
        dens = jnp.where(at, dens_t[which], dens)
    scale = occupied * (0.1 / dens)
    own = [scale * shear * (1.0 / 12.0), scale * (lame + shear) * (1.0 / 72.0), scale * factor, dens * occupied, occupied]
    for k, row in enumerate(own):
        consts[k : k + 1, :] = row
    consts[5:8, :] = jnp.zeros((3, WIDE), F32)
    masses[...] = jnp.broadcast_to(own[3], masses.shape)
    for copy in copies:
        copy.wait()
    for k, out in enumerate((se, so)):
        top = jnp.logical_xor(top_first, k == 1)
        for c in range(3):
            first, second = held_now[k, c, 0] * occupied, held_now[k, c, 1] * occupied
            out[c] = jnp.where(top, second, first)
            out[3 + c] = jnp.where(top, first, second)
            out[6 + c] = held_prev[k, c, 0] * occupied
        out[9, 0:8] = consts[...]


def pack_kernel(place, consts, se, so, masses, now, prev, pe, po, carried_out):
    even_story = place[0] % 2 == 0
    step = lax.broadcasted_iota(jnp.int32, masses.shape, 0)
    carried = 16.0 * jnp.sum(jnp.where(step > place[0], masses[...], 0.0), 0, keepdims=True)
    carried_out[...] = jnp.broadcast_to(carried, carried_out.shape)
    occupied = consts[4:5, :]

    def ghost(plane, x, over):
        take = even_story if over else jnp.logical_not(even_story)
        return jnp.where(take, se[plane, x : x + 1, :], so[plane, x : x + 1, :])

    def fill(out, near, far):
        for c in range(3):
            for kind, source, x in ((0, now, near), (3, now, far), (6, prev, near)):
                plane = kind + c
                base = plane * PAD
                out[base + 4 : base + 20, :] = source[c, :, x, :] * occupied
                if kind < 6:
                    out[base + 3 : base + 4, :] = ghost(c, x, False)
                    out[base + 2 : base + 3, :] = ghost(3 + c, x, False)
                    out[base + 20 : base + 21, :] = ghost(c, x, True)
                    out[base + 21 : base + 22, :] = ghost(3 + c, x, True)
                else:
                    out[base + 3 : base + 4, :] = ghost(6 + c, x, False)
                    out[base + 20 : base + 21, :] = ghost(6 + c, x, True)
        rows = (0, 1, 22, 23)
        for k, r in enumerate(rows):
            out[r : r + 1, :] = consts[k : k + 1, :]
            out[PAD + r : PAD + r + 1, :] = ghost(9, k, True)
            out[2 * PAD + r : 2 * PAD + r + 1, :] = ghost(9, k, False)
        out[3 * PAD : 3 * PAD + 1, :] = carried

    even_plan = place[1] % 2 == 0
    pe[...] = jnp.zeros(pe.shape, F32)
    po[...] = jnp.zeros(po.shape, F32)

    @pl.when(even_plan)
    def _():
        fill(pe, 15, 14)
        fill(po, 0, 1)

    @pl.when(jnp.logical_not(even_plan))
    def _():
        fill(pe, 0, 1)
        fill(po, 15, 14)


def pack_coefficients(pack):
    rows = (0, 1, 22, 23)
    sets = [[pack[k * PAD + r : k * PAD + r + 1, :] for r in rows] for k in range(3)]
    return coefficients(sets[0], sets[1], sets[2], pack[3 * PAD : 3 * PAD + 1, :])


def update(here, before, lap, coup, a, b, gu, gd, below, above):
    geometric = gu * (above - here) - gd * (here - below)
    return 2.0 * here - before + a * lap + b * coup - geometric


def main_kernel(place, consts, carried, se, so, now, prev, out, edge, u0, u1, before, coef):
    even_story = place[0] % 2 == 0

    def ghost(plane, over):
        take = even_story if over else jnp.logical_not(even_story)
        return jnp.where(take, se[plane], so[plane])

    own = [consts[k : k + 1, :] for k in range(4)]
    over_plane, under_plane = ghost(9, True), ghost(9, False)
    over = [over_plane[k : k + 1, :] for k in range(4)]
    under = [under_plane[k : k + 1, :] for k in range(4)]
    for k, rows in enumerate(coefficients(own, over, under, carried[0:1, :])):
        coef[k] = rows
    occupied = jnp.broadcast_to(consts[4:5, :], (16, WIDE))
    for c in range(3):
        u0[c, 0] = ghost(3 + c, False)
        u0[c, 1] = ghost(c, False)
        u0[c, 18] = ghost(c, True)
        u0[c, 19] = ghost(3 + c, True)
        before[c, 0] = ghost(6 + c, False)
        before[c, 17] = ghost(6 + c, True)

    @pl.loop(0, 16)
    def _(z):
        for c in range(3):
            u0[c, z + 2] = now[c, z] * occupied
            before[c, z + 1] = prev[c, z] * occupied

    @pl.loop(0, 18)
    def _(i):
        below = [u0[c, i] for c in range(3)]
        here = [u0[c, i + 1] for c in range(3)]
        above = [u0[c, i + 2] for c in range(3)]
        lap, coup = stencil(below, here, above)
        a, b, gu, gd = (coef[k, pl.ds(i + 3, 1), :] for k in range(4))
        for c in range(3):
            u1[c, i] = update(here[c], before[c, i], lap[c], coup[c], a, b, gu, gd, below[c], above[c])

    def level(c, i):
        return u1[c, i]

    @pl.loop(0, 16)
    def _(z):
        below = [level(c, z) for c in range(3)]
        here = [level(c, z + 1) for c in range(3)]
        above = [level(c, z + 2) for c in range(3)]
        lap, coup = stencil(below, here, above)
        a, b, gu, gd = (coef[k, pl.ds(z + 4, 1), :] for k in range(4))
        for c in range(3):
            out[c, z] = update(here[c], u0[c, z + 2], lap[c], coup[c], a, b, gu, gd, below[c], above[c])

    for k, x in enumerate((1, 2, 14, 13)):
        for c in range(3):
            base = (k * 3 + c) * PAD
            edge[base : base + 3, :] = jnp.zeros((3, WIDE), F32)
            edge[base + 3 : base + 21, :] = u1[c, :, x, :]
            edge[base + 21 : base + PAD, :] = jnp.zeros((3, WIDE), F32)


def tail_kernel(place, pe_sent, po_sent, pe_got, po_got, edge, inner, out):
    even_plan = place[1] % 2 == 0
    out[...] = inner[...]
    order = (1, 0, 2)

    def planes(ref, kind):
        return [ref[(kind + c) * PAD : (kind + c + 1) * PAD, :] for c in order]

    def advance(below, here, above, before, coefs, sign):
        a, b, gu, gd = coefs
        lap, coup = stencil(below, here, above, sign)
        news = []
        for c in range(3):
            lower, upper = row_shift(here[c])
            news.append(update(here[c], before[c], lap[c], coup[c], a, b, gu, gd, lower, upper))
        return news

    def one_side(sent, got, right, near, far):
        sign = 1.0 if right else -1.0
        base = 6 * PAD if right else 0

        def inner_plane(k):
            return [edge[base + (k * 3 + c) * PAD : base + (k * 3 + c + 1) * PAD, :] for c in order]

        own_coefs, got_coefs = pack_coefficients(sent), pack_coefficients(got)
        own_near, own_far = planes(sent, 0), planes(sent, 3)
        got_near, got_far = planes(got, 0), planes(got, 3)
        ghost_1 = advance(own_near, got_near, got_far, planes(got, 6), got_coefs, sign)
        near_1 = advance(own_far, own_near, got_near, planes(sent, 6), own_coefs, sign)
        near_2 = advance(inner_plane(0), near_1, ghost_1, own_near, own_coefs, sign)
        far_2 = advance(inner_plane(1), inner_plane(0), near_1, own_far, own_coefs, sign)
        for k, c in enumerate(order):
            out[c, :, near, :] = near_2[k][4:20]
            out[c, :, far, :] = far_2[k][4:20]

    @pl.when(even_plan)
    def _():
        one_side(pe_sent, pe_got, True, 15, 14)
        one_side(po_sent, po_got, False, 0, 1)

    @pl.when(jnp.logical_not(even_plan))
    def _():
        one_side(pe_sent, pe_got, False, 0, 1)
        one_side(po_sent, po_got, True, 15, 14)


VM = pl.BlockSpec(memory_space=pltpu.VMEM)
SM = pl.BlockSpec(memory_space=pltpu.SMEM)
HB = pl.BlockSpec(memory_space=pl.ANY)


def shape(*dims):
    return jax.ShapeDtypeStruct(dims, F32)


def call(kernel, outs, ins, scratch=(), flops=0, moved=0):
    return pl.pallas_call(
        kernel,
        out_shape=outs,
        in_specs=ins,
        out_specs=[VM] * len(outs),
        scratch_shapes=list(scratch),
        compiler_params=pltpu.CompilerParams(vmem_limit_bytes=24 * 2**20),
        cost_estimate=pl.CostEstimate(flops=flops, bytes_accessed=moved, transcendentals=0),
    )


def local(u_now, u_prev, occupancy, materials, shear_table, lame_table, density_table):
    height = u_now.shape[1] * lax.axis_size("story")
    stories = lax.axis_size("story")
    place = jnp.stack([lax.axis_index("story"), lax.axis_index("plan")]).astype(jnp.int32)
    face, slab = shape(10, 16, WIDE), shape(9 * PAD, WIDE)
    se, so, masses, consts = call(
        functools.partial(prep_kernel, factor=0.8 / height),
        [face, face, shape(stories, WIDE), shape(8, WIDE)],
        [SM] * 6 + [HB] * 2,
        [pltpu.VMEM((2, 3, 2, 16, WIDE), F32), pltpu.VMEM((2, 3, 1, 16, WIDE), F32), pltpu.SemaphoreType.DMA((4,))],
        moved=1 << 20,
    )(place, occupancy.reshape(-1), materials.reshape(-1), shear_table, lame_table, density_table, u_now, u_prev)
    so_got = swap(so, "story", 1)
    se_got = swap(se, "story", 0)
    masses = lax.all_to_all(masses, "story", 0, 0, tiled=True)
    cells = u_now.shape
    pe, po, carried = call(pack_kernel, [slab, slab, shape(8, WIDE)], [SM] + [VM] * 6, moved=2 << 20)(
        place, consts, se_got, so_got, masses, u_now, u_prev
    )
    po_got = swap(po, "plan", 1)
    pe_got = swap(pe, "plan", 0)
    inner, edge = call(
        main_kernel,
        [shape(*cells), shape(12 * PAD, WIDE)],
        [SM] + [VM] * 6,
        [
            pltpu.VMEM((3, 20, 16, WIDE), F32),
            pltpu.VMEM((3, 18, 16, WIDE), F32),
            pltpu.VMEM((3, 18, 16, WIDE), F32),
            pltpu.VMEM((4, PAD, WIDE), F32),
        ],
        flops=60_000_000,
        moved=4 << 20,
    )(place, consts, carried, se_got, so_got, u_now, u_prev)
    (out,) = call(tail_kernel, [shape(*cells)], [SM] + [VM] * 6, flops=10_000_000, moved=3 << 20)(
        place, pe, po, pe_got, po_got, edge, inner
    )
    return out


def solution(mesh):
    in_specs = (
        P(None, "story", "plan", None),
        P(None, "story", "plan", None),
        P("story", "plan", None),
        P("story", "plan", None),
        P(),
        P(),
        P(),
    )
    out_specs = P(None, "story", "plan", None)
    return jax.shard_map(local, mesh=mesh, in_specs=in_specs, out_specs=out_specs, check_vma=False)
```

```python
import functools

import jax
import jax.numpy as jnp
from jax import lax
from jax.experimental import pallas as pl
from jax.experimental.pallas import tpu as pltpu
from jax.sharding import PartitionSpec as P

BLOCK = 16
WIDE = 256
PAD = 24
F32 = jnp.float32


def swap(values, axis, first):
    pairs = []
    for low in range(first, lax.axis_size(axis) - 1, 2):
        pairs += [(low, low + 1), (low + 1, low)]
    return lax.ppermute(values, axis, pairs)


def row_shift(v):
    count = v.shape[0] // 8
    row = lax.broadcasted_iota(jnp.int32, (8, v.shape[1]), 0)
    tiles = [v[8 * k : 8 * k + 8] for k in range(count)]
    down = [jnp.zeros_like(tiles[0])] + [pltpu.roll(t, 1, 0) for t in tiles]
    up = [pltpu.roll(t, 7, 0) for t in tiles] + [jnp.zeros_like(tiles[0])]
    lower = [jnp.where(row == 0, down[k], down[k + 1]) for k in range(count)]
    upper = [jnp.where(row == 7, up[k + 1], up[k]) for k in range(count)]
    return jnp.concatenate(lower, 0), jnp.concatenate(upper, 0)


def lane_shift(v):
    half = WIDE // 2
    lane = lax.broadcasted_iota(jnp.int32, (v.shape[0], half), 1)
    first, second = v[:, :half], v[:, half:]
    first_down, second_down = pltpu.roll(first, 1, 1), pltpu.roll(second, 1, 1)
    first_up, second_up = pltpu.roll(first, half - 1, 1), pltpu.roll(second, half - 1, 1)
    lower = [jnp.where(lane == 0, 0.0, first_down), jnp.where(lane == 0, first_down, second_down)]
    upper = [jnp.where(lane == half - 1, second_up, first_up), jnp.where(lane == half - 1, 0.0, second_up)]
    return jnp.concatenate(lower, 1), jnp.concatenate(upper, 1)


def lane_smooth(v):
    lower, upper = lane_shift(v)
    return lower + upper + 4.0 * v


def lane_first(v):
    lower, upper = lane_shift(v)
    return upper - lower


def total(terms):
    terms = [t for t in terms if t is not None]
    return functools.reduce(lambda p, q: p + q, terms)


def stencil(below, here, above, sign=None):
    zs, zf = [], []
    for j in range(3):
        zs.append(total([below and below[j], above and above[j], here and 4.0 * here[j]]))
        if below and above:
            zf.append(above[j] - below[j])
        else:
            zf.append(above[j] if above else -below[j])
    if sign is not None:
        zf = [sign * v for v in zf]
    zs_sh = [row_shift(v) for v in zs]
    zf_sh = [row_shift(v) for v in zf]
    s_zs = [lo + up + 4.0 * v for (lo, up), v in zip(zs_sh, zs)]
    lap = []
    if here:
        s_mid = [lo + up + 4.0 * v for (lo, up), v in zip([row_shift(v) for v in here], here)]
        inner = [s_zs[j] - 2.0 * (s_mid[j] + zs[j]) for j in range(3)]
        curl = 2.0 * s_zs[0] - 12.0 * s_mid[0]
    else:
        inner = [s_zs[j] - 2.0 * zs[j] for j in range(3)]
        curl = 2.0 * s_zs[0]
    for j in range(3):
        lap.append(lane_smooth(inner[j]) - 2.0 * s_zs[j])
    f_zf0 = zf_sh[0][1] - zf_sh[0][0]
    f_zf1 = zf_sh[1][1] - zf_sh[1][0]
    s_zf0 = zf_sh[0][0] + zf_sh[0][1] + 4.0 * zf[0]
    s_zf2 = zf_sh[2][0] + zf_sh[2][1] + 4.0 * zf[2]
    f_zs1 = zs_sh[1][1] - zs_sh[1][0]
    f_zs2 = zs_sh[2][1] - zs_sh[2][0]
    c0 = lane_smooth(curl + 3.0 * f_zf1) + lane_first(3.0 * s_zf2)
    c1 = lane_smooth(2.0 * s_zs[1] - 12.0 * zs[1] + 3.0 * f_zf0) + lane_first(3.0 * f_zs2)
    c2 = lane_first(3.0 * (s_zf0 + f_zs1)) + 2.0 * lane_smooth(s_zs[2]) - 12.0 * s_zs[2]
    return lap, [c0, c1, c2]


def coefficients(own, over, under, carried):
    z = lax.broadcasted_iota(jnp.int32, (PAD, WIDE), 0) - 4
    zf = z.astype(F32)

    def pick(k):
        return jnp.where(z < 0, under[k], jnp.where(z > 15, over[k], own[k]))

    a, b, g = pick(0), pick(1), pick(2)
    mass, mass_over, mass_under = own[3], over[3], under[3]
    upper = jnp.where(z > 15, carried - mass_over, carried + mass * (15.0 - zf))
    lower = jnp.where(z < 0, carried + 16.0 * mass + mass_under, carried + mass * (16.0 - zf))
    return a, b, g * upper, g * lower


def prep_kernel(place, occ_h, mat_h, shear_h, lame_h, dens_h, now, prev, se, so, masses, consts, occ, mat, shear_t, lame_t, dens_t, held_now, held_prev, sems, *, factor):
    top_first = place[0] % 2 == 0
    smalls = []
    for k, (source, target) in enumerate(((occ_h, occ), (mat_h, mat), (shear_h, shear_t), (lame_h, lame_t), (dens_h, dens_t))):
        smalls.append(pltpu.make_async_copy(source, target, sems.at[4 + k]))
    copies = []
    for k in range(2):
        top = jnp.logical_xor(top_first, k == 1)
        copies.append(pltpu.make_async_copy(now.at[:, pl.ds(jnp.where(top, 14, 0), 2)], held_now.at[k], sems.at[2 * k]))
        copies.append(pltpu.make_async_copy(prev.at[:, pl.ds(jnp.where(top, 15, 0), 1)], held_prev.at[k], sems.at[2 * k + 1]))
    for copy in smalls + copies:
        copy.start()
    for copy in smalls:
        copy.wait()
    block = lax.broadcasted_iota(jnp.int32, (1, WIDE), 1) // BLOCK
    zero = jnp.zeros((1, WIDE), F32)
    occupied, shear, lame, dens = zero, zero, zero, zero
    for j in range(BLOCK):
        at = block == j
        which = mat[j]
        occupied = jnp.where(at, occ[j].astype(F32), occupied)
        shear = jnp.where(at, shear_t[which], shear)
        lame = jnp.where(at, lame_t[which], lame)
        dens = jnp.where(at, dens_t[which], dens)
    scale = occupied * (0.1 / dens)
    own = [scale * shear * (1.0 / 12.0), scale * (lame + shear) * (1.0 / 72.0), scale * factor, dens * occupied, occupied]
    for k, row in enumerate(own):
        consts[k : k + 1, :] = row
    consts[5:8, :] = jnp.zeros((3, WIDE), F32)
    masses[...] = jnp.broadcast_to(own[3], masses.shape)
    for copy in copies:
        copy.wait()
    for k, out in enumerate((se, so)):
        top = jnp.logical_xor(top_first, k == 1)
        for c in range(3):
            first, second = held_now[k, c, 0] * occupied, held_now[k, c, 1] * occupied
            out[c] = jnp.where(top, second, first)
            out[3 + c] = jnp.where(top, first, second)
            out[6 + c] = held_prev[k, c, 0] * occupied
        out[9, 0:8] = consts[...]


def ghost_of(place, se, so):
    even_story = place[0] % 2 == 0

    def ghost(over, *where):
        take = even_story if over else jnp.logical_not(even_story)
        return jnp.where(take, se[where], so[where])

    return ghost


def fill(ghost, consts, coef, now, prev, out, far_rows, prev_rows, near, far, sign):
    occupied = consts[4:5, :]
    for c in range(3):
        for target, base, source, x in ((out, c * PAD, now, near), (far_rows, c * PAD, now, far), (prev_rows, c * PAD, prev, near)):
            target[base + 4 : base + 20, :] = source[c, :, x, :] * occupied
            kinds = (6,) if source is prev else (0, 3)
            for k, kind in enumerate(kinds):
                target[base + 3 - k : base + 4 - k, :] = ghost(False, kind + c, pl.ds(x, 1), slice(None))
                target[base + 20 + k : base + 21 + k, :] = ghost(True, kind + c, pl.ds(x, 1), slice(None))
    order = (1, 0, 2)

    def planes(ref):
        return [ref[c * PAD : (c + 1) * PAD, :] for c in order]

    here = planes(out)
    first = advance(planes(far_rows), here, None, planes(prev_rows), [coef[k] for k in range(4)], sign)
    for k, c in enumerate(order):
        out[3 * PAD + 16 * c : 3 * PAD + 16 * c + 16, :] = first[k][4:20]
        out[c * PAD : c * PAD + 1, :] = first[k][3:4]
        out[c * PAD + 23 : c * PAD + 24, :] = first[k][20:21]
    for k in range(2):
        row = 1 if k == 0 else 22
        out[row : row + 1, :] = consts[k : k + 1, :]
        out[PAD + row : PAD + row + 1, :] = ghost(True, 9, pl.ds(k, 1), slice(None))
        out[2 * PAD + row : 2 * PAD + row + 1, :] = ghost(False, 9, pl.ds(k, 1), slice(None))


def pack_po_kernel(place, consts, se, so, masses, now, prev, po, coef, far_rows, prev_rows):
    ghost = ghost_of(place, se, so)
    step = lax.broadcasted_iota(jnp.int32, masses.shape, 0)
    carried = 16.0 * jnp.sum(jnp.where(step > place[0], masses[...], 0.0), 0, keepdims=True)
    own = [consts[k : k + 1, :] for k in range(4)]
    over = [ghost(True, 9, pl.ds(k, 1), slice(None)) for k in range(4)]
    under = [ghost(False, 9, pl.ds(k, 1), slice(None)) for k in range(4)]
    for k, rows in enumerate(coefficients(own, over, under, carried)):
        coef[k] = rows
    even_plan = place[1] % 2 == 0

    @pl.when(even_plan)
    def _():
        fill(ghost, consts, coef, now, prev, po, far_rows, prev_rows, 0, 1, -1.0)

    @pl.when(jnp.logical_not(even_plan))
    def _():
        fill(ghost, consts, coef, now, prev, po, far_rows, prev_rows, 15, 14, None)


def pack_pe_kernel(place, consts, coef, se, so, now, prev, pe, far_rows, prev_rows):
    ghost = ghost_of(place, se, so)
    even_plan = place[1] % 2 == 0

    @pl.when(even_plan)
    def _():
        fill(ghost, consts, coef, now, prev, pe, far_rows, prev_rows, 15, 14, None)

    @pl.when(jnp.logical_not(even_plan))
    def _():
        fill(ghost, consts, coef, now, prev, pe, far_rows, prev_rows, 0, 1, -1.0)


def advance(below, here, above, before, coefs, sign):
    a, b, gu, gd = coefs
    lap, coup = stencil(below, here, above, sign)
    news = []
    for c in range(3):
        lower, upper = row_shift(here[c])
        news.append(update(here[c], before[c], lap[c], coup[c], a, b, gu, gd, lower, upper))
    return news


def update(here, before, lap, coup, a, b, gu, gd, below, above):
    geometric = gu * (above - here) - gd * (here - below)
    return 2.0 * here - before + a * lap + b * coup - geometric


def main_kernel(place, consts, coef, se, so, now, prev, out, u0, u1, before):
    ghost = ghost_of(place, se, so)
    occupied = jnp.broadcast_to(consts[4:5, :], (16, WIDE))
    for c in range(3):
        u0[c, 0] = ghost(False, 3 + c)
        u0[c, 1] = ghost(False, c)
        u0[c, 18] = ghost(True, c)
        u0[c, 19] = ghost(True, 3 + c)
        before[c, 0] = ghost(False, 6 + c)
        before[c, 17] = ghost(True, 6 + c)

    @pl.loop(0, 16)
    def _(z):
        for c in range(3):
            u0[c, z + 2] = now[c, z] * occupied
            before[c, z + 1] = prev[c, z] * occupied

    def one(source, earlier, target, i, shift):
        below, here, above = ([source[c, i + k] for c in range(3)] for k in range(3))
        lap, coup = stencil(below, here, above)
        a, b, gu, gd = (coef[k, pl.ds(i + shift, 1), :] for k in range(4))
        for c in range(3):
            target[c, i] = update(here[c], earlier(c, i), lap[c], coup[c], a, b, gu, gd, below[c], above[c])

    @pl.loop(0, 18)
    def _(i):
        one(u0, lambda c, i: before[c, i], u1, i, 3)

    @pl.loop(0, 16)
    def _(i):
        one(u1, lambda c, i: u0[c, i + 2], out, i, 4)


def tail_kernel(place, coef, pe_sent, po_sent, pe_got, po_got, inner, out, held):
    even_plan = place[1] % 2 == 0
    out[...] = inner[...]
    order = (1, 0, 2)

    def planes(ref):
        return [ref[c * PAD : (c + 1) * PAD, :] for c in order]

    def one_side(sent, got, near, far, sign):
        for c in range(3):
            base = c * PAD
            held[base : base + 4, :] = got[base : base + 1, :] + jnp.zeros((4, WIDE), F32)
            held[base + 4 : base + 20, :] = got[3 * PAD + 16 * c : 3 * PAD + 16 * c + 16, :]
            held[base + 20 : base + PAD, :] = got[base + 23 : base + 24, :] + jnp.zeros((4, WIDE), F32)
        a, b, gu, gd = (coef[k] for k in range(4))
        z = lax.broadcasted_iota(jnp.int32, (PAD, WIDE), 0) - 4

        def pick(row):
            own, over, under = (got[k * PAD + row : k * PAD + row + 1, :] for k in range(3))
            return jnp.where(z < 0, under, jnp.where(z > 15, over, own))

        got_a, got_b = pick(1), pick(22)
        lap, coup = stencil(None, None, planes(got), sign)
        delta = [a * lap[k] + b * coup[k] for k in range(3)]
        lap, coup = stencil(planes(sent), None, None, sign)
        outer = [p + got_a * lap[k] + got_b * coup[k] for k, p in enumerate(planes(held))]
        zero = jnp.zeros((PAD, WIDE), F32)
        near_more = advance(None, delta, outer, [zero] * 3, (a, b, gu, gd), sign)
        lap, coup = stencil(None, None, delta, sign)
        for k, c in enumerate(order):
            out[c, :, near, :] += near_more[k][4:20]
            out[c, :, far, :] += (a * lap[k] + b * coup[k])[4:20]

    @pl.when(even_plan)
    def _():
        one_side(pe_sent, pe_got, 15, 14, None)
        one_side(po_sent, po_got, 0, 1, -1.0)

    @pl.when(jnp.logical_not(even_plan))
    def _():
        one_side(pe_sent, pe_got, 0, 1, -1.0)
        one_side(po_sent, po_got, 15, 14, None)


VM = pl.BlockSpec(memory_space=pltpu.VMEM)
SM = pl.BlockSpec(memory_space=pltpu.SMEM)
HB = pl.BlockSpec(memory_space=pltpu.HBM)


def shape(*dims):
    return jax.ShapeDtypeStruct(dims, F32)


def call(kernel, outs, ins, scratch=(), flops=0, moved=0):
    return pl.pallas_call(
        kernel,
        out_shape=outs,
        in_specs=ins,
        out_specs=[VM] * len(outs),
        scratch_shapes=list(scratch),
        compiler_params=pltpu.CompilerParams(vmem_limit_bytes=24 * 2**20),
        cost_estimate=pl.CostEstimate(flops=flops, bytes_accessed=moved, transcendentals=0),
    )


def local(u_now, u_prev, occupancy, materials, shear_table, lame_table, density_table):
    height = u_now.shape[1] * lax.axis_size("story")
    stories = lax.axis_size("story")
    mats = shear_table.shape[0]
    place = jnp.stack([lax.axis_index("story"), lax.axis_index("plan")]).astype(jnp.int32)
    face, slab, table = shape(10, 16, WIDE), shape(3 * PAD + 48, WIDE), shape(4, PAD, WIDE)
    planes = [pltpu.VMEM((3 * PAD, WIDE), F32)] * 2
    se, so, masses, consts = call(
        functools.partial(prep_kernel, factor=0.8 / height),
        [face, face, shape(stories, WIDE), shape(8, WIDE)],
        [SM] + [HB] * 7,
        [
            pltpu.SMEM((BLOCK,), jnp.int32),
            pltpu.SMEM((BLOCK,), jnp.int32),
            pltpu.SMEM((mats,), F32),
            pltpu.SMEM((mats,), F32),
            pltpu.SMEM((mats,), F32),
            pltpu.VMEM((2, 3, 2, 16, WIDE), F32),
            pltpu.VMEM((2, 3, 1, 16, WIDE), F32),
            pltpu.SemaphoreType.DMA((9,)),
        ],
        moved=1 << 20,
    )(place, occupancy.reshape(-1), materials.reshape(-1), shear_table, lame_table, density_table, u_now, u_prev)
    so_got = swap(so, "story", 1)
    se_got = swap(se, "story", 0)
    masses = lax.all_to_all(masses, "story", 0, 0, tiled=True)
    cells = u_now.shape
    po, coef = call(pack_po_kernel, [slab, table], [SM] + [VM] * 6, planes, moved=1 << 20)(
        place, consts, se_got, so_got, masses, u_now, u_prev
    )
    po_got = swap(po, "plan", 1)
    (pe,) = call(pack_pe_kernel, [slab], [SM] + [VM] * 6, planes, moved=1 << 20)(
        place, consts, coef, se_got, so_got, u_now, u_prev
    )
    pe_got = swap(pe, "plan", 0)
    (inner,) = call(
        main_kernel,
        [shape(*cells)],
        [SM] + [VM] * 6,
        [
            pltpu.VMEM((3, 20, 16, WIDE), F32),
            pltpu.VMEM((3, 18, 16, WIDE), F32),
            pltpu.VMEM((3, 18, 16, WIDE), F32),
        ],
        flops=60_000_000,
        moved=4 << 20,
    )(place, consts, coef, se_got, so_got, u_now, u_prev)
    (out,) = call(
        tail_kernel, [shape(*cells)], [SM] + [VM] * 6, [pltpu.VMEM((3 * PAD, WIDE), F32)], flops=10_000_000, moved=3 << 20
    )(place, coef, pe, po, pe_got, po_got, inner)
    return out


def solution(mesh):
    in_specs = (
        P(None, "story", "plan", None),
        P(None, "story", "plan", None),
        P("story", "plan", None),
        P("story", "plan", None),
        P(),
        P(),
        P(),
    )
    out_specs = P(None, "story", "plan", None)
    return jax.shard_map(local, mesh=mesh, in_specs=in_specs, out_specs=out_specs, check_vma=False)
```

```python
import functools

import jax
import jax.numpy as jnp
from jax import lax
from jax.experimental import pallas as pl
from jax.experimental.pallas import tpu as pltpu
from jax.sharding import PartitionSpec as P

BLOCK = 16
WIDE = 256
PAD = 24
F32 = jnp.float32


def swap(values, axis, first):
    pairs = []
    for low in range(first, lax.axis_size(axis) - 1, 2):
        pairs += [(low, low + 1), (low + 1, low)]
    return lax.ppermute(values, axis, pairs)


def row_shift(v):
    count = v.shape[0] // 8
    row = lax.broadcasted_iota(jnp.int32, (8, v.shape[1]), 0)
    tiles = [v[8 * k : 8 * k + 8] for k in range(count)]
    down = [jnp.zeros_like(tiles[0])] + [pltpu.roll(t, 1, 0) for t in tiles]
    up = [pltpu.roll(t, 7, 0) for t in tiles] + [jnp.zeros_like(tiles[0])]
    lower = [jnp.where(row == 0, down[k], down[k + 1]) for k in range(count)]
    upper = [jnp.where(row == 7, up[k + 1], up[k]) for k in range(count)]
    return jnp.concatenate(lower, 0), jnp.concatenate(upper, 0)


def lane_shift(v):
    half = WIDE // 2
    lane = lax.broadcasted_iota(jnp.int32, (v.shape[0], half), 1)
    first, second = v[:, :half], v[:, half:]
    first_down, second_down = pltpu.roll(first, 1, 1), pltpu.roll(second, 1, 1)
    first_up, second_up = pltpu.roll(first, half - 1, 1), pltpu.roll(second, half - 1, 1)
    lower = [jnp.where(lane == 0, 0.0, first_down), jnp.where(lane == 0, first_down, second_down)]
    upper = [jnp.where(lane == half - 1, second_up, first_up), jnp.where(lane == half - 1, 0.0, second_up)]
    return jnp.concatenate(lower, 1), jnp.concatenate(upper, 1)


def lane_smooth(v):
    lower, upper = lane_shift(v)
    return lower + upper + 4.0 * v


def lane_first(v):
    lower, upper = lane_shift(v)
    return upper - lower


def total(terms):
    terms = [t for t in terms if t is not None]
    return functools.reduce(lambda p, q: p + q, terms)


def stencil(below, here, above, sign=None):
    zs, zf = [], []
    for j in range(3):
        zs.append(total([below and below[j], above and above[j], here and 4.0 * here[j]]))
        if below and above:
            zf.append(above[j] - below[j])
        else:
            zf.append(above[j] if above else -below[j])
    if sign is not None:
        zf = [sign * v for v in zf]
    zs_sh = [row_shift(v) for v in zs]
    zf_sh = [row_shift(v) for v in zf]
    s_zs = [lo + up + 4.0 * v for (lo, up), v in zip(zs_sh, zs)]
    lap = []
    if here:
        s_mid = [lo + up + 4.0 * v for (lo, up), v in zip([row_shift(v) for v in here], here)]
        inner = [s_zs[j] - 2.0 * (s_mid[j] + zs[j]) for j in range(3)]
        curl = 2.0 * s_zs[0] - 12.0 * s_mid[0]
    else:
        inner = [s_zs[j] - 2.0 * zs[j] for j in range(3)]
        curl = 2.0 * s_zs[0]
    for j in range(3):
        lap.append(lane_smooth(inner[j]) - 2.0 * s_zs[j])
    f_zf0 = zf_sh[0][1] - zf_sh[0][0]
    f_zf1 = zf_sh[1][1] - zf_sh[1][0]
    s_zf0 = zf_sh[0][0] + zf_sh[0][1] + 4.0 * zf[0]
    s_zf2 = zf_sh[2][0] + zf_sh[2][1] + 4.0 * zf[2]
    f_zs1 = zs_sh[1][1] - zs_sh[1][0]
    f_zs2 = zs_sh[2][1] - zs_sh[2][0]
    c0 = lane_smooth(curl + 3.0 * f_zf1) + lane_first(3.0 * s_zf2)
    c1 = lane_smooth(2.0 * s_zs[1] - 12.0 * zs[1] + 3.0 * f_zf0) + lane_first(3.0 * f_zs2)
    c2 = lane_first(3.0 * (s_zf0 + f_zs1)) + 2.0 * lane_smooth(s_zs[2]) - 12.0 * s_zs[2]
    return lap, [c0, c1, c2]


def coefficients(own, over, under, carried):
    z = lax.broadcasted_iota(jnp.int32, (PAD, WIDE), 0) - 4
    zf = z.astype(F32)

    def pick(k):
        return jnp.where(z < 0, under[k], jnp.where(z > 15, over[k], own[k]))

    a, b, g = pick(0), pick(1), pick(2)
    mass, mass_over, mass_under = own[3], over[3], under[3]
    upper = jnp.where(z > 15, carried - mass_over, carried + mass * (15.0 - zf))
    lower = jnp.where(z < 0, carried + 16.0 * mass + mass_under, carried + mass * (16.0 - zf))
    return a, b, g * upper, g * lower


def prep_kernel(place, occ_h, mat_h, shear_h, lame_h, dens_h, now, prev, se, so, masses, consts, occ, mat, shear_t, lame_t, dens_t, held_now, held_prev, sems, *, factor):
    top_first = place[0] % 2 == 0
    smalls = []
    for k, (source, target) in enumerate(((occ_h, occ), (mat_h, mat), (shear_h, shear_t), (lame_h, lame_t), (dens_h, dens_t))):
        smalls.append(pltpu.make_async_copy(source, target, sems.at[4 + k]))
    copies = []
    for k in range(2):
        top = jnp.logical_xor(top_first, k == 1)
        copies.append(pltpu.make_async_copy(now.at[:, pl.ds(jnp.where(top, 14, 0), 2)], held_now.at[k], sems.at[2 * k]))
        copies.append(pltpu.make_async_copy(prev.at[:, pl.ds(jnp.where(top, 15, 0), 1)], held_prev.at[k], sems.at[2 * k + 1]))
    for copy in smalls + copies:
        copy.start()
    for copy in smalls:
        copy.wait()
    block = lax.broadcasted_iota(jnp.int32, (1, WIDE), 1) // BLOCK
    zero = jnp.zeros((1, WIDE), F32)
    occupied, shear, lame, dens = zero, zero, zero, zero
    for j in range(BLOCK):
        at = block == j
        which = mat[j]
        occupied = jnp.where(at, occ[j].astype(F32), occupied)
        shear = jnp.where(at, shear_t[which], shear)
        lame = jnp.where(at, lame_t[which], lame)
        dens = jnp.where(at, dens_t[which], dens)
    scale = occupied * (0.1 / dens)
    own = [scale * shear * (1.0 / 12.0), scale * (lame + shear) * (1.0 / 72.0), scale * factor, dens * occupied, occupied]
    for k, row in enumerate(own):
        consts[k : k + 1, :] = row
    consts[5:8, :] = jnp.zeros((3, WIDE), F32)
    masses[...] = jnp.broadcast_to(own[3], masses.shape)
    for copy in copies:
        copy.wait()
    for k, out in enumerate((se, so)):
        top = jnp.logical_xor(top_first, k == 1)
        for c in range(3):
            first, second = held_now[k, c, 0] * occupied, held_now[k, c, 1] * occupied
            out[c] = jnp.where(top, second, first)
            out[3 + c] = jnp.where(top, first, second)
            out[6 + c] = held_prev[k, c, 0] * occupied
        out[9, 0:8] = consts[...]


def ghost_of(place, se, so):
    even_story = place[0] % 2 == 0

    def ghost(over, *where):
        take = even_story if over else jnp.logical_not(even_story)
        return jnp.where(take, se[where], so[where])

    return ghost


def fill(ghost, consts, coef, now, prev, out, far_rows, prev_rows, near, far, sign):
    occupied = consts[4:5, :]
    for c in range(3):
        for target, base, source, x in ((out, c * PAD, now, near), (far_rows, c * PAD, now, far), (prev_rows, c * PAD, prev, near)):
            target[base + 4 : base + 20, :] = source[c, :, x, :] * occupied
            kinds = (6,) if source is prev else (0, 3)
            for k, kind in enumerate(kinds):
                target[base + 3 - k : base + 4 - k, :] = ghost(False, kind + c, pl.ds(x, 1), slice(None))
                target[base + 20 + k : base + 21 + k, :] = ghost(True, kind + c, pl.ds(x, 1), slice(None))
    order = (1, 0, 2)

    def planes(ref):
        return [ref[c * PAD : (c + 1) * PAD, :] for c in order]

    here = planes(out)
    first = advance(planes(far_rows), here, None, planes(prev_rows), [coef[k] for k in range(4)], sign)
    for k, c in enumerate(order):
        out[3 * PAD + 16 * c : 3 * PAD + 16 * c + 16, :] = first[k][4:20]
        out[c * PAD : c * PAD + 1, :] = first[k][3:4]
        out[c * PAD + 23 : c * PAD + 24, :] = first[k][20:21]
    for k in range(2):
        row = 1 if k == 0 else 22
        out[row : row + 1, :] = consts[k : k + 1, :]
        out[PAD + row : PAD + row + 1, :] = ghost(True, 9, pl.ds(k, 1), slice(None))
        out[2 * PAD + row : 2 * PAD + row + 1, :] = ghost(False, 9, pl.ds(k, 1), slice(None))


def pack_po_kernel(place, consts, se, so, masses, now, prev, po, coef, far_rows, prev_rows):
    ghost = ghost_of(place, se, so)
    step = lax.broadcasted_iota(jnp.int32, masses.shape, 0)
    carried = 16.0 * jnp.sum(jnp.where(step > place[0], masses[...], 0.0), 0, keepdims=True)
    own = [consts[k : k + 1, :] for k in range(4)]
    over = [ghost(True, 9, pl.ds(k, 1), slice(None)) for k in range(4)]
    under = [ghost(False, 9, pl.ds(k, 1), slice(None)) for k in range(4)]
    for k, rows in enumerate(coefficients(own, over, under, carried)):
        coef[k] = rows
    even_plan = place[1] % 2 == 0

    @pl.when(even_plan)
    def _():
        fill(ghost, consts, coef, now, prev, po, far_rows, prev_rows, 0, 1, -1.0)

    @pl.when(jnp.logical_not(even_plan))
    def _():
        fill(ghost, consts, coef, now, prev, po, far_rows, prev_rows, 15, 14, None)


def pack_pe_kernel(place, consts, coef, se, so, now, prev, pe, far_rows, prev_rows):
    ghost = ghost_of(place, se, so)
    even_plan = place[1] % 2 == 0

    @pl.when(even_plan)
    def _():
        fill(ghost, consts, coef, now, prev, pe, far_rows, prev_rows, 15, 14, None)

    @pl.when(jnp.logical_not(even_plan))
    def _():
        fill(ghost, consts, coef, now, prev, pe, far_rows, prev_rows, 0, 1, -1.0)


def advance(below, here, above, before, coefs, sign):
    a, b, gu, gd = coefs
    lap, coup = stencil(below, here, above, sign)
    news = []
    for c in range(3):
        lower, upper = row_shift(here[c])
        news.append(update(here[c], before[c], lap[c], coup[c], a, b, gu, gd, lower, upper))
    return news


def update(here, before, lap, coup, a, b, gu, gd, below, above):
    geometric = gu * (above - here) - gd * (here - below)
    return 2.0 * here - before + a * lap + b * coup - geometric


def main_kernel(place, consts, coef, se, so, now, prev, out, u0, u1, before):
    ghost = ghost_of(place, se, so)
    occupied = jnp.broadcast_to(consts[4:5, :], (16, WIDE))
    for c in range(3):
        u0[c, 0] = ghost(False, 3 + c)
        u0[c, 1] = ghost(False, c)
        u0[c, 18] = ghost(True, c)
        u0[c, 19] = ghost(True, 3 + c)
        before[c, 0] = ghost(False, 6 + c)
        before[c, 17] = ghost(True, 6 + c)

    @pl.loop(0, 16)
    def _(z):
        for c in range(3):
            u0[c, z + 2] = now[c, z] * occupied
            before[c, z + 1] = prev[c, z] * occupied

    def one(source, earlier, target, i, shift):
        below, here, above = ([source[c, i + k] for c in range(3)] for k in range(3))
        lap, coup = stencil(below, here, above)
        a, b, gu, gd = (coef[k, pl.ds(i + shift, 1), :] for k in range(4))
        for c in range(3):
            target[c, i] = update(here[c], earlier(c, i), lap[c], coup[c], a, b, gu, gd, below[c], above[c])

    @pl.loop(0, 18)
    def _(i):
        one(u0, lambda c, i: before[c, i], u1, i, 3)

    @pl.loop(0, 16)
    def _(i):
        one(u1, lambda c, i: u0[c, i + 2], out, i, 4)


def tail_kernel(place, coef, pe_sent, po_sent, pe_got, po_got, inner, out, held):
    even_plan = place[1] % 2 == 0
    out[...] = inner[...]
    order = (1, 0, 2)

    def planes(ref):
        return [ref[c * PAD : (c + 1) * PAD, :] for c in order]

    def one_side(sent, got, near, far, sign):
        for c in range(3):
            base = c * PAD
            held[base : base + 4, :] = got[base : base + 1, :] + jnp.zeros((4, WIDE), F32)
            held[base + 4 : base + 20, :] = got[3 * PAD + 16 * c : 3 * PAD + 16 * c + 16, :]
            held[base + 20 : base + PAD, :] = got[base + 23 : base + 24, :] + jnp.zeros((4, WIDE), F32)
        a, b, gu, gd = (coef[k] for k in range(4))
        z = lax.broadcasted_iota(jnp.int32, (PAD, WIDE), 0) - 4

        def pick(row):
            own, over, under = (got[k * PAD + row : k * PAD + row + 1, :] for k in range(3))
            return jnp.where(z < 0, under, jnp.where(z > 15, over, own))

        got_a, got_b = pick(1), pick(22)
        lap, coup = stencil(None, None, planes(got), sign)
        delta = [a * lap[k] + b * coup[k] for k in range(3)]
        lap, coup = stencil(planes(sent), None, None, sign)
        outer = [p + got_a * lap[k] + got_b * coup[k] for k, p in enumerate(planes(held))]
        zero = jnp.zeros((PAD, WIDE), F32)
        near_more = advance(None, delta, outer, [zero] * 3, (a, b, gu, gd), sign)
        lap, coup = stencil(None, None, delta, sign)
        for k, c in enumerate(order):
            out[c, :, near, :] += near_more[k][4:20]
            out[c, :, far, :] += (a * lap[k] + b * coup[k])[4:20]

    @pl.when(even_plan)
    def _():
        one_side(pe_sent, pe_got, 15, 14, None)
        one_side(po_sent, po_got, 0, 1, -1.0)

    @pl.when(jnp.logical_not(even_plan))
    def _():
        one_side(pe_sent, pe_got, 0, 1, -1.0)
        one_side(po_sent, po_got, 15, 14, None)


VM = pl.BlockSpec(memory_space=pltpu.VMEM)
SM = pl.BlockSpec(memory_space=pltpu.SMEM)
HB = pl.BlockSpec(memory_space=pltpu.HBM)


def shape(*dims):
    return jax.ShapeDtypeStruct(dims, F32)


def call(kernel, outs, ins, scratch=(), flops=0, moved=0, grant=24):
    return pl.pallas_call(
        kernel,
        out_shape=outs,
        in_specs=ins,
        out_specs=[VM] * len(outs),
        scratch_shapes=list(scratch),
        compiler_params=pltpu.CompilerParams(vmem_limit_bytes=grant * 2**20),
        cost_estimate=pl.CostEstimate(flops=flops, bytes_accessed=moved, transcendentals=0),
    )


def local(u_now, u_prev, occupancy, materials, shear_table, lame_table, density_table):
    height = u_now.shape[1] * lax.axis_size("story")
    stories = lax.axis_size("story")
    mats = shear_table.shape[0]
    place = jnp.stack([lax.axis_index("story"), lax.axis_index("plan")]).astype(jnp.int32)
    face, slab, table = shape(10, 16, WIDE), shape(3 * PAD + 48, WIDE), shape(4, PAD, WIDE)
    planes = [pltpu.VMEM((3 * PAD, WIDE), F32)] * 2
    se, so, masses, consts = call(
        functools.partial(prep_kernel, factor=0.8 / height),
        [face, face, shape(stories, WIDE), shape(8, WIDE)],
        [SM] + [HB] * 7,
        [
            pltpu.SMEM((BLOCK,), jnp.int32),
            pltpu.SMEM((BLOCK,), jnp.int32),
            pltpu.SMEM((mats,), F32),
            pltpu.SMEM((mats,), F32),
            pltpu.SMEM((mats,), F32),
            pltpu.VMEM((2, 3, 2, 16, WIDE), F32),
            pltpu.VMEM((2, 3, 1, 16, WIDE), F32),
            pltpu.SemaphoreType.DMA((9,)),
        ],
        moved=1 << 20,
        grant=60,
    )(place, occupancy.reshape(-1), materials.reshape(-1), shear_table, lame_table, density_table, u_now, u_prev)
    so_got = swap(so, "story", 1)
    se_got = swap(se, "story", 0)
    masses = lax.all_to_all(masses, "story", 0, 0, tiled=True)
    cells = u_now.shape
    po, coef = call(pack_po_kernel, [shape(3 * PAD + 56, WIDE), table], [SM] + [VM] * 6, planes, moved=1 << 20)(
        place, consts, se_got, so_got, masses, u_now, u_prev
    )
    po_got = swap(po, "plan", 1)
    (pe,) = call(pack_pe_kernel, [slab], [SM] + [VM] * 6, planes, moved=1 << 20)(
        place, consts, coef, se_got, so_got, u_now, u_prev
    )
    pe_got = swap(pe, "plan", 0)
    (inner,) = call(
        main_kernel,
        [shape(*cells)],
        [SM] + [VM] * 6,
        [
            pltpu.VMEM((3, 20, 16, WIDE), F32),
            pltpu.VMEM((3, 18, 16, WIDE), F32),
            pltpu.VMEM((3, 18, 16, WIDE), F32),
        ],
        flops=60_000_000,
        moved=4 << 20,
    )(place, consts, coef, se_got, so_got, u_now, u_prev)
    (out,) = call(
        tail_kernel, [shape(*cells)], [SM] + [VM] * 6, [pltpu.VMEM((3 * PAD, WIDE), F32)], flops=10_000_000, moved=3 << 20
    )(place, coef, pe, po, pe_got, po_got, inner)
    return out


def solution(mesh):
    in_specs = (
        P(None, "story", "plan", None),
        P(None, "story", "plan", None),
        P("story", "plan", None),
        P("story", "plan", None),
        P(),
        P(),
        P(),
    )
    out_specs = P(None, "story", "plan", None)
    return jax.shard_map(local, mesh=mesh, in_specs=in_specs, out_specs=out_specs, check_vma=False)
```

```python
import functools

import jax
import jax.numpy as jnp
from jax import lax
from jax.experimental import pallas as pl
from jax.experimental.pallas import tpu as pltpu
from jax.sharding import PartitionSpec as P

BLOCK = 16
WIDE = 256
PAD = 24
F32 = jnp.float32


def swap(values, axis, first):
    pairs = []
    for low in range(first, lax.axis_size(axis) - 1, 2):
        pairs += [(low, low + 1), (low + 1, low)]
    return lax.ppermute(values, axis, pairs)


def row_shift(v):
    count = v.shape[0] // 8
    row = lax.broadcasted_iota(jnp.int32, (8, v.shape[1]), 0)
    tiles = [v[8 * k : 8 * k + 8] for k in range(count)]
    down = [jnp.zeros_like(tiles[0])] + [pltpu.roll(t, 1, 0) for t in tiles]
    up = [pltpu.roll(t, 7, 0) for t in tiles] + [jnp.zeros_like(tiles[0])]
    lower = [jnp.where(row == 0, down[k], down[k + 1]) for k in range(count)]
    upper = [jnp.where(row == 7, up[k + 1], up[k]) for k in range(count)]
    return jnp.concatenate(lower, 0), jnp.concatenate(upper, 0)


def lane_shift(v):
    half = WIDE // 2
    lane = lax.broadcasted_iota(jnp.int32, (v.shape[0], half), 1)
    first, second = v[:, :half], v[:, half:]
    first_down, second_down = pltpu.roll(first, 1, 1), pltpu.roll(second, 1, 1)
    first_up, second_up = pltpu.roll(first, half - 1, 1), pltpu.roll(second, half - 1, 1)
    lower = [jnp.where(lane == 0, 0.0, first_down), jnp.where(lane == 0, first_down, second_down)]
    upper = [jnp.where(lane == half - 1, second_up, first_up), jnp.where(lane == half - 1, 0.0, second_up)]
    return jnp.concatenate(lower, 1), jnp.concatenate(upper, 1)


def lane_smooth(v):
    lower, upper = lane_shift(v)
    return lower + upper + 4.0 * v


def lane_first(v):
    lower, upper = lane_shift(v)
    return upper - lower


def total(terms):
    terms = [t for t in terms if t is not None]
    return functools.reduce(lambda p, q: p + q, terms)


def stencil(below, here, above, sign=None):
    zs, zf = [], []
    for j in range(3):
        zs.append(total([below and below[j], above and above[j], here and 4.0 * here[j]]))
        if below and above:
            zf.append(above[j] - below[j])
        else:
            zf.append(above[j] if above else -below[j])
    if sign is not None:
        zf = [sign * v for v in zf]
    zs_sh = [row_shift(v) for v in zs]
    zf_sh = [row_shift(v) for v in zf]
    s_zs = [lo + up + 4.0 * v for (lo, up), v in zip(zs_sh, zs)]
    lap = []
    if here:
        s_mid = [lo + up + 4.0 * v for (lo, up), v in zip([row_shift(v) for v in here], here)]
        inner = [s_zs[j] - 2.0 * (s_mid[j] + zs[j]) for j in range(3)]
        curl = 2.0 * s_zs[0] - 12.0 * s_mid[0]
    else:
        inner = [s_zs[j] - 2.0 * zs[j] for j in range(3)]
        curl = 2.0 * s_zs[0]
    for j in range(3):
        lap.append(lane_smooth(inner[j]) - 2.0 * s_zs[j])
    f_zf0 = zf_sh[0][1] - zf_sh[0][0]
    f_zf1 = zf_sh[1][1] - zf_sh[1][0]
    s_zf0 = zf_sh[0][0] + zf_sh[0][1] + 4.0 * zf[0]
    s_zf2 = zf_sh[2][0] + zf_sh[2][1] + 4.0 * zf[2]
    f_zs1 = zs_sh[1][1] - zs_sh[1][0]
    f_zs2 = zs_sh[2][1] - zs_sh[2][0]
    c0 = lane_smooth(curl + 3.0 * f_zf1) + lane_first(3.0 * s_zf2)
    c1 = lane_smooth(2.0 * s_zs[1] - 12.0 * zs[1] + 3.0 * f_zf0) + lane_first(3.0 * f_zs2)
    c2 = lane_first(3.0 * (s_zf0 + f_zs1)) + 2.0 * lane_smooth(s_zs[2]) - 12.0 * s_zs[2]
    return lap, [c0, c1, c2]


def coefficients(own, over, under, carried):
    z = lax.broadcasted_iota(jnp.int32, (PAD, WIDE), 0) - 4
    zf = z.astype(F32)

    def pick(k):
        return jnp.where(z < 0, under[k], jnp.where(z > 15, over[k], own[k]))

    a, b, g = pick(0), pick(1), pick(2)
    mass, mass_over, mass_under = own[3], over[3], under[3]
    upper = jnp.where(z > 15, carried - mass_over, carried + mass * (15.0 - zf))
    lower = jnp.where(z < 0, carried + 16.0 * mass + mass_under, carried + mass * (16.0 - zf))
    return a, b, g * upper, g * lower


def prep_kernel(place, occ, mat, shear_t, lame_t, dens_t, now, prev, se, so, masses, consts, held_now, held_prev, sems, *, factor):
    top_first = place[0] % 2 == 0
    copies = []
    for k in range(2):
        top = jnp.logical_xor(top_first, k == 1)
        copies.append(pltpu.make_async_copy(now.at[:, pl.ds(jnp.where(top, 14, 0), 2)], held_now.at[k], sems.at[2 * k]))
        copies.append(pltpu.make_async_copy(prev.at[:, pl.ds(jnp.where(top, 15, 0), 1)], held_prev.at[k], sems.at[2 * k + 1]))
    for copy in copies:
        copy.start()
    block = lax.broadcasted_iota(jnp.int32, (1, WIDE), 1) // BLOCK
    zero = jnp.zeros((1, WIDE), F32)
    occupied, shear, lame, dens = zero, zero, zero, zero
    for j in range(BLOCK):
        at = block == j
        which = mat[j]
        occupied = jnp.where(at, occ[j].astype(F32), occupied)
        shear = jnp.where(at, shear_t[which], shear)
        lame = jnp.where(at, lame_t[which], lame)
        dens = jnp.where(at, dens_t[which], dens)
    scale = occupied * (0.1 / dens)
    own = [scale * shear * (1.0 / 12.0), scale * (lame + shear) * (1.0 / 72.0), scale * factor, dens * occupied, occupied]
    for k, row in enumerate(own):
        consts[k : k + 1, :] = row
    consts[5:8, :] = jnp.zeros((3, WIDE), F32)
    masses[...] = jnp.broadcast_to(own[3], masses.shape)
    for copy in copies:
        copy.wait()
    for k, out in enumerate((se, so)):
        top = jnp.logical_xor(top_first, k == 1)
        for c in range(3):
            first, second = held_now[k, c, 0] * occupied, held_now[k, c, 1] * occupied
            out[c] = jnp.where(top, second, first)
            out[3 + c] = jnp.where(top, first, second)
            out[6 + c] = held_prev[k, c, 0] * occupied
        out[9, 0:8] = consts[...]


def ghost_of(place, se, so):
    even_story = place[0] % 2 == 0

    def ghost(over, *where):
        take = even_story if over else jnp.logical_not(even_story)
        return jnp.where(take, se[where], so[where])

    return ghost


def fill(ghost, consts, coef, now, prev, out, far_rows, prev_rows, near, far, sign):
    occupied = consts[4:5, :]
    for c in range(3):
        for target, base, source, x in ((out, c * PAD, now, near), (far_rows, c * PAD, now, far), (prev_rows, c * PAD, prev, near)):
            target[base + 4 : base + 20, :] = source[c, :, x, :] * occupied
            kinds = (6,) if source is prev else (0, 3)
            for k, kind in enumerate(kinds):
                target[base + 3 - k : base + 4 - k, :] = ghost(False, kind + c, pl.ds(x, 1), slice(None))
                target[base + 20 + k : base + 21 + k, :] = ghost(True, kind + c, pl.ds(x, 1), slice(None))
    order = (1, 0, 2)

    def planes(ref):
        return [ref[c * PAD : (c + 1) * PAD, :] for c in order]

    here = planes(out)
    first = advance(planes(far_rows), here, None, planes(prev_rows), [coef[k] for k in range(4)], sign)
    for k, c in enumerate(order):
        out[3 * PAD + 16 * c : 3 * PAD + 16 * c + 16, :] = first[k][4:20]
        out[c * PAD : c * PAD + 1, :] = first[k][3:4]
        out[c * PAD + 23 : c * PAD + 24, :] = first[k][20:21]
    for k in range(2):
        row = 1 if k == 0 else 22
        out[row : row + 1, :] = consts[k : k + 1, :]
        out[PAD + row : PAD + row + 1, :] = ghost(True, 9, pl.ds(k, 1), slice(None))
        out[2 * PAD + row : 2 * PAD + row + 1, :] = ghost(False, 9, pl.ds(k, 1), slice(None))


def pack_po_kernel(place, consts, se, so, masses, now, prev, po, coef, far_rows, prev_rows):
    ghost = ghost_of(place, se, so)
    step = lax.broadcasted_iota(jnp.int32, masses.shape, 0)
    carried = 16.0 * jnp.sum(jnp.where(step > place[0], masses[...], 0.0), 0, keepdims=True)
    own = [consts[k : k + 1, :] for k in range(4)]
    over = [ghost(True, 9, pl.ds(k, 1), slice(None)) for k in range(4)]
    under = [ghost(False, 9, pl.ds(k, 1), slice(None)) for k in range(4)]
    for k, rows in enumerate(coefficients(own, over, under, carried)):
        coef[k] = rows
    even_plan = place[1] % 2 == 0

    @pl.when(even_plan)
    def _():
        fill(ghost, consts, coef, now, prev, po, far_rows, prev_rows, 0, 1, -1.0)

    @pl.when(jnp.logical_not(even_plan))
    def _():
        fill(ghost, consts, coef, now, prev, po, far_rows, prev_rows, 15, 14, None)


def advance(below, here, above, before, coefs, sign):
    a, b, gu, gd = coefs
    lap, coup = stencil(below, here, above, sign)
    news = []
    for c in range(3):
        lower, upper = row_shift(here[c])
        news.append(update(here[c], before[c], lap[c], coup[c], a, b, gu, gd, lower, upper))
    return news


def update(here, before, lap, coup, a, b, gu, gd, below, above):
    geometric = gu * (above - here) - gd * (here - below)
    return 2.0 * here - before + a * lap + b * coup - geometric


def main_kernel(place, consts, coef, se, so, now, prev, out, u0, u1, before):
    ghost = ghost_of(place, se, so)
    occupied = jnp.broadcast_to(consts[4:5, :], (16, WIDE))
    for c in range(3):
        u0[c, 0] = ghost(False, 3 + c)
        u0[c, 1] = ghost(False, c)
        u0[c, 18] = ghost(True, c)
        u0[c, 19] = ghost(True, 3 + c)
        before[c, 0] = ghost(False, 6 + c)
        before[c, 17] = ghost(True, 6 + c)

    @pl.loop(0, 16, unroll=4)
    def _(z):
        for c in range(3):
            u0[c, z + 2] = now[c, z] * occupied
            before[c, z + 1] = prev[c, z] * occupied

    def one(source, earlier, target, i, shift):
        below, here, above = ([source[c, i + k] for c in range(3)] for k in range(3))
        lap, coup = stencil(below, here, above)
        a, b, gu, gd = (coef[k, pl.ds(i + shift, 1), :] for k in range(4))
        for c in range(3):
            target[c, i] = update(here[c], earlier(c, i), lap[c], coup[c], a, b, gu, gd, below[c], above[c])

    @pl.loop(0, 18, unroll=3)
    def _(i):
        one(u0, lambda c, i: before[c, i], u1, i, 3)

    @pl.loop(0, 16, unroll=4)
    def _(i):
        one(u1, lambda c, i: u0[c, i + 2], out, i, 4)


def pack_pe_kernel(place, consts, coef, se, so, now, prev, pe, far_rows, prev_rows):
    ghost = ghost_of(place, se, so)
    even_plan = place[1] % 2 == 0

    @pl.when(even_plan)
    def _():
        fill(ghost, consts, coef, now, prev, pe, far_rows, prev_rows, 15, 14, None)

    @pl.when(jnp.logical_not(even_plan))
    def _():
        fill(ghost, consts, coef, now, prev, pe, far_rows, prev_rows, 0, 1, -1.0)


def one_side(coef, sent, got, work, held, near, far, sign):
    order = (1, 0, 2)

    def planes(ref):
        return [ref[c * PAD : (c + 1) * PAD, :] for c in order]

    for c in range(3):
        base = c * PAD
        held[base : base + 4, :] = got[base : base + 1, :] + jnp.zeros((4, WIDE), F32)
        held[base + 4 : base + 20, :] = got[3 * PAD + 16 * c : 3 * PAD + 16 * c + 16, :]
        held[base + 20 : base + PAD, :] = got[base + 23 : base + 24, :] + jnp.zeros((4, WIDE), F32)
    a, b, gu, gd = (coef[k] for k in range(4))
    z = lax.broadcasted_iota(jnp.int32, (PAD, WIDE), 0) - 4

    def pick(row):
        own, over, under = (got[k * PAD + row : k * PAD + row + 1, :] for k in range(3))
        return jnp.where(z < 0, under, jnp.where(z > 15, over, own))

    got_a, got_b = pick(1), pick(22)
    lap, coup = stencil(None, None, planes(got), sign)
    delta = [a * lap[k] + b * coup[k] for k in range(3)]
    lap, coup = stencil(planes(sent), None, None, sign)
    outer = [p + got_a * lap[k] + got_b * coup[k] for k, p in enumerate(planes(held))]
    zero = jnp.zeros((PAD, WIDE), F32)
    near_more = advance(None, delta, outer, [zero] * 3, (a, b, gu, gd), sign)
    lap, coup = stencil(None, None, delta, sign)
    for k, c in enumerate(order):
        work[c, :, near, :] += near_more[k][4:20]
        work[c, :, far, :] += (a * lap[k] + b * coup[k])[4:20]


def write_half(work, out, first, sems):
    copies = [pltpu.make_async_copy(work.at[c], out.at[c, :, pl.ds(first, 8), :], sems.at[c]) for c in range(3)]
    for copy in copies:
        copy.start()
    for copy in copies:
        copy.wait()


def tail_pe_kernel(place, coef, sent, got, inner, out, rest, work, held, sems):
    even_plan = place[1] % 2 == 0

    @pl.when(even_plan)
    def _():
        work[...] = inner[:, :, 8:16, :]
        rest[...] = inner[:, :, 0:8, :]
        one_side(coef, sent, got, work, held, 7, 6, None)
        write_half(work, out, 8, sems)

    @pl.when(jnp.logical_not(even_plan))
    def _():
        work[...] = inner[:, :, 0:8, :]
        rest[...] = inner[:, :, 8:16, :]
        one_side(coef, sent, got, work, held, 0, 1, -1.0)
        write_half(work, out, 0, sems)


def tail_po_kernel(place, coef, sent, got, rest, half, out, work, held, sems):
    even_plan = place[1] % 2 == 0
    work[...] = rest[...]

    @pl.when(even_plan)
    def _():
        one_side(coef, sent, got, work, held, 0, 1, -1.0)
        write_half(work, out, 0, sems)

    @pl.when(jnp.logical_not(even_plan))
    def _():
        one_side(coef, sent, got, work, held, 7, 6, None)
        write_half(work, out, 8, sems)


VM = pl.BlockSpec(memory_space=pltpu.VMEM)
SM = pl.BlockSpec(memory_space=pltpu.SMEM)
HB = pl.BlockSpec(memory_space=pltpu.HBM)


def shape(*dims):
    return jax.ShapeDtypeStruct(dims, F32)


def call(kernel, outs, ins, scratch=(), flops=0, moved=0, grant=24.0, places=None, aliases=None):
    return pl.pallas_call(
        kernel,
        out_shape=outs,
        in_specs=ins,
        out_specs=places or [VM] * len(outs),
        scratch_shapes=list(scratch),
        input_output_aliases=aliases or {},
        compiler_params=pltpu.CompilerParams(vmem_limit_bytes=int(grant * 2**20)),
        cost_estimate=pl.CostEstimate(flops=flops, bytes_accessed=moved, transcendentals=0),
    )


def local(u_now, u_prev, occupancy, materials, shear_table, lame_table, density_table):
    height = u_now.shape[1] * lax.axis_size("story")
    stories = lax.axis_size("story")
    place = jnp.stack([lax.axis_index("story"), lax.axis_index("plan")]).astype(jnp.int32)
    face, table = shape(10, 16, WIDE), shape(4, PAD, WIDE)
    rows = 3 * PAD + 48
    planes = [pltpu.VMEM((3 * PAD, WIDE), F32)] * 2
    se, so, masses, consts = call(
        functools.partial(prep_kernel, factor=0.8 / height),
        [face, face, shape(stories, WIDE), shape(8, WIDE)],
        [SM] * 6 + [HB] * 2,
        [
            pltpu.VMEM((2, 3, 2, 16, WIDE), F32),
            pltpu.VMEM((2, 3, 1, 16, WIDE), F32),
            pltpu.SemaphoreType.DMA((4,)),
        ],
        moved=1 << 20,
        grant=53.2,
    )(place, occupancy.reshape(-1), materials.reshape(-1), shear_table, lame_table, density_table, u_now, u_prev)
    so_got = swap(so, "story", 1)
    se_got = swap(se, "story", 0)
    masses = lax.all_to_all(masses, "story", 0, 0, tiled=True)
    cells = u_now.shape
    po, coef = call(pack_po_kernel, [shape(rows + 8, WIDE), table], [SM] + [VM] * 6, planes, moved=1 << 20)(
        place, consts, se_got, so_got, masses, u_now, u_prev
    )
    po_got = swap(po, "plan", 1)
    levels = [
        pltpu.VMEM((3, 20, 16, WIDE), F32),
        pltpu.VMEM((3, 18, 16, WIDE), F32),
        pltpu.VMEM((3, 18, 16, WIDE), F32),
    ]
    (pe,) = call(pack_pe_kernel, [shape(rows, WIDE)], [SM] + [VM] * 6, planes, moved=1 << 20)(
        place, consts, coef, se_got, so_got, u_now, u_prev
    )
    pe_got = swap(pe, "plan", 0)
    (inner,) = call(main_kernel, [shape(*cells)], [SM] + [VM] * 6, levels, flops=60_000_000, moved=4 << 20)(
        place, consts, coef, se_got, so_got, u_now, u_prev
    )
    half = shape(3, 16, 8, WIDE)
    work = [pltpu.VMEM((3, 16, 8, WIDE), F32), pltpu.VMEM((3 * PAD, WIDE), F32), pltpu.SemaphoreType.DMA((3,))]
    out, rest = call(
        tail_pe_kernel, [shape(*cells), half], [SM] + [VM] * 4, work, flops=5_000_000, moved=2 << 20, places=[HB, VM]
    )(place, coef, pe, pe_got, inner)
    (out,) = call(
        tail_po_kernel, [shape(*cells)], [SM] + [VM] * 4 + [HB], work, flops=5_000_000, moved=2 << 20, places=[HB], aliases={5: 0}
    )(place, coef, po, po_got, rest, out)
    return out


def solution(mesh):
    in_specs = (
        P(None, "story", "plan", None),
        P(None, "story", "plan", None),
        P("story", "plan", None),
        P("story", "plan", None),
        P(),
        P(),
        P(),
    )
    out_specs = P(None, "story", "plan", None)
    return jax.shard_map(local, mesh=mesh, in_specs=in_specs, out_specs=out_specs, check_vma=False)
```

```python
import functools

import jax
import jax.numpy as jnp
from jax import lax
from jax.experimental import pallas as pl
from jax.experimental.pallas import tpu as pltpu
from jax.sharding import PartitionSpec as P

BLOCK = 16
WIDE = 256
PAD = 24
F32 = jnp.float32


def swap(values, axis, first):
    pairs = []
    for low in range(first, lax.axis_size(axis) - 1, 2):
        pairs += [(low, low + 1), (low + 1, low)]
    return lax.ppermute(values, axis, pairs)


def row_shift(v):
    count = v.shape[0] // 8
    row = lax.broadcasted_iota(jnp.int32, (8, v.shape[1]), 0)
    tiles = [v[8 * k : 8 * k + 8] for k in range(count)]
    down = [jnp.zeros_like(tiles[0])] + [pltpu.roll(t, 1, 0) for t in tiles]
    up = [pltpu.roll(t, 7, 0) for t in tiles] + [jnp.zeros_like(tiles[0])]
    lower = [jnp.where(row == 0, down[k], down[k + 1]) for k in range(count)]
    upper = [jnp.where(row == 7, up[k + 1], up[k]) for k in range(count)]
    return jnp.concatenate(lower, 0), jnp.concatenate(upper, 0)


def lane_shift(v):
    half = WIDE // 2
    lane = lax.broadcasted_iota(jnp.int32, (v.shape[0], half), 1)
    first, second = v[:, :half], v[:, half:]
    first_down, second_down = pltpu.roll(first, 1, 1), pltpu.roll(second, 1, 1)
    first_up, second_up = pltpu.roll(first, half - 1, 1), pltpu.roll(second, half - 1, 1)
    lower = [jnp.where(lane == 0, 0.0, first_down), jnp.where(lane == 0, first_down, second_down)]
    upper = [jnp.where(lane == half - 1, second_up, first_up), jnp.where(lane == half - 1, 0.0, second_up)]
    return jnp.concatenate(lower, 1), jnp.concatenate(upper, 1)


def lane_smooth(v):
    lower, upper = lane_shift(v)
    return lower + upper + 4.0 * v


def lane_first(v):
    lower, upper = lane_shift(v)
    return upper - lower


def total(terms):
    terms = [t for t in terms if t is not None]
    return functools.reduce(lambda p, q: p + q, terms)


def stencil(below, here, above, sign=None):
    zs, zf = [], []
    for j in range(3):
        zs.append(total([below and below[j], above and above[j], here and 4.0 * here[j]]))
        if below and above:
            zf.append(above[j] - below[j])
        else:
            zf.append(above[j] if above else -below[j])
    if sign is not None:
        zf = [sign * v for v in zf]
    zs_sh = [row_shift(v) for v in zs]
    zf_sh = [row_shift(v) for v in zf]
    s_zs = [lo + up + 4.0 * v for (lo, up), v in zip(zs_sh, zs)]
    lap = []
    if here:
        s_mid = [lo + up + 4.0 * v for (lo, up), v in zip([row_shift(v) for v in here], here)]
        inner = [s_zs[j] - 2.0 * (s_mid[j] + zs[j]) for j in range(3)]
        curl = 2.0 * s_zs[0] - 12.0 * s_mid[0]
    else:
        inner = [s_zs[j] - 2.0 * zs[j] for j in range(3)]
        curl = 2.0 * s_zs[0]
    for j in range(3):
        lap.append(lane_smooth(inner[j]) - 2.0 * s_zs[j])
    f_zf0 = zf_sh[0][1] - zf_sh[0][0]
    f_zf1 = zf_sh[1][1] - zf_sh[1][0]
    s_zf0 = zf_sh[0][0] + zf_sh[0][1] + 4.0 * zf[0]
    s_zf2 = zf_sh[2][0] + zf_sh[2][1] + 4.0 * zf[2]
    f_zs1 = zs_sh[1][1] - zs_sh[1][0]
    f_zs2 = zs_sh[2][1] - zs_sh[2][0]
    c0 = lane_smooth(curl + 3.0 * f_zf1) + lane_first(3.0 * s_zf2)
    c1 = lane_smooth(2.0 * s_zs[1] - 12.0 * zs[1] + 3.0 * f_zf0) + lane_first(3.0 * f_zs2)
    c2 = lane_first(3.0 * (s_zf0 + f_zs1)) + 2.0 * lane_smooth(s_zs[2]) - 12.0 * s_zs[2]
    return lap, [c0, c1, c2]


def coefficients(own, over, under, carried):
    z = lax.broadcasted_iota(jnp.int32, (PAD, WIDE), 0) - 4
    zf = z.astype(F32)

    def pick(k):
        return jnp.where(z < 0, under[k], jnp.where(z > 15, over[k], own[k]))

    a, b, g = pick(0), pick(1), pick(2)
    mass, mass_over, mass_under = own[3], over[3], under[3]
    upper = jnp.where(z > 15, carried - mass_over, carried + mass * (15.0 - zf))
    lower = jnp.where(z < 0, carried + 16.0 * mass + mass_under, carried + mass * (16.0 - zf))
    return a, b, g * upper, g * lower


def prep_kernel(place, occ, mat, shear_t, lame_t, dens_t, now, prev, se, so, masses, consts, held_now, held_prev, sems, *, factor):
    top_first = place[0] % 2 == 0
    copies = []
    for k in range(2):
        top = jnp.logical_xor(top_first, k == 1)
        copies.append(pltpu.make_async_copy(now.at[:, pl.ds(jnp.where(top, 14, 0), 2)], held_now.at[k], sems.at[2 * k]))
        copies.append(pltpu.make_async_copy(prev.at[:, pl.ds(jnp.where(top, 15, 0), 1)], held_prev.at[k], sems.at[2 * k + 1]))
    for copy in copies:
        copy.start()
    block = lax.broadcasted_iota(jnp.int32, (1, WIDE), 1) // BLOCK
    zero = jnp.zeros((1, WIDE), F32)
    occupied, shear, lame, dens = zero, zero, zero, zero
    for j in range(BLOCK):
        at = block == j
        which = mat[j]
        occupied = jnp.where(at, occ[j].astype(F32), occupied)
        shear = jnp.where(at, shear_t[which], shear)
        lame = jnp.where(at, lame_t[which], lame)
        dens = jnp.where(at, dens_t[which], dens)
    scale = occupied * (0.1 / dens)
    own = [scale * shear * (1.0 / 12.0), scale * (lame + shear) * (1.0 / 72.0), scale * factor, dens * occupied, occupied]
    for k, row in enumerate(own):
        consts[k : k + 1, :] = row
    consts[5:8, :] = jnp.zeros((3, WIDE), F32)
    masses[...] = jnp.broadcast_to(own[3], masses.shape)
    for copy in copies:
        copy.wait()
    for k, out in enumerate((se, so)):
        top = jnp.logical_xor(top_first, k == 1)
        for c in range(3):
            first, second = held_now[k, c, 0] * occupied, held_now[k, c, 1] * occupied
            out[c] = jnp.where(top, second, first)
            out[3 + c] = jnp.where(top, first, second)
            out[6 + c] = held_prev[k, c, 0] * occupied
        out[9, 0:8] = consts[...]


def ghost_of(place, se, so):
    even_story = place[0] % 2 == 0

    def ghost(over, *where):
        take = even_story if over else jnp.logical_not(even_story)
        return jnp.where(take, se[where], so[where])

    return ghost


def fill(right, ghost, consts, coef, now, prev, out, far_rows, prev_rows):
    occupied = consts[4:5, :]

    def load(near, far):
        for c in range(3):
            for target, source, x in ((out, now, near), (far_rows, now, far), (prev_rows, prev, near)):
                base = c * PAD
                target[base + 4 : base + 20, :] = source[c, :, x, :] * occupied
                kinds = (6,) if source is prev else (0, 3)
                for k, kind in enumerate(kinds):
                    target[base + 3 - k : base + 4 - k, :] = ghost(False, kind + c, pl.ds(x, 1), slice(None))
                    target[base + 20 + k : base + 21 + k, :] = ghost(True, kind + c, pl.ds(x, 1), slice(None))

    @pl.when(right)
    def _():
        load(15, 14)

    @pl.when(jnp.logical_not(right))
    def _():
        load(0, 1)

    order = (1, 0, 2)

    def planes(ref):
        return [ref[c * PAD : (c + 1) * PAD, :] for c in order]

    first = advance(planes(far_rows), planes(out), None, planes(prev_rows), [coef[k] for k in range(4)], jnp.where(right, 1.0, -1.0))
    for k, c in enumerate(order):
        out[3 * PAD + 16 * c : 3 * PAD + 16 * c + 16, :] = first[k][4:20]
        out[c * PAD : c * PAD + 1, :] = first[k][3:4]
        out[c * PAD + 23 : c * PAD + 24, :] = first[k][20:21]
    for k in range(2):
        row = 1 if k == 0 else 22
        out[row : row + 1, :] = consts[k : k + 1, :]
        out[PAD + row : PAD + row + 1, :] = ghost(True, 9, pl.ds(k, 1), slice(None))
        out[2 * PAD + row : 2 * PAD + row + 1, :] = ghost(False, 9, pl.ds(k, 1), slice(None))


def pack_po_kernel(place, consts, se, so, masses, now, prev, po, coef, far_rows, prev_rows):
    ghost = ghost_of(place, se, so)
    step = lax.broadcasted_iota(jnp.int32, masses.shape, 0)
    carried = 16.0 * jnp.sum(jnp.where(step > place[0], masses[...], 0.0), 0, keepdims=True)
    own = [consts[k : k + 1, :] for k in range(4)]
    over = [ghost(True, 9, pl.ds(k, 1), slice(None)) for k in range(4)]
    under = [ghost(False, 9, pl.ds(k, 1), slice(None)) for k in range(4)]
    for k, rows in enumerate(coefficients(own, over, under, carried)):
        coef[k] = rows
    fill(place[1] % 2 == 1, ghost, consts, coef, now, prev, po, far_rows, prev_rows)


def advance(below, here, above, before, coefs, sign):
    a, b, gu, gd = coefs
    lap, coup = stencil(below, here, above, sign)
    news = []
    for c in range(3):
        lower, upper = row_shift(here[c])
        news.append(update(here[c], before[c], lap[c], coup[c], a, b, gu, gd, lower, upper))
    return news


def update(here, before, lap, coup, a, b, gu, gd, below, above):
    geometric = gu * (above - here) - gd * (here - below)
    return 2.0 * here - before + a * lap + b * coup - geometric


def crosses(place, plans):
    return jnp.logical_or(place[1] == plans // 2 - 1, place[1] == plans // 2)


def both_steps(place, consts, coef, se, so, now, prev, out, u0, u1, before):
    ghost = ghost_of(place, se, so)
    occupied = jnp.broadcast_to(consts[4:5, :], (16, WIDE))
    for c in range(3):
        u0[c, 0] = ghost(False, 3 + c)
        u0[c, 1] = ghost(False, c)
        u0[c, 18] = ghost(True, c)
        u0[c, 19] = ghost(True, 3 + c)
        before[c, 0] = ghost(False, 6 + c)
        before[c, 17] = ghost(True, 6 + c)

    @pl.loop(0, 16, unroll=4)
    def _(z):
        for c in range(3):
            u0[c, z + 2] = now[c, z] * occupied
            before[c, z + 1] = prev[c, z] * occupied

    def one(source, earlier, target, i, shift):
        below, here, above = ([source[c, i + k] for c in range(3)] for k in range(3))
        lap, coup = stencil(below, here, above)
        a, b, gu, gd = (coef[k, pl.ds(i + shift, 1), :] for k in range(4))
        for c in range(3):
            target[c, i] = update(here[c], earlier(c, i), lap[c], coup[c], a, b, gu, gd, below[c], above[c])

    @pl.loop(0, 18, unroll=3)
    def _(i):
        one(u0, lambda c, i: before[c, i], u1, i, 3)

    @pl.loop(0, 16, unroll=4)
    def _(i):
        one(u1, lambda c, i: u0[c, i + 2], out, i, 4)


def early_kernel(place, consts, coef, se, so, now, prev, pe, out, far_rows, prev_rows, u0, u1, before, *, plans):
    fill(place[1] % 2 == 0, ghost_of(place, se, so), consts, coef, now, prev, pe, far_rows, prev_rows)

    @pl.when(jnp.logical_not(crosses(place, plans)))
    def _():
        both_steps(place, consts, coef, se, so, now, prev, out, u0, u1, before)


def late_kernel(place, consts, coef, se, so, now, prev, out, u0, u1, before, *, plans):
    @pl.when(crosses(place, plans))
    def _():
        both_steps(place, consts, coef, se, so, now, prev, out, u0, u1, before)


def one_side(coef, sent, got, held, sign):
    order = (1, 0, 2)

    def planes(ref):
        return [ref[c * PAD : (c + 1) * PAD, :] for c in order]

    for c in range(3):
        base = c * PAD
        held[base : base + 4, :] = got[base : base + 1, :] + jnp.zeros((4, WIDE), F32)
        held[base + 4 : base + 20, :] = got[3 * PAD + 16 * c : 3 * PAD + 16 * c + 16, :]
        held[base + 20 : base + PAD, :] = got[base + 23 : base + 24, :] + jnp.zeros((4, WIDE), F32)
    a, b, gu, gd = (coef[k] for k in range(4))
    z = lax.broadcasted_iota(jnp.int32, (PAD, WIDE), 0) - 4

    def pick(row):
        own, over, under = (got[k * PAD + row : k * PAD + row + 1, :] for k in range(3))
        return jnp.where(z < 0, under, jnp.where(z > 15, over, own))

    got_a, got_b = pick(1), pick(22)
    lap, coup = stencil(None, None, planes(got), sign)
    delta = [a * lap[k] + b * coup[k] for k in range(3)]
    lap, coup = stencil(planes(sent), None, None, sign)
    outer = [p + got_a * lap[k] + got_b * coup[k] for k, p in enumerate(planes(held))]
    zero = jnp.zeros((PAD, WIDE), F32)
    near_more = advance(None, delta, outer, [zero] * 3, (a, b, gu, gd), sign)
    lap, coup = stencil(None, None, delta, sign)
    near, far = [None] * 3, [None] * 3
    for k, c in enumerate(order):
        near[c] = near_more[k][4:20]
        far[c] = (a * lap[k] + b * coup[k])[4:20]
    return near, far


def write_half(right, near, far, work, out, sems):
    def put(near_row, far_row, first):
        copies = []
        for c in range(3):
            work[c, :, near_row, :] += near[c]
            work[c, :, far_row, :] += far[c]
            copies.append(pltpu.make_async_copy(work.at[c], out.at[c, :, pl.ds(first, 8), :], sems.at[c]))
            copies[-1].start()
        for copy in copies:
            copy.wait()

    @pl.when(right)
    def _():
        put(7, 6, 8)

    @pl.when(jnp.logical_not(right))
    def _():
        put(0, 1, 0)


def tail_pe_kernel(place, coef, sent, got, early, late, out, rest, work, held, sems, *, plans):
    right = place[1] % 2 == 0
    for inner, use in ((late, crosses(place, plans)), (early, jnp.logical_not(crosses(place, plans)))):

        @pl.when(jnp.logical_and(use, right))
        def _(inner=inner):
            work[...] = inner[:, :, 8:16, :]
            rest[...] = inner[:, :, 0:8, :]

        @pl.when(jnp.logical_and(use, jnp.logical_not(right)))
        def _(inner=inner):
            work[...] = inner[:, :, 0:8, :]
            rest[...] = inner[:, :, 8:16, :]

    near, far = one_side(coef, sent, got, held, jnp.where(right, 1.0, -1.0))
    write_half(right, near, far, work, out, sems)


def tail_po_kernel(place, coef, sent, got, rest, half, out, work, held, sems):
    right = place[1] % 2 == 1
    work[...] = rest[...]
    near, far = one_side(coef, sent, got, held, jnp.where(right, 1.0, -1.0))
    write_half(right, near, far, work, out, sems)


VM = pl.BlockSpec(memory_space=pltpu.VMEM)
SM = pl.BlockSpec(memory_space=pltpu.SMEM)
HB = pl.BlockSpec(memory_space=pltpu.HBM)


def shape(*dims):
    return jax.ShapeDtypeStruct(dims, F32)


def call(kernel, outs, ins, scratch=(), flops=0, moved=0, grant=24.0, places=None, aliases=None):
    return pl.pallas_call(
        kernel,
        out_shape=outs,
        in_specs=ins,
        out_specs=places or [VM] * len(outs),
        scratch_shapes=list(scratch),
        input_output_aliases=aliases or {},
        compiler_params=pltpu.CompilerParams(vmem_limit_bytes=int(grant * 2**20)),
        cost_estimate=pl.CostEstimate(flops=flops, bytes_accessed=moved, transcendentals=0),
    )


def local(u_now, u_prev, occupancy, materials, shear_table, lame_table, density_table):
    height = u_now.shape[1] * lax.axis_size("story")
    stories, plans = lax.axis_size("story"), lax.axis_size("plan")
    place = jnp.stack([lax.axis_index("story"), lax.axis_index("plan")]).astype(jnp.int32)
    face, table = shape(10, 16, WIDE), shape(4, PAD, WIDE)
    rows = 3 * PAD + 48
    planes = [pltpu.VMEM((3 * PAD, WIDE), F32)] * 2
    se, so, masses, consts = call(
        functools.partial(prep_kernel, factor=0.8 / height),
        [face, face, shape(stories, WIDE), shape(8, WIDE)],
        [SM] * 6 + [HB] * 2,
        [
            pltpu.VMEM((2, 3, 2, 16, WIDE), F32),
            pltpu.VMEM((2, 3, 1, 16, WIDE), F32),
            pltpu.SemaphoreType.DMA((4,)),
        ],
        moved=1 << 20,
        grant=53.2,
    )(place, occupancy.reshape(-1), materials.reshape(-1), shear_table, lame_table, density_table, u_now, u_prev)
    so_got = swap(so, "story", 1)
    se_got = swap(se, "story", 0)
    masses = lax.all_to_all(masses, "story", 0, 0, tiled=True)
    cells = u_now.shape
    po, coef = call(pack_po_kernel, [shape(rows + 8, WIDE), table], [SM] + [VM] * 6, planes, moved=1 << 20)(
        place, consts, se_got, so_got, masses, u_now, u_prev
    )
    po_got = swap(po, "plan", 1)
    levels = [
        pltpu.VMEM((3, 20, 16, WIDE), F32),
        pltpu.VMEM((3, 18, 16, WIDE), F32),
        pltpu.VMEM((3, 18, 16, WIDE), F32),
    ]
    own = (place, consts, coef, se_got, so_got, u_now, u_prev)
    pe, early = call(
        functools.partial(early_kernel, plans=plans),
        [shape(rows, WIDE), shape(*cells)],
        [SM] + [VM] * 6,
        planes + levels,
        flops=60_000_000,
        moved=4 << 20,
    )(*own)
    pe_got = swap(pe, "plan", 0)
    (late,) = call(
        functools.partial(late_kernel, plans=plans), [shape(*cells)], [SM] + [VM] * 6, levels, flops=60_000_000, moved=4 << 20
    )(*own)
    half = shape(3, 16, 8, WIDE)
    work = [pltpu.VMEM((3, 16, 8, WIDE), F32), pltpu.VMEM((3 * PAD, WIDE), F32), pltpu.SemaphoreType.DMA((3,))]
    out, rest = call(
        functools.partial(tail_pe_kernel, plans=plans),
        [shape(*cells), half],
        [SM] + [VM] * 5,
        work,
        flops=5_000_000,
        moved=2 << 20,
        places=[HB, VM],
    )(place, coef, pe, pe_got, early, late)
    (out,) = call(
        tail_po_kernel, [shape(*cells)], [SM] + [VM] * 4 + [HB], work, flops=5_000_000, moved=2 << 20, places=[HB], aliases={5: 0}
    )(place, coef, po, po_got, rest, out)
    return out


def solution(mesh):
    in_specs = (
        P(None, "story", "plan", None),
        P(None, "story", "plan", None),
        P("story", "plan", None),
        P("story", "plan", None),
        P(),
        P(),
        P(),
    )
    out_specs = P(None, "story", "plan", None)
    return jax.shard_map(local, mesh=mesh, in_specs=in_specs, out_specs=out_specs, check_vma=False)
```

```python
import functools

import jax
import jax.numpy as jnp
from jax import lax
from jax.experimental import pallas as pl
from jax.experimental.pallas import tpu as pltpu
from jax.sharding import PartitionSpec as P

BLOCK = 16
WIDE = 256
PAD = 24
F32 = jnp.float32


def swap(values, axis, first):
    pairs = []
    for low in range(first, lax.axis_size(axis) - 1, 2):
        pairs += [(low, low + 1), (low + 1, low)]
    return lax.ppermute(values, axis, pairs)


def row_shift(v):
    count = v.shape[0] // 8
    row = lax.broadcasted_iota(jnp.int32, (8, v.shape[1]), 0)
    tiles = [v[8 * k : 8 * k + 8] for k in range(count)]
    down = [jnp.zeros_like(tiles[0])] + [pltpu.roll(t, 1, 0) for t in tiles]
    up = [pltpu.roll(t, 7, 0) for t in tiles] + [jnp.zeros_like(tiles[0])]
    lower = [jnp.where(row == 0, down[k], down[k + 1]) for k in range(count)]
    upper = [jnp.where(row == 7, up[k + 1], up[k]) for k in range(count)]
    return jnp.concatenate(lower, 0), jnp.concatenate(upper, 0)


def lane_shift(v):
    half = WIDE // 2
    lane = lax.broadcasted_iota(jnp.int32, (v.shape[0], half), 1)
    first, second = v[:, :half], v[:, half:]
    first_down, second_down = pltpu.roll(first, 1, 1), pltpu.roll(second, 1, 1)
    first_up, second_up = pltpu.roll(first, half - 1, 1), pltpu.roll(second, half - 1, 1)
    lower = [jnp.where(lane == 0, 0.0, first_down), jnp.where(lane == 0, first_down, second_down)]
    upper = [jnp.where(lane == half - 1, second_up, first_up), jnp.where(lane == half - 1, 0.0, second_up)]
    return jnp.concatenate(lower, 1), jnp.concatenate(upper, 1)


def lane_smooth(v):
    lower, upper = lane_shift(v)
    return lower + upper + 4.0 * v


def lane_first(v):
    lower, upper = lane_shift(v)
    return upper - lower


def total(terms):
    terms = [t for t in terms if t is not None]
    return functools.reduce(lambda p, q: p + q, terms)


def stencil(below, here, above, sign=None):
    zs, zf = [], []
    for j in range(3):
        zs.append(total([below and below[j], above and above[j], here and 4.0 * here[j]]))
        if below and above:
            zf.append(above[j] - below[j])
        else:
            zf.append(above[j] if above else -below[j])
    if sign is not None:
        zf = [sign * v for v in zf]
    zs_sh = [row_shift(v) for v in zs]
    zf_sh = [row_shift(v) for v in zf]
    s_zs = [lo + up + 4.0 * v for (lo, up), v in zip(zs_sh, zs)]
    lap = []
    if here:
        s_mid = [lo + up + 4.0 * v for (lo, up), v in zip([row_shift(v) for v in here], here)]
        inner = [s_zs[j] - 2.0 * (s_mid[j] + zs[j]) for j in range(3)]
        curl = 2.0 * s_zs[0] - 12.0 * s_mid[0]
    else:
        inner = [s_zs[j] - 2.0 * zs[j] for j in range(3)]
        curl = 2.0 * s_zs[0]
    for j in range(3):
        lap.append(lane_smooth(inner[j]) - 2.0 * s_zs[j])
    f_zf0 = zf_sh[0][1] - zf_sh[0][0]
    f_zf1 = zf_sh[1][1] - zf_sh[1][0]
    s_zf0 = zf_sh[0][0] + zf_sh[0][1] + 4.0 * zf[0]
    s_zf2 = zf_sh[2][0] + zf_sh[2][1] + 4.0 * zf[2]
    f_zs1 = zs_sh[1][1] - zs_sh[1][0]
    f_zs2 = zs_sh[2][1] - zs_sh[2][0]
    c0 = lane_smooth(curl + 3.0 * f_zf1) + lane_first(3.0 * s_zf2)
    c1 = lane_smooth(2.0 * s_zs[1] - 12.0 * zs[1] + 3.0 * f_zf0) + lane_first(3.0 * f_zs2)
    c2 = lane_first(3.0 * (s_zf0 + f_zs1)) + 2.0 * lane_smooth(s_zs[2]) - 12.0 * s_zs[2]
    return lap, [c0, c1, c2]


def coefficients(own, over, under, carried):
    z = lax.broadcasted_iota(jnp.int32, (PAD, WIDE), 0) - 4
    zf = z.astype(F32)

    def pick(k):
        return jnp.where(z < 0, under[k], jnp.where(z > 15, over[k], own[k]))

    a, b, g = pick(0), pick(1), pick(2)
    mass, mass_over, mass_under = own[3], over[3], under[3]
    upper = jnp.where(z > 15, carried - mass_over, carried + mass * (15.0 - zf))
    lower = jnp.where(z < 0, carried + 16.0 * mass + mass_under, carried + mass * (16.0 - zf))
    return a, b, g * upper, g * lower


def parity(axis):
    return lax.axis_index(axis) % 2 == 0


def slice_kernel(now, prev, se, so, sems):
    even = parity("story")
    copies = []
    for k, out in enumerate((se, so)):
        top = jnp.logical_xor(even, k == 1)
        near, far = jnp.where(top, 15, 0), jnp.where(top, 14, 1)
        for j, (source, z) in enumerate(((now, near), (now, far), (prev, near))):
            copies.append(pltpu.make_async_copy(source.at[:, z], out.at[pl.ds(3 * j, 3)], sems.at[3 * k + j]))
    for copy in copies:
        copy.start()
    for copy in copies:
        copy.wait()


def block_kernel(occ, mat, shear_t, lame_t, dens_t, out, held, *, factor):
    segment = lax.broadcasted_iota(jnp.int32, (8, 128), 1) // BLOCK

    def repeat(ref):
        held[...] = jnp.zeros((8, 128), F32)
        held[0:1, 0:BLOCK] = ref[...].astype(F32)
        once = held[...]
        return once + sum(pltpu.roll(once, BLOCK * k, 1) for k in range(1, 5))

    occupied, which = repeat(occ), repeat(mat)
    found = []
    for table in (shear_t, lame_t, dens_t):
        value = jnp.zeros((8, 128), F32)
        for k in range(table.shape[1]):
            value = jnp.where(which == k, table[0:1, k : k + 1], value)
        found.append(value)
    shear, lame, dens = found
    scale = occupied * (0.1 / dens)
    parts = (scale * shear * (1.0 / 12.0), scale * (lame + shear) * (1.0 / 72.0), scale * factor, dens * occupied, occupied)
    row = jnp.zeros((8, 128), F32)
    for k, part in enumerate(parts):
        row = jnp.where(segment == k, part, row)
    out[...] = jnp.broadcast_to(row[0:1], out.shape)


def ghost_of(se, so, consts):
    even = parity("story")

    def ghost(over, plane, *where):
        take = even if over else jnp.logical_not(even)
        row = 9 if over else 14
        return jnp.where(take, se[(plane,) + where], so[(plane,) + where]) * consts[row : row + 1, :]

    return ghost


def fill(right, ghost, consts, coef, now, prev, out, far_rows, prev_rows):
    occupied = consts[4:5, :]

    def load(near, far):
        for c in range(3):
            for target, source, x in ((out, now, near), (far_rows, now, far), (prev_rows, prev, near)):
                base = c * PAD
                target[base + 4 : base + 20, :] = source[c, :, x, :] * occupied
                kinds = (6,) if source is prev else (0, 3)
                for k, kind in enumerate(kinds):
                    target[base + 3 - k : base + 4 - k, :] = ghost(False, kind + c, pl.ds(x, 1), slice(None))
                    target[base + 20 + k : base + 21 + k, :] = ghost(True, kind + c, pl.ds(x, 1), slice(None))

    @pl.when(right)
    def _():
        load(15, 14)

    @pl.when(jnp.logical_not(right))
    def _():
        load(0, 1)

    order = (1, 0, 2)

    def planes(ref):
        return [ref[c * PAD : (c + 1) * PAD, :] for c in order]

    first = advance(planes(far_rows), planes(out), None, planes(prev_rows), [coef[k] for k in range(4)], jnp.where(right, 1.0, -1.0))
    for k, c in enumerate(order):
        out[3 * PAD + 16 * c : 3 * PAD + 16 * c + 16, :] = first[k][4:20]
        out[c * PAD : c * PAD + 1, :] = first[k][3:4]
        out[c * PAD + 23 : c * PAD + 24, :] = first[k][20:21]
    for k, row in enumerate((1, 22)):
        for j in range(3):
            out[j * PAD + row : j * PAD + row + 1, :] = consts[5 * j + k : 5 * j + k + 1, :]


def pack_po_kernel(blocks, se, so, now, prev, po, coef, consts, far_rows, prev_rows):
    place = lax.axis_index("story")
    step = lax.broadcasted_iota(jnp.int32, blocks.shape, 0)
    rows = [jnp.sum(jnp.where(step == place + k, blocks[...], 0.0), 0, keepdims=True) for k in (0, 1, -1)]
    rows.append(16.0 * jnp.sum(jnp.where(step > place, blocks[...], 0.0), 0, keepdims=True))
    stacked = jnp.concatenate(rows + [jnp.zeros((4, 128), F32)], 0)
    lane = lax.broadcasted_iota(jnp.int32, (8, 128), 1) // BLOCK

    def spread(k):
        halves = [jnp.take_along_axis(stacked, lane + (BLOCK * k + 8 * h), 1, mode="promise_in_bounds") for h in (0, 1)]
        return jnp.concatenate(halves, 1)

    sets = [[], [], []]
    for k in range(5):
        wide = spread(k)
        for j in range(3):
            sets[j].append(wide[j : j + 1])
            consts[5 * j + k : 5 * j + k + 1, :] = wide[j : j + 1]
        if k == 3:
            carried = wide[3:4]
    consts[15:16, :] = carried
    for k, value in enumerate(coefficients(sets[0], sets[1], sets[2], carried)):
        coef[k] = value
    fill(jnp.logical_not(parity("plan")), ghost_of(se, so, consts), consts, coef, now, prev, po, far_rows, prev_rows)


def advance(below, here, above, before, coefs, sign):
    a, b, gu, gd = coefs
    lap, coup = stencil(below, here, above, sign)
    news = []
    for c in range(3):
        lower, upper = row_shift(here[c])
        news.append(update(here[c], before[c], lap[c], coup[c], a, b, gu, gd, lower, upper))
    return news


def update(here, before, lap, coup, a, b, gu, gd, below, above):
    geometric = gu * (above - here) - gd * (here - below)
    return 2.0 * here - before + a * lap + b * coup - geometric


def crosses(plans):
    place = lax.axis_index("plan")
    return jnp.logical_or(place == plans // 2 - 1, place == plans // 2)


def both_steps(consts, coef, se, so, now, prev, out, u0, u1, before):
    ghost = ghost_of(se, so, consts)
    occupied = jnp.broadcast_to(consts[4:5, :], (16, WIDE))
    for c in range(3):
        u0[c, 0] = ghost(False, 3 + c)
        u0[c, 1] = ghost(False, c)
        u0[c, 18] = ghost(True, c)
        u0[c, 19] = ghost(True, 3 + c)
        before[c, 0] = ghost(False, 6 + c)
        before[c, 17] = ghost(True, 6 + c)

    @pl.loop(0, 16, unroll=4)
    def _(z):
        for c in range(3):
            u0[c, z + 2] = now[c, z] * occupied
            before[c, z + 1] = prev[c, z] * occupied

    def one(source, earlier, target, i, shift):
        below, here, above = ([source[c, i + k] for c in range(3)] for k in range(3))
        lap, coup = stencil(below, here, above)
        a, b, gu, gd = (coef[k, pl.ds(i + shift, 1), :] for k in range(4))
        for c in range(3):
            target[c, i] = update(here[c], earlier(c, i), lap[c], coup[c], a, b, gu, gd, below[c], above[c])

    @pl.loop(0, 18, unroll=3)
    def _(i):
        one(u0, lambda c, i: before[c, i], u1, i, 3)

    @pl.loop(0, 16, unroll=4)
    def _(i):
        one(u1, lambda c, i: u0[c, i + 2], out, i, 4)


def early_kernel(consts, coef, se, so, now, prev, pe, out, far_rows, prev_rows, u0, u1, before, *, plans):
    fill(parity("plan"), ghost_of(se, so, consts), consts, coef, now, prev, pe, far_rows, prev_rows)

    @pl.when(jnp.logical_not(crosses(plans)))
    def _():
        both_steps(consts, coef, se, so, now, prev, out, u0, u1, before)


def late_kernel(consts, coef, se, so, now, prev, out, u0, u1, before, *, plans):
    @pl.when(crosses(plans))
    def _():
        both_steps(consts, coef, se, so, now, prev, out, u0, u1, before)


def one_side(coef, sent, got, held, sign):
    order = (1, 0, 2)

    def planes(ref):
        return [ref[c * PAD : (c + 1) * PAD, :] for c in order]

    for c in range(3):
        base = c * PAD
        held[base : base + 4, :] = got[base : base + 1, :] + jnp.zeros((4, WIDE), F32)
        held[base + 4 : base + 20, :] = got[3 * PAD + 16 * c : 3 * PAD + 16 * c + 16, :]
        held[base + 20 : base + PAD, :] = got[base + 23 : base + 24, :] + jnp.zeros((4, WIDE), F32)
    a, b, gu, gd = (coef[k] for k in range(4))
    z = lax.broadcasted_iota(jnp.int32, (PAD, WIDE), 0) - 4

    def pick(row):
        own, over, under = (got[k * PAD + row : k * PAD + row + 1, :] for k in range(3))
        return jnp.where(z < 0, under, jnp.where(z > 15, over, own))

    got_a, got_b = pick(1), pick(22)
    lap, coup = stencil(None, None, planes(got), sign)
    delta = [a * lap[k] + b * coup[k] for k in range(3)]
    lap, coup = stencil(planes(sent), None, None, sign)
    outer = [p + got_a * lap[k] + got_b * coup[k] for k, p in enumerate(planes(held))]
    zero = jnp.zeros((PAD, WIDE), F32)
    near_more = advance(None, delta, outer, [zero] * 3, (a, b, gu, gd), sign)
    lap, coup = stencil(None, None, delta, sign)
    near, far = [None] * 3, [None] * 3
    for k, c in enumerate(order):
        near[c] = near_more[k][4:20]
        far[c] = (a * lap[k] + b * coup[k])[4:20]
    return near, far


def write_half(right, near, far, work, out, sems):
    def put(near_row, far_row, first):
        copies = []
        for c in range(3):
            work[c, :, near_row, :] += near[c]
            work[c, :, far_row, :] += far[c]
            copies.append(pltpu.make_async_copy(work.at[c], out.at[c, :, pl.ds(first, 8), :], sems.at[c]))
            copies[-1].start()
        for copy in copies:
            copy.wait()

    @pl.when(right)
    def _():
        put(7, 6, 8)

    @pl.when(jnp.logical_not(right))
    def _():
        put(0, 1, 0)


def tail_pe_kernel(coef, sent, got, early, late, out, rest, work, held, sems, *, plans):
    right = parity("plan")
    for inner, use in ((late, crosses(plans)), (early, jnp.logical_not(crosses(plans)))):

        @pl.when(jnp.logical_and(use, right))
        def _(inner=inner):
            work[...] = inner[:, :, 8:16, :]
            rest[...] = inner[:, :, 0:8, :]

        @pl.when(jnp.logical_and(use, jnp.logical_not(right)))
        def _(inner=inner):
            work[...] = inner[:, :, 0:8, :]
            rest[...] = inner[:, :, 8:16, :]

    near, far = one_side(coef, sent, got, held, jnp.where(right, 1.0, -1.0))
    write_half(right, near, far, work, out, sems)


def tail_po_kernel(coef, sent, got, rest, half, out, work, held, sems):
    right = jnp.logical_not(parity("plan"))
    work[...] = rest[...]
    near, far = one_side(coef, sent, got, held, jnp.where(right, 1.0, -1.0))
    write_half(right, near, far, work, out, sems)


VM = pl.BlockSpec(memory_space=pltpu.VMEM)
HB = pl.BlockSpec(memory_space=pltpu.HBM)


def shape(*dims):
    return jax.ShapeDtypeStruct(dims, F32)


def call(kernel, outs, ins, scratch=(), flops=0, moved=0, grant=24.0, places=None, aliases=None):
    return pl.pallas_call(
        kernel,
        out_shape=outs,
        in_specs=ins,
        out_specs=places or [VM] * len(outs),
        scratch_shapes=list(scratch),
        input_output_aliases=aliases or {},
        compiler_params=pltpu.CompilerParams(vmem_limit_bytes=int(grant * 2**20)),
        cost_estimate=pl.CostEstimate(flops=flops, bytes_accessed=moved, transcendentals=0),
    )


def local(u_now, u_prev, occupancy, materials, shear_table, lame_table, density_table):
    height = u_now.shape[1] * lax.axis_size("story")
    stories, plans = lax.axis_size("story"), lax.axis_size("plan")
    face, table = shape(9, 16, WIDE), shape(4, PAD, WIDE)
    rows = 3 * PAD + 48
    planes = [pltpu.VMEM((3 * PAD, WIDE), F32)] * 2
    se, so = call(slice_kernel, [face, face], [HB] * 2, [pltpu.SemaphoreType.DMA((6,))], moved=1 << 20, grant=53.2)(u_now, u_prev)
    so_got = swap(so, "story", 1)
    se_got = swap(se, "story", 0)
    small = [occupancy, materials, shear_table, lame_table, density_table]
    (blocks,) = call(
        functools.partial(block_kernel, factor=0.8 / height),
        [shape(stories, 128)],
        [VM] * 5,
        [pltpu.VMEM((8, 128), F32)],
    )(*(v.reshape(1, -1) for v in small))
    blocks = lax.all_to_all(blocks, "story", 0, 0, tiled=True)
    cells = u_now.shape
    po, coef, consts = call(pack_po_kernel, [shape(rows + 8, WIDE), table, shape(16, WIDE)], [VM] * 5, planes, moved=1 << 20)(
        blocks, se_got, so_got, u_now, u_prev
    )
    po_got = swap(po, "plan", 1)
    levels = [
        pltpu.VMEM((3, 20, 16, WIDE), F32),
        pltpu.VMEM((3, 18, 16, WIDE), F32),
        pltpu.VMEM((3, 18, 16, WIDE), F32),
    ]
    own = (consts, coef, se_got, so_got, u_now, u_prev)
    pe, early = call(
        functools.partial(early_kernel, plans=plans),
        [shape(rows, WIDE), shape(*cells)],
        [VM] * 6,
        planes + levels,
        flops=60_000_000,
        moved=4 << 20,
    )(*own)
    pe_got = swap(pe, "plan", 0)
    (late,) = call(
        functools.partial(late_kernel, plans=plans), [shape(*cells)], [VM] * 6, levels, flops=60_000_000, moved=4 << 20
    )(*own)
    half = shape(3, 16, 8, WIDE)
    work = [pltpu.VMEM((3, 16, 8, WIDE), F32), pltpu.VMEM((3 * PAD, WIDE), F32), pltpu.SemaphoreType.DMA((3,))]
    out, rest = call(
        functools.partial(tail_pe_kernel, plans=plans),
        [shape(*cells), half],
        [VM] * 5,
        work,
        flops=5_000_000,
        moved=2 << 20,
        places=[HB, VM],
    )(coef, pe, pe_got, early, late)
    (out,) = call(
        tail_po_kernel, [shape(*cells)], [VM] * 4 + [HB], work, flops=5_000_000, moved=2 << 20, places=[HB], aliases={4: 0}
    )(coef, po, po_got, rest, out)
    return out


def solution(mesh):
    in_specs = (
        P(None, "story", "plan", None),
        P(None, "story", "plan", None),
        P("story", "plan", None),
        P("story", "plan", None),
        P(),
        P(),
        P(),
    )
    out_specs = P(None, "story", "plan", None)
    return jax.shard_map(local, mesh=mesh, in_specs=in_specs, out_specs=out_specs, check_vma=False)
```

```python
import functools

import jax
import jax.numpy as jnp
from jax import lax
from jax.experimental import pallas as pl
from jax.experimental.pallas import tpu as pltpu
from jax.sharding import PartitionSpec as P

BLOCK = 16
WIDE = 256
PAD = 24
F32 = jnp.float32


def swap(values, axis, first):
    pairs = []
    for low in range(first, lax.axis_size(axis) - 1, 2):
        pairs += [(low, low + 1), (low + 1, low)]
    return lax.ppermute(values, axis, pairs)


def row_shift(v):
    count = v.shape[0] // 8
    row = lax.broadcasted_iota(jnp.int32, (8, v.shape[1]), 0)
    tiles = [v[8 * k : 8 * k + 8] for k in range(count)]
    down = [jnp.zeros_like(tiles[0])] + [pltpu.roll(t, 1, 0) for t in tiles]
    up = [pltpu.roll(t, 7, 0) for t in tiles] + [jnp.zeros_like(tiles[0])]
    lower = [jnp.where(row == 0, down[k], down[k + 1]) for k in range(count)]
    upper = [jnp.where(row == 7, up[k + 1], up[k]) for k in range(count)]
    return jnp.concatenate(lower, 0), jnp.concatenate(upper, 0)


def lane_shift(v):
    half = WIDE // 2
    lane = lax.broadcasted_iota(jnp.int32, (v.shape[0], half), 1)
    first, second = v[:, :half], v[:, half:]
    first_down, second_down = pltpu.roll(first, 1, 1), pltpu.roll(second, 1, 1)
    first_up, second_up = pltpu.roll(first, half - 1, 1), pltpu.roll(second, half - 1, 1)
    lower = [jnp.where(lane == 0, 0.0, first_down), jnp.where(lane == 0, first_down, second_down)]
    upper = [jnp.where(lane == half - 1, second_up, first_up), jnp.where(lane == half - 1, 0.0, second_up)]
    return jnp.concatenate(lower, 1), jnp.concatenate(upper, 1)


def lane_smooth(v):
    lower, upper = lane_shift(v)
    return lower + upper + 4.0 * v


def lane_first(v):
    lower, upper = lane_shift(v)
    return upper - lower


def total(terms):
    terms = [t for t in terms if t is not None]
    return functools.reduce(lambda p, q: p + q, terms)


def stencil(below, here, above, sign=None):
    zs, zf = [], []
    for j in range(3):
        zs.append(total([below and below[j], above and above[j], here and 4.0 * here[j]]))
        if below and above:
            zf.append(above[j] - below[j])
        else:
            zf.append(above[j] if above else -below[j])
    if sign is not None:
        zf = [sign * v for v in zf]
    zs_sh = [row_shift(v) for v in zs]
    zf_sh = [row_shift(v) for v in zf]
    s_zs = [lo + up + 4.0 * v for (lo, up), v in zip(zs_sh, zs)]
    lap = []
    if here:
        s_mid = [lo + up + 4.0 * v for (lo, up), v in zip([row_shift(v) for v in here], here)]
        inner = [s_zs[j] - 2.0 * (s_mid[j] + zs[j]) for j in range(3)]
        curl = 2.0 * s_zs[0] - 12.0 * s_mid[0]
    else:
        inner = [s_zs[j] - 2.0 * zs[j] for j in range(3)]
        curl = 2.0 * s_zs[0]
    for j in range(3):
        lap.append(lane_smooth(inner[j]) - 2.0 * s_zs[j])
    f_zf0 = zf_sh[0][1] - zf_sh[0][0]
    f_zf1 = zf_sh[1][1] - zf_sh[1][0]
    s_zf0 = zf_sh[0][0] + zf_sh[0][1] + 4.0 * zf[0]
    s_zf2 = zf_sh[2][0] + zf_sh[2][1] + 4.0 * zf[2]
    f_zs1 = zs_sh[1][1] - zs_sh[1][0]
    f_zs2 = zs_sh[2][1] - zs_sh[2][0]
    c0 = lane_smooth(curl + 3.0 * f_zf1) + lane_first(3.0 * s_zf2)
    c1 = lane_smooth(2.0 * s_zs[1] - 12.0 * zs[1] + 3.0 * f_zf0) + lane_first(3.0 * f_zs2)
    c2 = lane_first(3.0 * (s_zf0 + f_zs1)) + 2.0 * lane_smooth(s_zs[2]) - 12.0 * s_zs[2]
    return lap, [c0, c1, c2]


def coefficients(own, over, under, carried):
    z = lax.broadcasted_iota(jnp.int32, (PAD, WIDE), 0) - 4
    zf = z.astype(F32)

    def pick(k):
        return jnp.where(z < 0, under[k], jnp.where(z > 15, over[k], own[k]))

    a, b, g = pick(0), pick(1), pick(2)
    mass, mass_over, mass_under = own[3], over[3], under[3]
    upper = jnp.where(z > 15, carried - mass_over, carried + mass * (15.0 - zf))
    lower = jnp.where(z < 0, carried + 16.0 * mass + mass_under, carried + mass * (16.0 - zf))
    return a, b, g * upper, g * lower


def parity(axis):
    return lax.axis_index(axis) % 2 == 0


def slice_kernel(now, prev, occ_h, mat_h, shear_h, lame_h, dens_h, so, se, blocks, occ, mat, shear_t, lame_t, dens_t, held, sems, *, factor):
    even = parity("story")
    smalls = []
    for k, (source, target) in enumerate(((occ_h, occ), (mat_h, mat), (shear_h, shear_t), (lame_h, lame_t), (dens_h, dens_t))):
        smalls.append(pltpu.make_async_copy(source, target, sems.at[6 + k]))
    copies = []
    for k, out in enumerate((se, so)):
        top = jnp.logical_xor(even, k == 1)
        near, far = jnp.where(top, 15, 0), jnp.where(top, 14, 1)
        for j, (source, z) in enumerate(((now, near), (now, far), (prev, near))):
            copies.append(pltpu.make_async_copy(source.at[:, z], out.at[pl.ds(3 * j, 3)], sems.at[3 * k + j]))
    for copy in smalls + copies:
        copy.start()
    for copy in smalls:
        copy.wait()
    segment = lax.broadcasted_iota(jnp.int32, (8, 128), 1) // BLOCK

    def repeat(ref):
        held[...] = jnp.zeros((8, 128), F32)
        held[0:1, 0:BLOCK] = ref[...].astype(F32)
        once = held[...]
        return once + sum(pltpu.roll(once, BLOCK * k, 1) for k in range(1, 5))

    occupied, which = repeat(occ), repeat(mat)
    found = []
    for table in (shear_t, lame_t, dens_t):
        value = jnp.zeros((8, 128), F32)
        for k in range(table.shape[1]):
            value = jnp.where(which == k, table[0:1, k : k + 1], value)
        found.append(value)
    shear, lame, dens = found
    scale = occupied * (0.1 / dens)
    parts = (scale * shear * (1.0 / 12.0), scale * (lame + shear) * (1.0 / 72.0), scale * factor, dens * occupied, occupied)
    row = jnp.zeros((8, 128), F32)
    for k, part in enumerate(parts):
        row = jnp.where(segment == k, part, row)
    blocks[...] = jnp.broadcast_to(row[0:1], blocks.shape)
    for copy in copies:
        copy.wait()


def ghost_of(se, so, consts):
    even = parity("story")

    def ghost(over, plane, *where):
        take = even if over else jnp.logical_not(even)
        row = 9 if over else 14
        return jnp.where(take, se[(plane,) + where], so[(plane,) + where]) * consts[row : row + 1, :]

    return ghost


def fill(right, ghost, consts, coef, now, prev, out, far_rows, prev_rows):
    occupied = consts[4:5, :]

    def load(near, far):
        for c in range(3):
            for target, source, x in ((out, now, near), (far_rows, now, far), (prev_rows, prev, near)):
                base = c * PAD
                target[base + 4 : base + 20, :] = source[c, :, x, :] * occupied
                kinds = (6,) if source is prev else (0, 3)
                for k, kind in enumerate(kinds):
                    target[base + 3 - k : base + 4 - k, :] = ghost(False, kind + c, pl.ds(x, 1), slice(None))
                    target[base + 20 + k : base + 21 + k, :] = ghost(True, kind + c, pl.ds(x, 1), slice(None))

    @pl.when(right)
    def _():
        load(15, 14)

    @pl.when(jnp.logical_not(right))
    def _():
        load(0, 1)

    order = (1, 0, 2)

    def planes(ref):
        return [ref[c * PAD : (c + 1) * PAD, :] for c in order]

    first = advance(planes(far_rows), planes(out), None, planes(prev_rows), [coef[k] for k in range(4)], jnp.where(right, 1.0, -1.0))
    for k, c in enumerate(order):
        out[3 * PAD + 16 * c : 3 * PAD + 16 * c + 16, :] = first[k][4:20]
        out[c * PAD : c * PAD + 1, :] = first[k][3:4]
        out[c * PAD + 23 : c * PAD + 24, :] = first[k][20:21]
    for k, row in enumerate((1, 22)):
        for j in range(3):
            out[j * PAD + row : j * PAD + row + 1, :] = consts[5 * j + k : 5 * j + k + 1, :]


def pack_po_kernel(blocks, se, so, now, prev, po, coef, consts, far_rows, prev_rows):
    place = lax.axis_index("story")
    step = lax.broadcasted_iota(jnp.int32, blocks.shape, 0)
    rows = [jnp.sum(jnp.where(step == place + k, blocks[...], 0.0), 0, keepdims=True) for k in (0, 1, -1)]
    rows.append(16.0 * jnp.sum(jnp.where(step > place, blocks[...], 0.0), 0, keepdims=True))
    stacked = jnp.concatenate(rows + [jnp.zeros((4, 128), F32)], 0)
    lane = lax.broadcasted_iota(jnp.int32, (8, 128), 1) // BLOCK

    def spread(k):
        halves = [jnp.take_along_axis(stacked, lane + (BLOCK * k + 8 * h), 1, mode="promise_in_bounds") for h in (0, 1)]
        return jnp.concatenate(halves, 1)

    sets = [[], [], []]
    for k in range(5):
        wide = spread(k)
        for j in range(3):
            sets[j].append(wide[j : j + 1])
            consts[5 * j + k : 5 * j + k + 1, :] = wide[j : j + 1]
        if k == 3:
            carried = wide[3:4]
    consts[15:16, :] = carried
    for k, value in enumerate(coefficients(sets[0], sets[1], sets[2], carried)):
        coef[k] = value
    fill(jnp.logical_not(parity("plan")), ghost_of(se, so, consts), consts, coef, now, prev, po, far_rows, prev_rows)


def advance(below, here, above, before, coefs, sign):
    a, b, gu, gd = coefs
    lap, coup = stencil(below, here, above, sign)
    news = []
    for c in range(3):
        lower, upper = row_shift(here[c])
        news.append(update(here[c], before[c], lap[c], coup[c], a, b, gu, gd, lower, upper))
    return news


def update(here, before, lap, coup, a, b, gu, gd, below, above):
    geometric = gu * (above - here) - gd * (here - below)
    return 2.0 * here - before + a * lap + b * coup - geometric


def crosses(plans):
    place = lax.axis_index("plan")
    return jnp.logical_or(place == plans // 2 - 1, place == plans // 2)


def both_steps(consts, coef, se, so, now, prev, out, u0, u1, before):
    ghost = ghost_of(se, so, consts)
    occupied = jnp.broadcast_to(consts[4:5, :], (16, WIDE))
    for c in range(3):
        u0[c, 0] = ghost(False, 3 + c)
        u0[c, 1] = ghost(False, c)
        u0[c, 18] = ghost(True, c)
        u0[c, 19] = ghost(True, 3 + c)
        before[c, 0] = ghost(False, 6 + c)
        before[c, 17] = ghost(True, 6 + c)

    @pl.loop(0, 16, unroll=4)
    def _(z):
        for c in range(3):
            u0[c, z + 2] = now[c, z] * occupied
            before[c, z + 1] = prev[c, z] * occupied

    def one(source, earlier, target, i, shift):
        below, here, above = ([source[c, i + k] for c in range(3)] for k in range(3))
        lap, coup = stencil(below, here, above)
        a, b, gu, gd = (coef[k, pl.ds(i + shift, 1), :] for k in range(4))
        for c in range(3):
            target[c, i] = update(here[c], earlier(c, i), lap[c], coup[c], a, b, gu, gd, below[c], above[c])

    @pl.loop(0, 18, unroll=3)
    def _(i):
        one(u0, lambda c, i: before[c, i], u1, i, 3)

    @pl.loop(0, 16, unroll=4)
    def _(i):
        one(u1, lambda c, i: u0[c, i + 2], out, i, 4)


def early_kernel(consts, coef, se, so, now, prev, pe, out, far_rows, prev_rows, u0, u1, before, *, plans):
    fill(parity("plan"), ghost_of(se, so, consts), consts, coef, now, prev, pe, far_rows, prev_rows)

    @pl.when(jnp.logical_not(crosses(plans)))
    def _():
        both_steps(consts, coef, se, so, now, prev, out, u0, u1, before)


def late_kernel(consts, coef, se, so, now, prev, out, u0, u1, before, *, plans):
    @pl.when(crosses(plans))
    def _():
        both_steps(consts, coef, se, so, now, prev, out, u0, u1, before)


def one_side(coef, sent, got, held, sign):
    order = (1, 0, 2)

    def planes(ref):
        return [ref[c * PAD : (c + 1) * PAD, :] for c in order]

    for c in range(3):
        base = c * PAD
        held[base : base + 4, :] = got[base : base + 1, :] + jnp.zeros((4, WIDE), F32)
        held[base + 4 : base + 20, :] = got[3 * PAD + 16 * c : 3 * PAD + 16 * c + 16, :]
        held[base + 20 : base + PAD, :] = got[base + 23 : base + 24, :] + jnp.zeros((4, WIDE), F32)
    a, b, gu, gd = (coef[k] for k in range(4))
    z = lax.broadcasted_iota(jnp.int32, (PAD, WIDE), 0) - 4

    def pick(row):
        own, over, under = (got[k * PAD + row : k * PAD + row + 1, :] for k in range(3))
        return jnp.where(z < 0, under, jnp.where(z > 15, over, own))

    got_a, got_b = pick(1), pick(22)
    lap, coup = stencil(None, None, planes(got), sign)
    delta = [a * lap[k] + b * coup[k] for k in range(3)]
    lap, coup = stencil(planes(sent), None, None, sign)
    outer = [p + got_a * lap[k] + got_b * coup[k] for k, p in enumerate(planes(held))]
    zero = jnp.zeros((PAD, WIDE), F32)
    near_more = advance(None, delta, outer, [zero] * 3, (a, b, gu, gd), sign)
    lap, coup = stencil(None, None, delta, sign)
    near, far = [None] * 3, [None] * 3
    for k, c in enumerate(order):
        near[c] = near_more[k][4:20]
        far[c] = (a * lap[k] + b * coup[k])[4:20]
    return near, far


def write_half(right, near, far, work, out, sems):
    def put(near_row, far_row, first):
        copies = []
        for c in range(3):
            work[c, :, near_row, :] += near[c]
            work[c, :, far_row, :] += far[c]
            copies.append(pltpu.make_async_copy(work.at[c], out.at[c, :, pl.ds(first, 8), :], sems.at[c]))
            copies[-1].start()
        for copy in copies:
            copy.wait()

    @pl.when(right)
    def _():
        put(7, 6, 8)

    @pl.when(jnp.logical_not(right))
    def _():
        put(0, 1, 0)


def tail_pe_kernel(coef, sent, got, early, late, out, rest, work, held, sems, *, plans):
    right = parity("plan")
    for inner, use in ((late, crosses(plans)), (early, jnp.logical_not(crosses(plans)))):

        @pl.when(jnp.logical_and(use, right))
        def _(inner=inner):
            work[...] = inner[:, :, 8:16, :]
            rest[...] = inner[:, :, 0:8, :]

        @pl.when(jnp.logical_and(use, jnp.logical_not(right)))
        def _(inner=inner):
            work[...] = inner[:, :, 0:8, :]
            rest[...] = inner[:, :, 8:16, :]

    near, far = one_side(coef, sent, got, held, jnp.where(right, 1.0, -1.0))
    write_half(right, near, far, work, out, sems)


def tail_po_kernel(coef, sent, got, rest, half, out, work, held, sems):
    right = jnp.logical_not(parity("plan"))
    work[...] = rest[...]
    near, far = one_side(coef, sent, got, held, jnp.where(right, 1.0, -1.0))
    write_half(right, near, far, work, out, sems)


VM = pl.BlockSpec(memory_space=pltpu.VMEM)
HB = pl.BlockSpec(memory_space=pltpu.HBM)


def shape(*dims):
    return jax.ShapeDtypeStruct(dims, F32)


def call(kernel, outs, ins, scratch=(), flops=0, moved=0, grant=24.0, places=None, aliases=None):
    return pl.pallas_call(
        kernel,
        out_shape=outs,
        in_specs=ins,
        out_specs=places or [VM] * len(outs),
        scratch_shapes=list(scratch),
        input_output_aliases=aliases or {},
        compiler_params=pltpu.CompilerParams(vmem_limit_bytes=int(grant * 2**20)),
        cost_estimate=pl.CostEstimate(flops=flops, bytes_accessed=moved, transcendentals=0),
    )


def local(u_now, u_prev, occupancy, materials, shear_table, lame_table, density_table):
    height = u_now.shape[1] * lax.axis_size("story")
    stories, plans = lax.axis_size("story"), lax.axis_size("plan")
    face, table = shape(9, 16, WIDE), shape(4, PAD, WIDE)
    rows = 3 * PAD + 48
    planes = [pltpu.VMEM((3 * PAD, WIDE), F32)] * 2
    small = [v.reshape(1, -1) for v in (occupancy, materials, shear_table, lame_table, density_table)]
    so, se, blocks = call(
        functools.partial(slice_kernel, factor=0.8 / height),
        [shape(10, 16, WIDE), face, shape(stories, 128)],
        [HB] * 7,
        [pltpu.VMEM(v.shape, v.dtype) for v in small] + [pltpu.VMEM((8, 128), F32), pltpu.SemaphoreType.DMA((11,))],
        moved=1 << 20,
    )(*(pltpu.with_memory_space_constraint(v, pltpu.HBM) for v in [u_now, u_prev] + small))
    so_got = swap(so, "story", 1)
    se_got = swap(se, "story", 0)
    blocks = lax.all_to_all(blocks, "story", 0, 0, tiled=True)
    cells = u_now.shape
    po, coef, consts = call(pack_po_kernel, [shape(rows + 8, WIDE), table, shape(16, WIDE)], [VM] * 5, planes, moved=1 << 20)(
        blocks, se_got, so_got, u_now, u_prev
    )
    po_got = swap(po, "plan", 1)
    levels = [
        pltpu.VMEM((3, 20, 16, WIDE), F32),
        pltpu.VMEM((3, 18, 16, WIDE), F32),
        pltpu.VMEM((3, 18, 16, WIDE), F32),
    ]
    own = (consts, coef, se_got, so_got, u_now, u_prev)
    pe, early = call(
        functools.partial(early_kernel, plans=plans),
        [shape(rows, WIDE), shape(*cells)],
        [VM] * 6,
        planes + levels,
        flops=60_000_000,
        moved=4 << 20,
    )(*own)
    pe_got = swap(pe, "plan", 0)
    (late,) = call(
        functools.partial(late_kernel, plans=plans), [shape(*cells)], [VM] * 6, levels, flops=60_000_000, moved=4 << 20
    )(*own)
    half = shape(3, 16, 8, WIDE)
    work = [pltpu.VMEM((3, 16, 8, WIDE), F32), pltpu.VMEM((3 * PAD, WIDE), F32), pltpu.SemaphoreType.DMA((3,))]
    out, rest = call(
        functools.partial(tail_pe_kernel, plans=plans),
        [shape(*cells), half],
        [VM] * 5,
        work,
        flops=5_000_000,
        moved=2 << 20,
        places=[HB, VM],
    )(coef, pe, pe_got, early, late)
    (out,) = call(
        tail_po_kernel, [shape(*cells)], [VM] * 4 + [HB], work, flops=5_000_000, moved=2 << 20, places=[HB], aliases={4: 0}
    )(coef, po, po_got, rest, out)
    return out


def solution(mesh):
    in_specs = (
        P(None, "story", "plan", None),
        P(None, "story", "plan", None),
        P("story", "plan", None),
        P("story", "plan", None),
        P(),
        P(),
        P(),
    )
    out_specs = P(None, "story", "plan", None)
    return jax.shard_map(local, mesh=mesh, in_specs=in_specs, out_specs=out_specs, check_vma=False)
```

```python
import functools

import jax
import jax.numpy as jnp
from jax import lax
from jax.experimental import pallas as pl
from jax.experimental.pallas import tpu as pltpu
from jax.sharding import PartitionSpec as P

BLOCK = 16
WIDE = 256
PAD = 24
F32 = jnp.float32


def swap(values, axis, first):
    pairs = []
    for low in range(first, lax.axis_size(axis) - 1, 2):
        pairs += [(low, low + 1), (low + 1, low)]
    return lax.ppermute(values, axis, pairs)


def row_shift(v):
    count = v.shape[0] // 8
    row = lax.broadcasted_iota(jnp.int32, (8, v.shape[1]), 0)
    tiles = [v[8 * k : 8 * k + 8] for k in range(count)]
    down = [jnp.zeros_like(tiles[0])] + [pltpu.roll(t, 1, 0) for t in tiles]
    up = [pltpu.roll(t, 7, 0) for t in tiles] + [jnp.zeros_like(tiles[0])]
    lower = [jnp.where(row == 0, down[k], down[k + 1]) for k in range(count)]
    upper = [jnp.where(row == 7, up[k + 1], up[k]) for k in range(count)]
    return jnp.concatenate(lower, 0), jnp.concatenate(upper, 0)


def lane_shift(v):
    half = WIDE // 2
    lane = lax.broadcasted_iota(jnp.int32, (v.shape[0], half), 1)
    first, second = v[:, :half], v[:, half:]
    first_down, second_down = pltpu.roll(first, 1, 1), pltpu.roll(second, 1, 1)
    first_up, second_up = pltpu.roll(first, half - 1, 1), pltpu.roll(second, half - 1, 1)
    lower = [jnp.where(lane == 0, 0.0, first_down), jnp.where(lane == 0, first_down, second_down)]
    upper = [jnp.where(lane == half - 1, second_up, first_up), jnp.where(lane == half - 1, 0.0, second_up)]
    return jnp.concatenate(lower, 1), jnp.concatenate(upper, 1)


def lane_smooth(v):
    lower, upper = lane_shift(v)
    return lower + upper + 4.0 * v


def lane_first(v):
    lower, upper = lane_shift(v)
    return upper - lower


def total(terms):
    terms = [t for t in terms if t is not None]
    return functools.reduce(lambda p, q: p + q, terms)


def stencil(below, here, above, sign=None):
    zs, zf = [], []
    for j in range(3):
        zs.append(total([below and below[j], above and above[j], here and 4.0 * here[j]]))
        if below and above:
            zf.append(above[j] - below[j])
        else:
            zf.append(above[j] if above else -below[j])
    if sign is not None:
        zf = [sign * v for v in zf]
    zs_sh = [row_shift(v) for v in zs]
    zf_sh = [row_shift(v) for v in zf]
    s_zs = [lo + up + 4.0 * v for (lo, up), v in zip(zs_sh, zs)]
    lap = []
    if here:
        s_mid = [lo + up + 4.0 * v for (lo, up), v in zip([row_shift(v) for v in here], here)]
        inner = [s_zs[j] - 2.0 * (s_mid[j] + zs[j]) for j in range(3)]
        curl = 2.0 * s_zs[0] - 12.0 * s_mid[0]
    else:
        inner = [s_zs[j] - 2.0 * zs[j] for j in range(3)]
        curl = 2.0 * s_zs[0]
    for j in range(3):
        lap.append(lane_smooth(inner[j]) - 2.0 * s_zs[j])
    f_zf0 = zf_sh[0][1] - zf_sh[0][0]
    f_zf1 = zf_sh[1][1] - zf_sh[1][0]
    s_zf0 = zf_sh[0][0] + zf_sh[0][1] + 4.0 * zf[0]
    s_zf2 = zf_sh[2][0] + zf_sh[2][1] + 4.0 * zf[2]
    f_zs1 = zs_sh[1][1] - zs_sh[1][0]
    f_zs2 = zs_sh[2][1] - zs_sh[2][0]
    c0 = lane_smooth(curl + 3.0 * f_zf1) + lane_first(3.0 * s_zf2)
    c1 = lane_smooth(2.0 * s_zs[1] - 12.0 * zs[1] + 3.0 * f_zf0) + lane_first(3.0 * f_zs2)
    c2 = lane_first(3.0 * (s_zf0 + f_zs1)) + 2.0 * lane_smooth(s_zs[2]) - 12.0 * s_zs[2]
    return lap, [c0, c1, c2]


def coefficients(own, over, under, carried):
    z = lax.broadcasted_iota(jnp.int32, (PAD, WIDE), 0) - 4
    zf = z.astype(F32)

    def pick(k):
        return jnp.where(z < 0, under[k], jnp.where(z > 15, over[k], own[k]))

    a, b, g = pick(0), pick(1), pick(2)
    mass, mass_over, mass_under = own[3], over[3], under[3]
    upper = jnp.where(z > 15, carried - mass_over, carried + mass * (15.0 - zf))
    lower = jnp.where(z < 0, carried + 16.0 * mass + mass_under, carried + mass * (16.0 - zf))
    return a, b, g * upper, g * lower


def parity(axis):
    return lax.axis_index(axis) % 2 == 0


def slice_kernel(now, prev, occ_h, mat_h, shear_h, lame_h, dens_h, so, se, blocks, occ, mat, shear_t, lame_t, dens_t, held, sems, *, factor):
    even = parity("story")
    smalls = []
    for k, (source, target) in enumerate(((occ_h, occ), (mat_h, mat), (shear_h, shear_t), (lame_h, lame_t), (dens_h, dens_t))):
        smalls.append(pltpu.make_async_copy(source, target, sems.at[6 + k]))
    copies = []
    for k, out in enumerate((se, so)):
        top = jnp.logical_xor(even, k == 1)
        near, far = jnp.where(top, 15, 0), jnp.where(top, 14, 1)
        for j, (source, z) in enumerate(((now, near), (now, far), (prev, near))):
            copies.append(pltpu.make_async_copy(source.at[:, z], out.at[pl.ds(3 * j, 3)], sems.at[3 * k + j]))
    for copy in smalls + copies:
        copy.start()
    for copy in smalls:
        copy.wait()
    segment = lax.broadcasted_iota(jnp.int32, (8, 128), 1) // BLOCK

    def repeat(ref):
        held[...] = jnp.zeros((8, 128), F32)
        held[0:1, 0:BLOCK] = ref[...].astype(F32)
        once = held[...]
        return once + sum(pltpu.roll(once, BLOCK * k, 1) for k in range(1, 5))

    occupied, which = repeat(occ), repeat(mat)
    found = []
    for table in (shear_t, lame_t, dens_t):
        value = jnp.zeros((8, 128), F32)
        for k in range(table.shape[1]):
            value = jnp.where(which == k, table[0:1, k : k + 1], value)
        found.append(value)
    shear, lame, dens = found
    scale = occupied * (0.1 / dens)
    parts = (scale * shear * (1.0 / 12.0), scale * (lame + shear) * (1.0 / 72.0), scale * factor, dens * occupied, occupied)
    row = jnp.zeros((8, 128), F32)
    for k, part in enumerate(parts):
        row = jnp.where(segment == k, part, row)
    blocks[...] = jnp.broadcast_to(row[0:1], blocks.shape)
    for copy in copies:
        copy.wait()


def ghost_of(se, so, consts):
    even = parity("story")

    def ghost(over, plane, *where):
        take = even if over else jnp.logical_not(even)
        row = 9 if over else 14
        return jnp.where(take, se[(plane,) + where], so[(plane,) + where]) * consts[row : row + 1, :]

    return ghost


def fill(right, ghost, consts, coef, now, prev, out, far_rows, prev_rows):
    occupied = consts[4:5, :]

    def load(near, far):
        for c in range(3):
            for target, source, x in ((out, now, near), (far_rows, now, far), (prev_rows, prev, near)):
                base = c * PAD
                target[base + 4 : base + 20, :] = source[c, :, x, :] * occupied
                kinds = (6,) if source is prev else (0, 3)
                for k, kind in enumerate(kinds):
                    target[base + 3 - k : base + 4 - k, :] = ghost(False, kind + c, pl.ds(x, 1), slice(None))
                    target[base + 20 + k : base + 21 + k, :] = ghost(True, kind + c, pl.ds(x, 1), slice(None))

    @pl.when(right)
    def _():
        load(15, 14)

    @pl.when(jnp.logical_not(right))
    def _():
        load(0, 1)

    order = (1, 0, 2)

    def planes(ref):
        return [ref[c * PAD : (c + 1) * PAD, :] for c in order]

    first = advance(planes(far_rows), planes(out), None, planes(prev_rows), [coef[k] for k in range(4)], jnp.where(right, 1.0, -1.0))
    lane = lax.broadcasted_iota(jnp.int32, (1, WIDE), 1)
    for k, c in enumerate(order):
        count = 16 if c < 2 else 15
        out[3 * PAD + 16 * c : 3 * PAD + 16 * c + count, :] = first[k][4 : 4 + count]
        out[c * PAD : c * PAD + 1, :] = first[k][3:4]
        out[c * PAD + 23 : c * PAD + 24, :] = first[k][20:21]
    out[2 * PAD + 22 : 2 * PAD + 23, :] = first[order.index(2)][19:20]
    for k, row in enumerate((1, 22)):
        out[row : row + 1, :] = consts[k : k + 1, :]
        out[PAD + row : PAD + row + 1, :] = jnp.where(lane % 2 == 0, consts[5 + k : 6 + k, :], consts[10 + k : 11 + k, :])


def pack_po_kernel(blocks, se, so, now, prev, po, coef, consts, far_rows, prev_rows):
    place = lax.axis_index("story")
    step = lax.broadcasted_iota(jnp.int32, blocks.shape, 0)
    rows = [jnp.sum(jnp.where(step == place + k, blocks[...], 0.0), 0, keepdims=True) for k in (0, 1, -1)]
    rows.append(16.0 * jnp.sum(jnp.where(step > place, blocks[...], 0.0), 0, keepdims=True))
    stacked = jnp.concatenate(rows + [jnp.zeros((4, 128), F32)], 0)
    lane = lax.broadcasted_iota(jnp.int32, (8, 128), 1) // BLOCK

    def spread(k):
        halves = [jnp.take_along_axis(stacked, lane + (BLOCK * k + 8 * h), 1, mode="promise_in_bounds") for h in (0, 1)]
        return jnp.concatenate(halves, 1)

    sets = [[], [], []]
    for k in range(5):
        wide = spread(k)
        for j in range(3):
            sets[j].append(wide[j : j + 1])
            consts[5 * j + k : 5 * j + k + 1, :] = wide[j : j + 1]
        if k == 3:
            carried = wide[3:4]
    consts[15:16, :] = carried
    for k, value in enumerate(coefficients(sets[0], sets[1], sets[2], carried)):
        coef[k] = value
    fill(jnp.logical_not(parity("plan")), ghost_of(se, so, consts), consts, coef, now, prev, po, far_rows, prev_rows)


def advance(below, here, above, before, coefs, sign):
    a, b, gu, gd = coefs
    lap, coup = stencil(below, here, above, sign)
    news = []
    for c in range(3):
        lower, upper = row_shift(here[c])
        news.append(update(here[c], before[c], lap[c], coup[c], a, b, gu, gd, lower, upper))
    return news


def update(here, before, lap, coup, a, b, gu, gd, below, above):
    geometric = gu * (above - here) - gd * (here - below)
    return 2.0 * here - before + a * lap + b * coup - geometric


def crosses(plans):
    place = lax.axis_index("plan")
    return jnp.logical_or(place == plans // 2 - 1, place == plans // 2)


def both_steps(consts, coef, se, so, now, prev, out, u0, u1, before):
    ghost = ghost_of(se, so, consts)
    occupied = jnp.broadcast_to(consts[4:5, :], (16, WIDE))
    for c in range(3):
        u0[c, 0] = ghost(False, 3 + c)
        u0[c, 1] = ghost(False, c)
        u0[c, 18] = ghost(True, c)
        u0[c, 19] = ghost(True, 3 + c)
        before[c, 0] = ghost(False, 6 + c)
        before[c, 17] = ghost(True, 6 + c)

    @pl.loop(0, 16, unroll=4)
    def _(z):
        for c in range(3):
            u0[c, z + 2] = now[c, z] * occupied
            before[c, z + 1] = prev[c, z] * occupied

    def one(source, earlier, target, i, shift):
        below, here, above = ([source[c, i + k] for c in range(3)] for k in range(3))
        lap, coup = stencil(below, here, above)
        a, b, gu, gd = (coef[k, pl.ds(i + shift, 1), :] for k in range(4))
        for c in range(3):
            target[c, i] = update(here[c], earlier(c, i), lap[c], coup[c], a, b, gu, gd, below[c], above[c])

    @pl.loop(0, 18, unroll=3)
    def _(i):
        one(u0, lambda c, i: before[c, i], u1, i, 3)

    @pl.loop(0, 16, unroll=4)
    def _(i):
        one(u1, lambda c, i: u0[c, i + 2], out, i, 4)


def early_kernel(consts, coef, se, so, now, prev, pe, out, far_rows, prev_rows, u0, u1, before, *, plans):
    fill(parity("plan"), ghost_of(se, so, consts), consts, coef, now, prev, pe, far_rows, prev_rows)

    @pl.when(jnp.logical_not(crosses(plans)))
    def _():
        both_steps(consts, coef, se, so, now, prev, out, u0, u1, before)


def planes_of(ref):
    return [ref[c * PAD : (c + 1) * PAD, :] for c in (1, 0, 2)]


def side_sign(right):
    return jnp.where(right, 1.0, -1.0)


def late_kernel(consts, coef, se, so, now, prev, early, pe_sent, po_sent, late, out, base, pe_own, po_own, u0, u1, before, sems, *, plans):
    right = parity("plan")
    cross = crosses(plans)

    @pl.when(cross)
    def _():
        both_steps(consts, coef, se, so, now, prev, late, u0, u1, before)

    def finish(inner, near, far, first):
        copies = [
            pltpu.make_async_copy(inner.at[c, :, pl.ds(first, 8), :], out.at[c, :, pl.ds(first, 8), :], sems.at[c]) for c in range(3)
        ]
        for copy in copies:
            copy.start()
        for c in range(3):
            base[0, c] = inner[c, :, near, :]
            base[1, c] = inner[c, :, far, :]
        for sent, own, sign in ((pe_sent, pe_own, side_sign(right)), (po_sent, po_own, -side_sign(right))):
            for k, v in enumerate(sum(stencil(planes_of(sent), None, None, sign), [])):
                own[k] = v
        for copy in copies:
            copy.wait()

    for inner, use in ((late, cross), (early, jnp.logical_not(cross))):

        @pl.when(jnp.logical_and(use, right))
        def _(inner=inner):
            finish(inner, 0, 1, 0)

        @pl.when(jnp.logical_and(use, jnp.logical_not(right)))
        def _(inner=inner):
            finish(inner, 15, 14, 8)


def one_side(coef, got, held, own, sign):
    for c in range(3):
        base = c * PAD
        count = 16 if c < 2 else 15
        held[base : base + 4, :] = got[base : base + 1, :] + jnp.zeros((4, WIDE), F32)
        held[base + 4 : base + 4 + count, :] = got[3 * PAD + 16 * c : 3 * PAD + 16 * c + count, :]
        held[base + 20 : base + PAD, :] = got[base + 23 : base + 24, :] + jnp.zeros((4, WIDE), F32)
    held[2 * PAD + 19 : 2 * PAD + 20, :] = got[2 * PAD + 22 : 2 * PAD + 23, :]
    a, b, gu, gd = (coef[k] for k in range(4))
    z = lax.broadcasted_iota(jnp.int32, (PAD, WIDE), 0) - 4
    even = lax.broadcasted_iota(jnp.int32, (8, WIDE), 1) % 2 == 0

    def pick(row):
        mixed = jnp.broadcast_to(got[PAD + row : PAD + row + 1, :], (8, WIDE))
        lower, upper = lane_shift(mixed)
        over = jnp.where(even, mixed, lower)[0:1]
        under = jnp.where(even, upper, mixed)[0:1]
        return jnp.where(z < 0, under, jnp.where(z > 15, over, got[row : row + 1, :]))

    got_a, got_b = pick(1), pick(22)
    lap, coup = stencil(None, None, planes_of(got), sign)
    delta = [a * lap[k] + b * coup[k] for k in range(3)]
    outer = [p + got_a * own[k] + got_b * own[3 + k] for k, p in enumerate(planes_of(held))]
    zero = jnp.zeros((PAD, WIDE), F32)
    near_more = advance(None, delta, outer, [zero] * 3, (a, b, gu, gd), sign)
    lap, coup = stencil(None, None, delta, sign)
    near, far = [None] * 3, [None] * 3
    for k, c in enumerate((1, 0, 2)):
        near[c] = near_more[k][4:20]
        far[c] = (a * lap[k] + b * coup[k])[4:20]
    return near, far


def tail_pe_kernel(coef, got, own, early, late, half, held, *, plans):
    right = parity("plan")
    near, far = one_side(coef, got, held, own, side_sign(right))

    def finish(inner, row, next_row, first):
        for c in range(3):
            half[c] = inner[c, :, first : first + 8, :]
            half[c, :, row - first, :] += near[c]
            half[c, :, next_row - first, :] += far[c]

    for inner, use in ((late, crosses(plans)), (early, jnp.logical_not(crosses(plans)))):

        @pl.when(jnp.logical_and(use, right))
        def _(inner=inner):
            finish(inner, 15, 14, 8)

        @pl.when(jnp.logical_and(use, jnp.logical_not(right)))
        def _(inner=inner):
            finish(inner, 0, 1, 0)


def tail_po_kernel(coef, got, own, base, half, before, out, work, held, sems):
    right = jnp.logical_not(parity("plan"))
    start = pl.multiple_of(jnp.where(right, 0, 8), 8)
    copies = [pltpu.make_async_copy(half.at[c], out.at[c, :, pl.ds(start, 8), :], sems.at[c]) for c in range(3)]
    for copy in copies:
        copy.start()
    near, far = one_side(coef, got, held, own, side_sign(right))

    def finish(row, next_row, first):
        last = []
        for c in range(3):
            work[c, :, row, :] = base[0, c] + near[c]
            work[c, :, next_row, :] = base[1, c] + far[c]
            rows = pl.ds(min(row, next_row), 2)
            last.append(pltpu.make_async_copy(work.at[c, :, rows, :], out.at[c, :, pl.ds(first + min(row, next_row), 2), :], sems.at[3 + c]))
            last[-1].start()
        for copy in last:
            copy.wait()

    @pl.when(right)
    def _():
        finish(7, 6, 8)

    @pl.when(jnp.logical_not(right))
    def _():
        finish(0, 1, 0)

    for copy in copies:
        copy.wait()


VM = pl.BlockSpec(memory_space=pltpu.VMEM)
HB = pl.BlockSpec(memory_space=pltpu.HBM)


def shape(*dims):
    return jax.ShapeDtypeStruct(dims, F32)


def call(kernel, outs, ins, scratch=(), flops=0, moved=0, grant=24.0, places=None, aliases=None):
    return pl.pallas_call(
        kernel,
        out_shape=outs,
        in_specs=ins,
        out_specs=places or [VM] * len(outs),
        scratch_shapes=list(scratch),
        input_output_aliases=aliases or {},
        compiler_params=pltpu.CompilerParams(vmem_limit_bytes=int(grant * 2**20)),
        cost_estimate=pl.CostEstimate(flops=flops, bytes_accessed=moved, transcendentals=0),
    )


def local(u_now, u_prev, occupancy, materials, shear_table, lame_table, density_table):
    height = u_now.shape[1] * lax.axis_size("story")
    stories, plans = lax.axis_size("story"), lax.axis_size("plan")
    face, table = shape(9, 16, WIDE), shape(4, PAD, WIDE)
    rows = 3 * PAD + 48
    planes = [pltpu.VMEM((3 * PAD, WIDE), F32)] * 2
    small = [v.reshape(1, -1) for v in (occupancy, materials, shear_table, lame_table, density_table)]
    so, se, blocks = call(
        functools.partial(slice_kernel, factor=0.8 / height),
        [shape(10, 16, WIDE), face, shape(stories, 128)],
        [HB] * 7,
        [pltpu.VMEM(v.shape, v.dtype) for v in small] + [pltpu.VMEM((8, 128), F32), pltpu.SemaphoreType.DMA((11,))],
        moved=1 << 20,
    )(*(pltpu.with_memory_space_constraint(v, pltpu.HBM) for v in [u_now, u_prev] + small))
    so_got = swap(so, "story", 1)
    se_got = swap(se, "story", 0)
    blocks = lax.all_to_all(blocks, "story", 0, 0, tiled=True)
    cells = u_now.shape
    po, coef, consts = call(pack_po_kernel, [shape(rows, WIDE), table, shape(16, WIDE)], [VM] * 5, planes, moved=1 << 20)(
        blocks, se_got, so_got, u_now, u_prev
    )
    po_got = swap(po, "plan", 1)
    levels = [
        pltpu.VMEM((3, 20, 16, WIDE), F32),
        pltpu.VMEM((3, 18, 16, WIDE), F32),
        pltpu.VMEM((3, 18, 16, WIDE), F32),
    ]
    own = (consts, coef, se_got, so_got, u_now, u_prev)
    pe, early = call(
        functools.partial(early_kernel, plans=plans),
        [shape(rows - 1, WIDE), shape(*cells)],
        [VM] * 6,
        planes + levels,
        flops=60_000_000,
        moved=4 << 20,
    )(*own)
    pe_got = swap(pe, "plan", 0)
    side = shape(6, PAD, WIDE)
    late, out, base, pe_own, po_own = call(
        functools.partial(late_kernel, plans=plans),
        [shape(*cells), shape(*cells), shape(2, 3, 16, WIDE), side, side],
        [VM] * 9,
        levels + [pltpu.SemaphoreType.DMA((3,))],
        flops=60_000_000,
        moved=4 << 20,
        places=[VM, HB, VM, VM, VM],
    )(*own, early, pe, po)
    held = pltpu.VMEM((3 * PAD, WIDE), F32)
    (half,) = call(
        functools.partial(tail_pe_kernel, plans=plans), [shape(3, 16, 8, WIDE)], [VM] * 5, [held], flops=5_000_000, moved=2 << 20
    )(coef, pe_got, pe_own, early, late)
    (out,) = call(
        tail_po_kernel,
        [shape(*cells)],
        [VM] * 5 + [HB],
        [pltpu.VMEM((3, 16, 8, WIDE), F32), held, pltpu.SemaphoreType.DMA((6,))],
        flops=5_000_000,
        moved=2 << 20,
        places=[HB],
        aliases={5: 0},
    )(coef, po_got, po_own, base, half, out)
    return out


def solution(mesh):
    in_specs = (
        P(None, "story", "plan", None),
        P(None, "story", "plan", None),
        P("story", "plan", None),
        P("story", "plan", None),
        P(),
        P(),
        P(),
    )
    out_specs = P(None, "story", "plan", None)
    return jax.shard_map(local, mesh=mesh, in_specs=in_specs, out_specs=out_specs, check_vma=False)
```

```python
import functools

import jax
import jax.numpy as jnp
from jax import lax
from jax.experimental import pallas as pl
from jax.experimental.pallas import tpu as pltpu
from jax.sharding import PartitionSpec as P

BLOCK = 16
WIDE = 256
PAD = 24
F32 = jnp.float32


def swap(values, axis, first):
    pairs = []
    for low in range(first, lax.axis_size(axis) - 1, 2):
        pairs += [(low, low + 1), (low + 1, low)]
    return lax.ppermute(values, axis, pairs)


def row_shift(v):
    count = v.shape[0] // 8
    row = lax.broadcasted_iota(jnp.int32, (8, v.shape[1]), 0)
    tiles = [v[8 * k : 8 * k + 8] for k in range(count)]
    down = [jnp.zeros_like(tiles[0])] + [pltpu.roll(t, 1, 0) for t in tiles]
    up = [pltpu.roll(t, 7, 0) for t in tiles] + [jnp.zeros_like(tiles[0])]
    lower = [jnp.where(row == 0, down[k], down[k + 1]) for k in range(count)]
    upper = [jnp.where(row == 7, up[k + 1], up[k]) for k in range(count)]
    return jnp.concatenate(lower, 0), jnp.concatenate(upper, 0)


def lane_shift(v):
    half = WIDE // 2
    lane = lax.broadcasted_iota(jnp.int32, (v.shape[0], half), 1)
    first, second = v[:, :half], v[:, half:]
    first_down, second_down = pltpu.roll(first, 1, 1), pltpu.roll(second, 1, 1)
    first_up, second_up = pltpu.roll(first, half - 1, 1), pltpu.roll(second, half - 1, 1)
    lower = [jnp.where(lane == 0, 0.0, first_down), jnp.where(lane == 0, first_down, second_down)]
    upper = [jnp.where(lane == half - 1, second_up, first_up), jnp.where(lane == half - 1, 0.0, second_up)]
    return jnp.concatenate(lower, 1), jnp.concatenate(upper, 1)


def lane_smooth(v):
    lower, upper = lane_shift(v)
    return lower + upper + 4.0 * v


def lane_first(v):
    lower, upper = lane_shift(v)
    return upper - lower


def total(terms):
    terms = [t for t in terms if t is not None]
    return functools.reduce(lambda p, q: p + q, terms)


def stencil(below, here, above, sign=None):
    zs, zf = [], []
    for j in range(3):
        zs.append(total([below and below[j], above and above[j], here and 4.0 * here[j]]))
        if below and above:
            zf.append(above[j] - below[j])
        else:
            zf.append(above[j] if above else -below[j])
    if sign is not None:
        zf = [sign * v for v in zf]
    zs_sh = [row_shift(v) for v in zs]
    zf_sh = [row_shift(v) for v in zf]
    s_zs = [lo + up + 4.0 * v for (lo, up), v in zip(zs_sh, zs)]
    lap = []
    if here:
        s_mid = [lo + up + 4.0 * v for (lo, up), v in zip([row_shift(v) for v in here], here)]
        inner = [s_zs[j] - 2.0 * (s_mid[j] + zs[j]) for j in range(3)]
        curl = 2.0 * s_zs[0] - 12.0 * s_mid[0]
    else:
        inner = [s_zs[j] - 2.0 * zs[j] for j in range(3)]
        curl = 2.0 * s_zs[0]
    for j in range(3):
        lap.append(lane_smooth(inner[j]) - 2.0 * s_zs[j])
    f_zf0 = zf_sh[0][1] - zf_sh[0][0]
    f_zf1 = zf_sh[1][1] - zf_sh[1][0]
    s_zf0 = zf_sh[0][0] + zf_sh[0][1] + 4.0 * zf[0]
    s_zf2 = zf_sh[2][0] + zf_sh[2][1] + 4.0 * zf[2]
    f_zs1 = zs_sh[1][1] - zs_sh[1][0]
    f_zs2 = zs_sh[2][1] - zs_sh[2][0]
    c0 = lane_smooth(curl + 3.0 * f_zf1) + lane_first(3.0 * s_zf2)
    c1 = lane_smooth(2.0 * s_zs[1] - 12.0 * zs[1] + 3.0 * f_zf0) + lane_first(3.0 * f_zs2)
    c2 = lane_first(3.0 * (s_zf0 + f_zs1)) + 2.0 * lane_smooth(s_zs[2]) - 12.0 * s_zs[2]
    return lap, [c0, c1, c2]


def coefficients(own, over, under, carried):
    z = lax.broadcasted_iota(jnp.int32, (PAD, WIDE), 0) - 4
    zf = z.astype(F32)

    def pick(k):
        return jnp.where(z < 0, under[k], jnp.where(z > 15, over[k], own[k]))

    a, b, g = pick(0), pick(1), pick(2)
    mass, mass_over, mass_under = own[3], over[3], under[3]
    upper = jnp.where(z > 15, carried - mass_over, carried + mass * (15.0 - zf))
    lower = jnp.where(z < 0, carried + 16.0 * mass + mass_under, carried + mass * (16.0 - zf))
    return a, b, g * upper, g * lower


def parity(axis):
    return lax.axis_index(axis) % 2 == 0


def slice_kernel(now, prev, occ_h, mat_h, shear_h, lame_h, dens_h, so, se, blocks, occ, mat, shear_t, lame_t, dens_t, held, held_blocks, sems, *, factor):
    even = parity("story")
    smalls = []
    for k, (source, target) in enumerate(((occ_h, occ), (mat_h, mat), (shear_h, shear_t), (lame_h, lame_t), (dens_h, dens_t))):
        smalls.append(pltpu.make_async_copy(source, target, sems.at[6 + k]))
    copies = []
    for k, out in enumerate((se, so)):
        top = jnp.logical_xor(even, k == 1)
        near, far = jnp.where(top, 15, 0), jnp.where(top, 14, 1)
        for j, (source, z) in enumerate(((now, near), (now, far), (prev, near))):
            copies.append(pltpu.make_async_copy(source.at[:, z], out.at[pl.ds(3 * j, 3)], sems.at[3 * k + j]))
    for copy in smalls + copies:
        copy.start()
    for copy in smalls:
        copy.wait()
    segment = lax.broadcasted_iota(jnp.int32, (8, 128), 1) // BLOCK

    def repeat(ref):
        held[...] = jnp.zeros((8, 128), F32)
        held[0:1, 0:BLOCK] = ref[...].astype(F32)
        once = held[...]
        return once + sum(pltpu.roll(once, BLOCK * k, 1) for k in range(1, 5))

    occupied, which = repeat(occ), repeat(mat)
    found = []
    for table in (shear_t, lame_t, dens_t):
        value = jnp.zeros((8, 128), F32)
        for k in range(table.shape[1]):
            value = jnp.where(which == k, table[0:1, k : k + 1], value)
        found.append(value)
    shear, lame, dens = found
    scale = occupied * (0.1 / dens)
    parts = (scale * shear * (1.0 / 12.0), scale * (lame + shear) * (1.0 / 72.0), scale * factor, dens * occupied, occupied)
    row = jnp.zeros((8, 128), F32)
    for k, part in enumerate(parts):
        row = jnp.where(segment == k, part, row)
    held_blocks[...] = jnp.broadcast_to(row[0:1], held_blocks.shape)
    copies.append(pltpu.make_async_copy(held_blocks, blocks, sems.at[11]))
    copies[-1].start()
    for copy in copies:
        copy.wait()


def ghost_of(se, so, consts):
    even = parity("story")

    def ghost(over, plane, *where):
        take = even if over else jnp.logical_not(even)
        row = 9 if over else 14
        return jnp.where(take, se[(plane,) + where], so[(plane,) + where]) * consts[row : row + 1, :]

    return ghost


def planes_kernel(now, prev, po, pe, token):
    even = parity("plan")
    token[...] = jnp.zeros(token.shape, F32)

    def load(out, near, far):
        for k, (source, x) in enumerate(((now, near), (now, far), (prev, near))):
            for c in range(3):
                base = (3 * k + c) * 16
                out[base : base + 16, :] = source[c, :, x, :]

    @pl.when(even)
    def _():
        load(pe, 15, 14)
        load(po, 0, 1)

    @pl.when(jnp.logical_not(even))
    def _():
        load(pe, 0, 1)
        load(po, 15, 14)


def fill(right, ghost, consts, coef, layers, out, far_rows, prev_rows):
    occupied = consts[4:5, :]

    def load(near, far):
        for kind, (target, x, sides) in enumerate(((out, near, (0, 3)), (far_rows, far, (0, 3)), (prev_rows, near, (6,)))):
            for c in range(3):
                base = c * PAD
                at = (3 * kind + c) * 16
                target[base + 4 : base + 20, :] = layers[at : at + 16, :] * occupied
                for k, side in enumerate(sides):
                    target[base + 3 - k : base + 4 - k, :] = ghost(False, side + c, pl.ds(x, 1), slice(None))
                    target[base + 20 + k : base + 21 + k, :] = ghost(True, side + c, pl.ds(x, 1), slice(None))

    @pl.when(right)
    def _():
        load(15, 14)

    @pl.when(jnp.logical_not(right))
    def _():
        load(0, 1)

    order = (1, 0, 2)

    def planes(ref):
        return [ref[c * PAD : (c + 1) * PAD, :] for c in order]

    first = advance(planes(far_rows), planes(out), None, planes(prev_rows), [coef[k] for k in range(4)], jnp.where(right, 1.0, -1.0))
    lane = lax.broadcasted_iota(jnp.int32, (1, WIDE), 1)
    for k, c in enumerate(order):
        count = 16 if c < 2 else 15
        out[3 * PAD + 16 * c : 3 * PAD + 16 * c + count, :] = first[k][4 : 4 + count]
        out[c * PAD : c * PAD + 1, :] = first[k][3:4]
        out[c * PAD + 23 : c * PAD + 24, :] = first[k][20:21]
    out[2 * PAD + 22 : 2 * PAD + 23, :] = first[order.index(2)][19:20]
    for k, row in enumerate((1, 22)):
        out[row : row + 1, :] = consts[k : k + 1, :]
        out[PAD + row : PAD + row + 1, :] = jnp.where(lane % 2 == 0, consts[5 + k : 6 + k, :], consts[10 + k : 11 + k, :])


def expand_kernel(blocks, token, coef, consts):
    place = lax.axis_index("story")
    step = lax.broadcasted_iota(jnp.int32, blocks.shape, 0)
    rows = [jnp.sum(jnp.where(step == place + k, blocks[...], 0.0), 0, keepdims=True) for k in (0, 1, -1)]
    rows.append(16.0 * jnp.sum(jnp.where(step > place, blocks[...], 0.0), 0, keepdims=True))
    stacked = jnp.concatenate(rows + [jnp.zeros((4, 128), F32)], 0)
    lane = lax.broadcasted_iota(jnp.int32, (8, 128), 1) // BLOCK

    def spread(k):
        halves = [jnp.take_along_axis(stacked, lane + (BLOCK * k + 8 * h), 1, mode="promise_in_bounds") for h in (0, 1)]
        return jnp.concatenate(halves, 1)

    sets = [[], [], []]
    for k in range(5):
        wide = spread(k)
        for j in range(3):
            sets[j].append(wide[j : j + 1])
            consts[5 * j + k : 5 * j + k + 1, :] = wide[j : j + 1]
        if k == 3:
            carried = wide[3:4]
    consts[15:16, :] = carried
    for k, value in enumerate(coefficients(sets[0], sets[1], sets[2], carried)):
        coef[k] = value


def pack_po_kernel(consts, coef, se, so, layers, po, far_rows, prev_rows):
    fill(jnp.logical_not(parity("plan")), ghost_of(se, so, consts), consts, coef, layers, po, far_rows, prev_rows)


def advance(below, here, above, before, coefs, sign):
    a, b, gu, gd = coefs
    lap, coup = stencil(below, here, above, sign)
    news = []
    for c in range(3):
        lower, upper = row_shift(here[c])
        news.append(update(here[c], before[c], lap[c], coup[c], a, b, gu, gd, lower, upper))
    return news


def update(here, before, lap, coup, a, b, gu, gd, below, above):
    geometric = gu * (above - here) - gd * (here - below)
    return 2.0 * here - before + a * lap + b * coup - geometric


def runs_late(plans):
    place = lax.axis_index("plan")
    return jnp.logical_not(jnp.logical_or(place == plans // 2 - 2, place == plans // 2 + 1))


def both_steps(consts, coef, se, so, now, prev, out, u0, u1, before):
    ghost = ghost_of(se, so, consts)
    occupied = jnp.broadcast_to(consts[4:5, :], (16, WIDE))
    for c in range(3):
        u0[c, 0] = ghost(False, 3 + c)
        u0[c, 1] = ghost(False, c)
        u0[c, 18] = ghost(True, c)
        u0[c, 19] = ghost(True, 3 + c)
        before[c, 0] = ghost(False, 6 + c)
        before[c, 17] = ghost(True, 6 + c)

    @pl.loop(0, 16, unroll=4)
    def _(z):
        for c in range(3):
            u0[c, z + 2] = now[c, z] * occupied
            before[c, z + 1] = prev[c, z] * occupied

    def one(source, earlier, target, i, shift):
        below, here, above = ([source[c, i + k] for c in range(3)] for k in range(3))
        lap, coup = stencil(below, here, above)
        a, b, gu, gd = (coef[k, pl.ds(i + shift, 1), :] for k in range(4))
        for c in range(3):
            target[c, i] = update(here[c], earlier(c, i), lap[c], coup[c], a, b, gu, gd, below[c], above[c])

    @pl.loop(0, 18, unroll=6)
    def _(i):
        one(u0, lambda c, i: before[c, i], u1, i, 3)

    @pl.loop(0, 16, unroll=8)
    def _(i):
        one(u1, lambda c, i: u0[c, i + 2], out, i, 4)


def early_kernel(consts, coef, se, so, now, prev, layers, pe, out, far_rows, prev_rows, u0, u1, before, *, plans):
    fill(parity("plan"), ghost_of(se, so, consts), consts, coef, layers, pe, far_rows, prev_rows)

    @pl.when(jnp.logical_not(runs_late(plans)))
    def _():
        both_steps(consts, coef, se, so, now, prev, out, u0, u1, before)


def planes_of(ref):
    return [ref[c * PAD : (c + 1) * PAD, :] for c in (1, 0, 2)]


def side_sign(right):
    return jnp.where(right, 1.0, -1.0)


def late_kernel(consts, coef, se, so, now, prev, early, pe_sent, po_sent, late, base, pe_own, po_own, u0, u1, before, *, plans):
    right = parity("plan")
    cross = runs_late(plans)

    @pl.when(cross)
    def _():
        both_steps(consts, coef, se, so, now, prev, late, u0, u1, before)

    for sent, own, sign in ((pe_sent, pe_own, side_sign(right)), (po_sent, po_own, -side_sign(right))):
        for k, v in enumerate(sum(stencil(planes_of(sent), None, None, sign), [])):
            own[k] = v

    def finish(inner, near, far):
        for c in range(3):
            base[0, c] = inner[c, :, near, :]
            base[1, c] = inner[c, :, far, :]

    for inner, use in ((late, cross), (early, jnp.logical_not(cross))):

        @pl.when(jnp.logical_and(use, right))
        def _(inner=inner):
            finish(inner, 0, 1)

        @pl.when(jnp.logical_and(use, jnp.logical_not(right)))
        def _(inner=inner):
            finish(inner, 15, 14)


def rows_of(v):
    lower, upper = row_shift(v)
    return lower + upper + 4.0 * v, upper - lower


def outer_terms(layer, sign):
    (v0, s0, f0), (v1, s1, f1), (v2, s2, f2) = layer
    lap = [lane_smooth(s - 2.0 * v) - 2.0 * s for v, s, _ in layer]
    c0 = lane_smooth(2.0 * s0 + (3.0 * sign) * f1) + lane_first((3.0 * sign) * s2)
    c1 = lane_smooth(2.0 * s1 - 12.0 * v1 + (3.0 * sign) * f0) + lane_first(3.0 * f2)
    c2 = lane_first(3.0 * (sign * s0 + f1)) + 2.0 * lane_smooth(s2) - 12.0 * s2
    return lap, [c0, c1, c2]


def both_terms(here, outer, sign):
    zs = [o[0] + 4.0 * h[0] for h, o in zip(here, outer)]
    s_zs = [o[1] + 4.0 * h[1] for h, o in zip(here, outer)]
    f_zs = [o[2] + 4.0 * h[2] for h, o in zip(here, outer)]
    lap = [lane_smooth(s_zs[j] - 2.0 * (here[j][1] + zs[j])) - 2.0 * s_zs[j] for j in range(3)]
    c0 = lane_smooth(2.0 * s_zs[0] - 12.0 * here[0][1] + (3.0 * sign) * outer[1][2]) + lane_first((3.0 * sign) * outer[2][1])
    c1 = lane_smooth(2.0 * s_zs[1] - 12.0 * zs[1] + (3.0 * sign) * outer[0][2]) + lane_first(3.0 * f_zs[2])
    c2 = lane_first(3.0 * (sign * outer[0][1] + f_zs[1])) + 2.0 * lane_smooth(s_zs[2]) - 12.0 * s_zs[2]
    return lap, [c0, c1, c2]


def one_side(coef, got, held, own, sign):
    for c in range(3):
        base = c * PAD
        count = 16 if c < 2 else 15
        held[base : base + 4, :] = got[base : base + 1, :] + jnp.zeros((4, WIDE), F32)
        held[base + 4 : base + 4 + count, :] = got[3 * PAD + 16 * c : 3 * PAD + 16 * c + count, :]
        held[base + 20 : base + PAD, :] = got[base + 23 : base + 24, :] + jnp.zeros((4, WIDE), F32)
    held[2 * PAD + 19 : 2 * PAD + 20, :] = got[2 * PAD + 22 : 2 * PAD + 23, :]
    a, b, gu, gd = (coef[k] for k in range(4))
    z = lax.broadcasted_iota(jnp.int32, (PAD, WIDE), 0) - 4
    even = lax.broadcasted_iota(jnp.int32, (8, WIDE), 1) % 2 == 0

    def pick(row):
        mixed = jnp.broadcast_to(got[PAD + row : PAD + row + 1, :], (8, WIDE))
        lower, upper = lane_shift(mixed)
        over = jnp.where(even, mixed, lower)[0:1]
        under = jnp.where(even, upper, mixed)[0:1]
        return jnp.where(z < 0, under, jnp.where(z > 15, over, got[row : row + 1, :]))

    got_a, got_b = pick(1), pick(22)
    lap, coup = outer_terms([(v,) + rows_of(v) for v in planes_of(got)], sign)
    delta = [a * lap[k] + b * coup[k] for k in range(3)]
    outer = [p + got_a * own[k] + got_b * own[3 + k] for k, p in enumerate(planes_of(held))]
    delta_rows = [(v,) + rows_of(v) for v in delta]
    outer_rows = [(v,) + rows_of(v) for v in outer]
    far_lap, far_coup = outer_terms(delta_rows, sign)
    near_lap, near_coup = both_terms(delta_rows, outer_rows, sign)
    near, far = [None] * 3, [None] * 3
    for k, c in enumerate((1, 0, 2)):
        lower, upper = row_shift(delta[k])
        geometric = gu * (upper - delta[k]) - gd * (delta[k] - lower)
        near[c] = (2.0 * delta[k] + a * near_lap[k] + b * near_coup[k] - geometric)[4:20]
        far[c] = (a * far_lap[k] + b * far_coup[k])[4:20]
    return near, far


def tail_pe_kernel(coef, got, own, early, late, out, half, held, sems, *, plans):
    right = parity("plan")
    cross = runs_late(plans)
    start = pl.multiple_of(jnp.where(right, 0, 8), 8)

    def copies(inner):
        return [pltpu.make_async_copy(inner.at[c, :, pl.ds(start, 8), :], out.at[c, :, pl.ds(start, 8), :], sems.at[c]) for c in range(3)]

    def begin(inner):
        for copy in copies(inner):
            copy.start()

    def finish(inner, row, next_row, first):
        for c in range(3):
            half[c] = inner[c, :, first : first + 8, :]
            half[c, :, row - first, :] += near[c]
            half[c, :, next_row - first, :] += far[c]
        for copy in copies(inner):
            copy.wait()

    places = ((late, cross), (early, jnp.logical_not(cross)))
    for inner, use in places:

        @pl.when(use)
        def _(inner=inner):
            begin(inner)

    near, far = one_side(coef, got, held, own, side_sign(right))
    for inner, use in places:

        @pl.when(jnp.logical_and(use, right))
        def _(inner=inner):
            finish(inner, 15, 14, 8)

        @pl.when(jnp.logical_and(use, jnp.logical_not(right)))
        def _(inner=inner):
            finish(inner, 0, 1, 0)


def tail_po_kernel(coef, got, own, base, half, before, out, work, held, sems):
    right = jnp.logical_not(parity("plan"))
    start = pl.multiple_of(jnp.where(right, 0, 8), 8)
    copies = [pltpu.make_async_copy(half.at[c], out.at[c, :, pl.ds(start, 8), :], sems.at[c]) for c in range(3)]
    for copy in copies:
        copy.start()
    near, far = one_side(coef, got, held, own, side_sign(right))

    def finish(row, next_row, first):
        last = []
        for c in range(3):
            work[c, :, row, :] = base[0, c] + near[c]
            work[c, :, next_row, :] = base[1, c] + far[c]
            rows = pl.ds(min(row, next_row), 2)
            last.append(pltpu.make_async_copy(work.at[c, :, rows, :], out.at[c, :, pl.ds(first + min(row, next_row), 2), :], sems.at[3 + c]))
            last[-1].start()
        for copy in last:
            copy.wait()

    @pl.when(right)
    def _():
        finish(7, 6, 8)

    @pl.when(jnp.logical_not(right))
    def _():
        finish(0, 1, 0)

    for copy in copies:
        copy.wait()


VM = pl.BlockSpec(memory_space=pltpu.VMEM)
HB = pl.BlockSpec(memory_space=pltpu.HBM)


def shape(*dims):
    return jax.ShapeDtypeStruct(dims, F32)


def call(kernel, outs, ins, scratch=(), flops=0, moved=0, grant=24.0, places=None, aliases=None):
    return pl.pallas_call(
        kernel,
        out_shape=outs,
        in_specs=ins,
        out_specs=places or [VM] * len(outs),
        scratch_shapes=list(scratch),
        input_output_aliases=aliases or {},
        compiler_params=pltpu.CompilerParams(vmem_limit_bytes=int(grant * 2**20)),
        cost_estimate=pl.CostEstimate(flops=flops, bytes_accessed=moved, transcendentals=0),
    )


def local(u_now, u_prev, occupancy, materials, shear_table, lame_table, density_table):
    height = u_now.shape[1] * lax.axis_size("story")
    stories, plans = lax.axis_size("story"), lax.axis_size("plan")
    face, table = shape(9, 16, WIDE), shape(4, PAD, WIDE)
    rows = 3 * PAD + 48
    planes = [pltpu.VMEM((3 * PAD, WIDE), F32)] * 2
    small = [v.reshape(1, -1) for v in (occupancy, materials, shear_table, lame_table, density_table)]
    so, se, blocks = call(
        functools.partial(slice_kernel, factor=0.8 / height),
        [face, shape(10, 16, WIDE), shape(stories, 128)],
        [HB] * 7,
        [pltpu.VMEM(v.shape, v.dtype) for v in small] + [pltpu.VMEM((8, 128), F32), pltpu.VMEM((stories, 128), F32), pltpu.SemaphoreType.DMA((12,))],
        moved=1 << 20,
        places=[VM, VM, HB],
    )(*(pltpu.with_memory_space_constraint(v, pltpu.HBM) for v in [u_now, u_prev] + small))
    so_got = swap(so, "story", 1)
    se_got = swap(se, "story", 0)
    blocks = lax.all_to_all(blocks, "story", 0, 0, tiled=True)
    cells = u_now.shape
    layers = shape(9 * 16, WIDE)
    po_layers, pe_layers, token = call(planes_kernel, [layers, layers, shape(8, 128)], [VM] * 2, flops=1_000_000_000, moved=16 << 20)(u_now, u_prev)
    coef, consts = call(expand_kernel, [table, shape(16, WIDE)], [VM] * 2, flops=20_000_000_000, moved=1 << 30)(blocks, token)
    (po,) = call(pack_po_kernel, [shape(rows, WIDE)], [VM] * 5, planes, moved=1 << 20)(consts, coef, se_got, so_got, po_layers)
    po_got = swap(po, "plan", 1)
    levels = [
        pltpu.VMEM((3, 20, 16, WIDE), F32),
        pltpu.VMEM((3, 18, 16, WIDE), F32),
        pltpu.VMEM((3, 18, 16, WIDE), F32),
    ]
    own = (consts, coef, se_got, so_got, u_now, u_prev)
    pe, early = call(
        functools.partial(early_kernel, plans=plans),
        [shape(rows - 1, WIDE), shape(*cells)],
        [VM] * 7,
        planes + levels,
        flops=60_000_000,
        moved=4 << 20,
    )(*own, pe_layers)
    pe_got = swap(pe, "plan", 0)
    side = shape(6, PAD, WIDE)
    late, base, pe_own, po_own = call(
        functools.partial(late_kernel, plans=plans),
        [shape(*cells), shape(2, 3, 16, WIDE), side, side],
        [VM] * 9,
        levels,
        flops=60_000_000,
        moved=4 << 20,
    )(*own, early, pe, po)
    held = pltpu.VMEM((3 * PAD, WIDE), F32)
    out, half = call(
        functools.partial(tail_pe_kernel, plans=plans),
        [shape(*cells), shape(3, 16, 8, WIDE)],
        [VM] * 5,
        [held, pltpu.SemaphoreType.DMA((3,))],
        flops=5_000_000,
        moved=2 << 20,
        places=[HB, VM],
    )(coef, pe_got, pe_own, early, late)
    (out,) = call(
        tail_po_kernel,
        [shape(*cells)],
        [VM] * 5 + [HB],
        [pltpu.VMEM((3, 16, 8, WIDE), F32), held, pltpu.SemaphoreType.DMA((6,))],
        flops=5_000_000,
        moved=2 << 20,
        places=[HB],
        aliases={5: 0},
    )(coef, po_got, po_own, base, half, out)
    return out


def solution(mesh):
    in_specs = (
        P(None, "story", "plan", None),
        P(None, "story", "plan", None),
        P("story", "plan", None),
        P("story", "plan", None),
        P(),
        P(),
        P(),
    )
    out_specs = P(None, "story", "plan", None)
    return jax.shard_map(local, mesh=mesh, in_specs=in_specs, out_specs=out_specs, check_vma=False)
```

```python
import functools

import jax
import jax.numpy as jnp
from jax import lax
from jax.experimental import pallas as pl
from jax.experimental.pallas import tpu as pltpu
from jax.sharding import PartitionSpec as P

BLOCK = 16
WIDE = 256
PAD = 24
F32 = jnp.float32


def swap(values, axis, first):
    pairs = []
    for low in range(first, lax.axis_size(axis) - 1, 2):
        pairs += [(low, low + 1), (low + 1, low)]
    return lax.ppermute(values, axis, pairs)


def row_shift(v):
    count = v.shape[0] // 8
    row = lax.broadcasted_iota(jnp.int32, (8, v.shape[1]), 0)
    tiles = [v[8 * k : 8 * k + 8] for k in range(count)]
    down = [jnp.zeros_like(tiles[0])] + [pltpu.roll(t, 1, 0) for t in tiles]
    up = [pltpu.roll(t, 7, 0) for t in tiles] + [jnp.zeros_like(tiles[0])]
    lower = [jnp.where(row == 0, down[k], down[k + 1]) for k in range(count)]
    upper = [jnp.where(row == 7, up[k + 1], up[k]) for k in range(count)]
    return jnp.concatenate(lower, 0), jnp.concatenate(upper, 0)


def lane_shift(v):
    half = WIDE // 2
    lane = lax.broadcasted_iota(jnp.int32, (v.shape[0], half), 1)
    first, second = v[:, :half], v[:, half:]
    first_down, second_down = pltpu.roll(first, 1, 1), pltpu.roll(second, 1, 1)
    first_up, second_up = pltpu.roll(first, half - 1, 1), pltpu.roll(second, half - 1, 1)
    lower = [jnp.where(lane == 0, 0.0, first_down), jnp.where(lane == 0, first_down, second_down)]
    upper = [jnp.where(lane == half - 1, second_up, first_up), jnp.where(lane == half - 1, 0.0, second_up)]
    return jnp.concatenate(lower, 1), jnp.concatenate(upper, 1)


def lane_smooth(v):
    lower, upper = lane_shift(v)
    return lower + upper + 4.0 * v


def lane_first(v):
    lower, upper = lane_shift(v)
    return upper - lower


def total(terms):
    terms = [t for t in terms if t is not None]
    return functools.reduce(lambda p, q: p + q, terms)


def stencil(below, here, above, sign=None):
    zs, zf = [], []
    for j in range(3):
        zs.append(total([below and below[j], above and above[j], here and 4.0 * here[j]]))
        if below and above:
            zf.append(above[j] - below[j])
        else:
            zf.append(above[j] if above else -below[j])
    if sign is not None:
        zf = [sign * v for v in zf]
    zs_sh = [row_shift(v) for v in zs]
    zf_sh = [row_shift(v) for v in zf]
    s_zs = [lo + up + 4.0 * v for (lo, up), v in zip(zs_sh, zs)]
    lap = []
    if here:
        s_mid = [lo + up + 4.0 * v for (lo, up), v in zip([row_shift(v) for v in here], here)]
        inner = [s_zs[j] - 2.0 * (s_mid[j] + zs[j]) for j in range(3)]
        curl = 2.0 * s_zs[0] - 12.0 * s_mid[0]
    else:
        inner = [s_zs[j] - 2.0 * zs[j] for j in range(3)]
        curl = 2.0 * s_zs[0]
    for j in range(3):
        lap.append(lane_smooth(inner[j]) - 2.0 * s_zs[j])
    f_zf0 = zf_sh[0][1] - zf_sh[0][0]
    f_zf1 = zf_sh[1][1] - zf_sh[1][0]
    s_zf0 = zf_sh[0][0] + zf_sh[0][1] + 4.0 * zf[0]
    s_zf2 = zf_sh[2][0] + zf_sh[2][1] + 4.0 * zf[2]
    f_zs1 = zs_sh[1][1] - zs_sh[1][0]
    f_zs2 = zs_sh[2][1] - zs_sh[2][0]
    c0 = lane_smooth(curl + 3.0 * f_zf1) + lane_first(3.0 * s_zf2)
    c1 = lane_smooth(2.0 * s_zs[1] - 12.0 * zs[1] + 3.0 * f_zf0) + lane_first(3.0 * f_zs2)
    c2 = lane_first(3.0 * (s_zf0 + f_zs1)) + 2.0 * lane_smooth(s_zs[2]) - 12.0 * s_zs[2]
    return lap, [c0, c1, c2]


def coefficients(own, over, under, carried):
    z = lax.broadcasted_iota(jnp.int32, (PAD, WIDE), 0) - 4
    zf = z.astype(F32)

    def pick(k):
        return jnp.where(z < 0, under[k], jnp.where(z > 15, over[k], own[k]))

    a, b, g = pick(0), pick(1), pick(2)
    mass, mass_over, mass_under = own[3], over[3], under[3]
    upper = jnp.where(z > 15, carried - mass_over, carried + mass * (15.0 - zf))
    lower = jnp.where(z < 0, carried + 16.0 * mass + mass_under, carried + mass * (16.0 - zf))
    return a, b, g * upper, g * lower


def parity(axis):
    return lax.axis_index(axis) % 2 == 0


def slice_kernel(now, prev, occ_h, mat_h, shear_h, lame_h, dens_h, small, se, so, blocks, occ, mat, shear_t, lame_t, dens_t, held, held_blocks, sems, *, factor):
    even = parity("story")
    smalls = []
    for k, (source, target) in enumerate(((occ_h, occ), (mat_h, mat), (shear_h, shear_t), (lame_h, lame_t), (dens_h, dens_t))):
        smalls.append(pltpu.make_async_copy(source, target, sems.at[6 + k]))
    copies = []
    for k, out in enumerate((se, so)):
        top = jnp.logical_xor(even, k == 1)
        near, far = jnp.where(top, 15, 0), jnp.where(top, 14, 1)
        for j, (source, z) in enumerate(((now, near), (now, far), (prev, near))):
            copies.append(pltpu.make_async_copy(source.at[:, z], out.at[pl.ds(3 * j, 3)], sems.at[3 * k + j]))
            if k == 1:
                for h, x in enumerate((0, 14)):
                    rows = small.at[pl.ds(3 * j, 3), pl.ds(2 * h, 2), :]
                    copies.append(pltpu.make_async_copy(source.at[:, z, pl.ds(x, 2), :], rows, sems.at[12 + 2 * j + h]))
    for copy in smalls + copies:
        copy.start()
    for copy in smalls:
        copy.wait()
    segment = lax.broadcasted_iota(jnp.int32, (8, 128), 1) // BLOCK

    def repeat(ref):
        held[...] = jnp.zeros((8, 128), F32)
        held[0:1, 0:BLOCK] = ref[...].astype(F32)
        once = held[...]
        return once + sum(pltpu.roll(once, BLOCK * k, 1) for k in range(1, 5))

    occupied, which = repeat(occ), repeat(mat)
    found = []
    for table in (shear_t, lame_t, dens_t):
        value = jnp.zeros((8, 128), F32)
        for k in range(table.shape[1]):
            value = jnp.where(which == k, table[0:1, k : k + 1], value)
        found.append(value)
    shear, lame, dens = found
    scale = occupied * (0.1 / dens)
    parts = (scale * shear * (1.0 / 12.0), scale * (lame + shear) * (1.0 / 72.0), scale * factor, dens * occupied, occupied)
    row = jnp.zeros((8, 128), F32)
    for k, part in enumerate(parts):
        row = jnp.where(segment == k, part, row)
    held_blocks[...] = jnp.broadcast_to(row[0:1], held_blocks.shape)
    copies.append(pltpu.make_async_copy(held_blocks, blocks, sems.at[11]))
    copies[-1].start()
    for copy in copies:
        copy.wait()


def ghost_of(se, so, consts):
    even = parity("story")

    def ghost(over, plane, *where):
        take = even if over else jnp.logical_not(even)
        row = 9 if over else 14
        return jnp.where(take, se[(plane,) + where], so[(plane,) + where]) * consts[row : row + 1, :]

    return ghost


def edge_of(se, small, consts):
    even = parity("story")

    def edge(over, plane, x):
        take = even if over else jnp.logical_not(even)
        row = 9 if over else 14
        at = x % 12
        return jnp.where(take, se[plane, x : x + 1, :], small[plane, at : at + 1, :]) * consts[row : row + 1, :]

    return edge


def planes_kernel(now, prev, po, pe, token):
    even = parity("plan")
    token[...] = jnp.zeros(token.shape, F32)

    def load(out, near, far):
        for k, (source, x) in enumerate(((now, near), (now, far), (prev, near))):
            for c in range(3):
                base = (3 * k + c) * 16
                out[base : base + 16, :] = source[c, :, x, :]

    @pl.when(even)
    def _():
        load(pe, 15, 14)
        load(po, 0, 1)

    @pl.when(jnp.logical_not(even))
    def _():
        load(pe, 0, 1)
        load(po, 15, 14)


def fill(right, edge, consts, coef, layers, out, far_rows, prev_rows):
    occupied = consts[4:5, :]

    def load(near, far):
        for kind, (target, x, sides) in enumerate(((out, near, (0, 3)), (far_rows, far, (0, 3)), (prev_rows, near, (6,)))):
            for c in range(3):
                base = c * PAD
                at = (3 * kind + c) * 16
                target[base + 4 : base + 20, :] = layers[at : at + 16, :] * occupied
                for k, side in enumerate(sides):
                    target[base + 3 - k : base + 4 - k, :] = edge(False, side + c, x)
                    target[base + 20 + k : base + 21 + k, :] = edge(True, side + c, x)

    @pl.when(right)
    def _():
        load(15, 14)

    @pl.when(jnp.logical_not(right))
    def _():
        load(0, 1)

    order = (1, 0, 2)

    def planes(ref):
        return [ref[c * PAD : (c + 1) * PAD, :] for c in order]

    first = advance(planes(far_rows), planes(out), None, planes(prev_rows), [coef[k] for k in range(4)], jnp.where(right, 1.0, -1.0))
    lane = lax.broadcasted_iota(jnp.int32, (1, WIDE), 1)
    for k, c in enumerate(order):
        count = 16 if c < 2 else 15
        out[3 * PAD + 16 * c : 3 * PAD + 16 * c + count, :] = first[k][4 : 4 + count]
        out[c * PAD : c * PAD + 1, :] = first[k][3:4]
        out[c * PAD + 23 : c * PAD + 24, :] = first[k][20:21]
    out[2 * PAD + 22 : 2 * PAD + 23, :] = first[order.index(2)][19:20]
    for k, row in enumerate((1, 22)):
        out[row : row + 1, :] = consts[k : k + 1, :]
        out[PAD + row : PAD + row + 1, :] = jnp.where(lane % 2 == 0, consts[5 + k : 6 + k, :], consts[10 + k : 11 + k, :])


def expand_kernel(blocks, token, coef, consts):
    place = lax.axis_index("story")
    step = lax.broadcasted_iota(jnp.int32, blocks.shape, 0)
    rows = [jnp.sum(jnp.where(step == place + k, blocks[...], 0.0), 0, keepdims=True) for k in (0, 1, -1)]
    rows.append(16.0 * jnp.sum(jnp.where(step > place, blocks[...], 0.0), 0, keepdims=True))
    stacked = jnp.concatenate(rows + [jnp.zeros((4, 128), F32)], 0)
    lane = lax.broadcasted_iota(jnp.int32, (8, 128), 1) // BLOCK

    def spread(k):
        halves = [jnp.take_along_axis(stacked, lane + (BLOCK * k + 8 * h), 1, mode="promise_in_bounds") for h in (0, 1)]
        return jnp.concatenate(halves, 1)

    sets = [[], [], []]
    for k in range(5):
        wide = spread(k)
        for j in range(3):
            sets[j].append(wide[j : j + 1])
            consts[5 * j + k : 5 * j + k + 1, :] = wide[j : j + 1]
        if k == 3:
            carried = wide[3:4]
    consts[15:16, :] = carried
    for k, value in enumerate(coefficients(sets[0], sets[1], sets[2], carried)):
        coef[k] = value


def pack_po_kernel(consts, coef, se, small, layers, po, far_rows, prev_rows):
    fill(jnp.logical_not(parity("plan")), edge_of(se, small, consts), consts, coef, layers, po, far_rows, prev_rows)


def advance(below, here, above, before, coefs, sign):
    a, b, gu, gd = coefs
    lap, coup = stencil(below, here, above, sign)
    news = []
    for c in range(3):
        lower, upper = row_shift(here[c])
        news.append(update(here[c], before[c], lap[c], coup[c], a, b, gu, gd, lower, upper))
    return news


def update(here, before, lap, coup, a, b, gu, gd, below, above):
    geometric = gu * (above - here) - gd * (here - below)
    return 2.0 * here - before + a * lap + b * coup - geometric


def both_steps(consts, coef, se, so, now, prev, out, u0, u1, before):
    ghost = ghost_of(se, so, consts)
    occupied = jnp.broadcast_to(consts[4:5, :], (16, WIDE))
    for c in range(3):
        u0[c, 0] = ghost(False, 3 + c)
        u0[c, 1] = ghost(False, c)
        u0[c, 18] = ghost(True, c)
        u0[c, 19] = ghost(True, 3 + c)
        before[c, 0] = ghost(False, 6 + c)
        before[c, 17] = ghost(True, 6 + c)

    @pl.loop(0, 16, unroll=4)
    def _(z):
        for c in range(3):
            u0[c, z + 2] = now[c, z] * occupied
            before[c, z + 1] = prev[c, z] * occupied

    def one(source, earlier, target, i, shift):
        below, here, above = ([source[c, i + k] for c in range(3)] for k in range(3))
        lap, coup = stencil(below, here, above)
        a, b, gu, gd = (coef[k, pl.ds(i + shift, 1), :] for k in range(4))
        for c in range(3):
            target[c, i] = update(here[c], earlier(c, i), lap[c], coup[c], a, b, gu, gd, below[c], above[c])

    @pl.loop(0, 18, unroll=6)
    def _(i):
        one(u0, lambda c, i: before[c, i], u1, i, 3)

    @pl.loop(0, 16, unroll=8)
    def _(i):
        one(u1, lambda c, i: u0[c, i + 2], out, i, 4)


def pack_pe_kernel(consts, coef, se, small, layers, pe, far_rows, prev_rows):
    fill(parity("plan"), edge_of(se, small, consts), consts, coef, layers, pe, far_rows, prev_rows)


def planes_of(ref):
    return [ref[c * PAD : (c + 1) * PAD, :] for c in (1, 0, 2)]


def side_sign(right):
    return jnp.where(right, 1.0, -1.0)


def main_kernel(consts, coef, se, so, now, prev, pe_sent, po_sent, inner, base, pe_own, po_own, u0, u1, before):
    right = parity("plan")
    both_steps(consts, coef, se, so, now, prev, inner, u0, u1, before)
    for sent, own, sign in ((pe_sent, pe_own, side_sign(right)), (po_sent, po_own, -side_sign(right))):
        for k, v in enumerate(sum(stencil(planes_of(sent), None, None, sign), [])):
            own[k] = v

    def finish(near, far):
        for c in range(3):
            base[0, c] = inner[c, :, near, :]
            base[1, c] = inner[c, :, far, :]

    @pl.when(right)
    def _():
        finish(0, 1)

    @pl.when(jnp.logical_not(right))
    def _():
        finish(15, 14)


def rows_of(v):
    lower, upper = row_shift(v)
    return lower + upper + 4.0 * v, upper - lower


def outer_terms(layer, sign):
    (v0, s0, f0), (v1, s1, f1), (v2, s2, f2) = layer
    lap = [lane_smooth(s - 2.0 * v) - 2.0 * s for v, s, _ in layer]
    c0 = lane_smooth(2.0 * s0 + (3.0 * sign) * f1) + lane_first((3.0 * sign) * s2)
    c1 = lane_smooth(2.0 * s1 - 12.0 * v1 + (3.0 * sign) * f0) + lane_first(3.0 * f2)
    c2 = lane_first(3.0 * (sign * s0 + f1)) + 2.0 * lane_smooth(s2) - 12.0 * s2
    return lap, [c0, c1, c2]


def both_terms(here, outer, sign):
    zs = [o[0] + 4.0 * h[0] for h, o in zip(here, outer)]
    s_zs = [o[1] + 4.0 * h[1] for h, o in zip(here, outer)]
    f_zs = [o[2] + 4.0 * h[2] for h, o in zip(here, outer)]
    lap = [lane_smooth(s_zs[j] - 2.0 * (here[j][1] + zs[j])) - 2.0 * s_zs[j] for j in range(3)]
    c0 = lane_smooth(2.0 * s_zs[0] - 12.0 * here[0][1] + (3.0 * sign) * outer[1][2]) + lane_first((3.0 * sign) * outer[2][1])
    c1 = lane_smooth(2.0 * s_zs[1] - 12.0 * zs[1] + (3.0 * sign) * outer[0][2]) + lane_first(3.0 * f_zs[2])
    c2 = lane_first(3.0 * (sign * outer[0][1] + f_zs[1])) + 2.0 * lane_smooth(s_zs[2]) - 12.0 * s_zs[2]
    return lap, [c0, c1, c2]


def one_side(coef, got, held, own, sign):
    for c in range(3):
        base = c * PAD
        count = 16 if c < 2 else 15
        held[base : base + 4, :] = got[base : base + 1, :] + jnp.zeros((4, WIDE), F32)
        held[base + 4 : base + 4 + count, :] = got[3 * PAD + 16 * c : 3 * PAD + 16 * c + count, :]
        held[base + 20 : base + PAD, :] = got[base + 23 : base + 24, :] + jnp.zeros((4, WIDE), F32)
    held[2 * PAD + 19 : 2 * PAD + 20, :] = got[2 * PAD + 22 : 2 * PAD + 23, :]
    a, b, gu, gd = (coef[k] for k in range(4))
    z = lax.broadcasted_iota(jnp.int32, (PAD, WIDE), 0) - 4
    even = lax.broadcasted_iota(jnp.int32, (8, WIDE), 1) % 2 == 0

    def pick(row):
        mixed = jnp.broadcast_to(got[PAD + row : PAD + row + 1, :], (8, WIDE))
        lower, upper = lane_shift(mixed)
        over = jnp.where(even, mixed, lower)[0:1]
        under = jnp.where(even, upper, mixed)[0:1]
        return jnp.where(z < 0, under, jnp.where(z > 15, over, got[row : row + 1, :]))

    got_a, got_b = pick(1), pick(22)
    lap, coup = outer_terms([(v,) + rows_of(v) for v in planes_of(got)], sign)
    delta = [a * lap[k] + b * coup[k] for k in range(3)]
    outer = [p + got_a * own[k] + got_b * own[3 + k] for k, p in enumerate(planes_of(held))]
    delta_rows = [(v,) + rows_of(v) for v in delta]
    outer_rows = [(v,) + rows_of(v) for v in outer]
    far_lap, far_coup = outer_terms(delta_rows, sign)
    near_lap, near_coup = both_terms(delta_rows, outer_rows, sign)
    near, far = [None] * 3, [None] * 3
    for k, c in enumerate((1, 0, 2)):
        lower, upper = row_shift(delta[k])
        geometric = gu * (upper - delta[k]) - gd * (delta[k] - lower)
        near[c] = (2.0 * delta[k] + a * near_lap[k] + b * near_coup[k] - geometric)[4:20]
        far[c] = (a * far_lap[k] + b * far_coup[k])[4:20]
    return near, far


def tail_pe_kernel(coef, got, own, inner, out, half, held, sems):
    right = parity("plan")
    start = pl.multiple_of(jnp.where(right, 0, 8), 8)
    copies = [pltpu.make_async_copy(inner.at[c, :, pl.ds(start, 8), :], out.at[c, :, pl.ds(start, 8), :], sems.at[c]) for c in range(3)]
    for copy in copies:
        copy.start()
    near, far = one_side(coef, got, held, own, side_sign(right))

    def finish(row, next_row, first):
        for c in range(3):
            half[c] = inner[c, :, first : first + 8, :]
            half[c, :, row - first, :] += near[c]
            half[c, :, next_row - first, :] += far[c]

    @pl.when(right)
    def _():
        finish(15, 14, 8)

    @pl.when(jnp.logical_not(right))
    def _():
        finish(0, 1, 0)

    for copy in copies:
        copy.wait()


def tail_po_kernel(coef, got, own, base, half, before, out, work, held, sems):
    right = jnp.logical_not(parity("plan"))
    start = pl.multiple_of(jnp.where(right, 0, 8), 8)
    copies = [pltpu.make_async_copy(half.at[c], out.at[c, :, pl.ds(start, 8), :], sems.at[c]) for c in range(3)]
    for copy in copies:
        copy.start()
    near, far = one_side(coef, got, held, own, side_sign(right))

    def finish(row, next_row, first):
        last = []
        for c in range(3):
            work[c, :, row, :] = base[0, c] + near[c]
            work[c, :, next_row, :] = base[1, c] + far[c]
            rows = pl.ds(min(row, next_row), 2)
            last.append(pltpu.make_async_copy(work.at[c, :, rows, :], out.at[c, :, pl.ds(first + min(row, next_row), 2), :], sems.at[3 + c]))
            last[-1].start()
        for copy in last:
            copy.wait()

    @pl.when(right)
    def _():
        finish(7, 6, 8)

    @pl.when(jnp.logical_not(right))
    def _():
        finish(0, 1, 0)

    for copy in copies:
        copy.wait()


VM = pl.BlockSpec(memory_space=pltpu.VMEM)
HB = pl.BlockSpec(memory_space=pltpu.HBM)


def shape(*dims):
    return jax.ShapeDtypeStruct(dims, F32)


def call(kernel, outs, ins, scratch=(), flops=0, moved=0, grant=24.0, places=None, aliases=None):
    return pl.pallas_call(
        kernel,
        out_shape=outs,
        in_specs=ins,
        out_specs=places or [VM] * len(outs),
        scratch_shapes=list(scratch),
        input_output_aliases=aliases or {},
        compiler_params=pltpu.CompilerParams(vmem_limit_bytes=int(grant * 2**20)),
        cost_estimate=pl.CostEstimate(flops=flops, bytes_accessed=moved, transcendentals=0),
    )


def local(u_now, u_prev, occupancy, materials, shear_table, lame_table, density_table):
    height = u_now.shape[1] * lax.axis_size("story")
    stories = lax.axis_size("story")
    face, table = shape(9, 16, WIDE), shape(4, PAD, WIDE)
    rows = 3 * PAD + 48
    planes = [pltpu.VMEM((3 * PAD, WIDE), F32)] * 2
    small = [v.reshape(1, -1) for v in (occupancy, materials, shear_table, lame_table, density_table)]
    small_so, se, so, blocks = call(
        functools.partial(slice_kernel, factor=0.8 / height),
        [shape(9, 4, WIDE), face, shape(10, 16, WIDE), shape(stories, 128)],
        [HB] * 7,
        [pltpu.VMEM(v.shape, v.dtype) for v in small] + [pltpu.VMEM((8, 128), F32), pltpu.VMEM((stories, 128), F32), pltpu.SemaphoreType.DMA((18,))],
        moved=1 << 20,
        places=[VM, VM, VM, HB],
    )(*(pltpu.with_memory_space_constraint(v, pltpu.HBM) for v in [u_now, u_prev] + small))
    small_got = swap(small_so, "story", 1)
    so_got = swap(so, "story", 1)
    se_got = swap(se, "story", 0)
    blocks = lax.all_to_all(blocks, "story", 0, 0, tiled=True)
    cells = u_now.shape
    layers = shape(9 * 16, WIDE)
    po_layers, pe_layers, token = call(planes_kernel, [layers, layers, shape(8, 128)], [VM] * 2, flops=1_000_000_000, moved=16 << 20)(u_now, u_prev)
    coef, consts = call(expand_kernel, [table, shape(16, WIDE)], [VM] * 2, flops=20_000_000_000, moved=1 << 30)(blocks, token)
    (po,) = call(pack_po_kernel, [shape(rows, WIDE)], [VM] * 5, planes, moved=1 << 20)(consts, coef, se_got, small_got, po_layers)
    po_got = swap(po, "plan", 1)
    levels = [
        pltpu.VMEM((3, 20, 16, WIDE), F32),
        pltpu.VMEM((3, 18, 16, WIDE), F32),
        pltpu.VMEM((3, 18, 16, WIDE), F32),
    ]
    (pe,) = call(pack_pe_kernel, [shape(rows - 1, WIDE)], [VM] * 5, planes, moved=1 << 20)(consts, coef, se_got, small_got, pe_layers)
    pe_got = swap(pe, "plan", 0)
    side = shape(6, PAD, WIDE)
    inner, base, pe_own, po_own = call(
        main_kernel, [shape(*cells), shape(2, 3, 16, WIDE), side, side], [VM] * 8, levels, flops=60_000_000, moved=4 << 20
    )(consts, coef, se_got, so_got, u_now, u_prev, pe, po)
    held = pltpu.VMEM((3 * PAD, WIDE), F32)
    out, half = call(
        tail_pe_kernel,
        [shape(*cells), shape(3, 16, 8, WIDE)],
        [VM] * 4,
        [held, pltpu.SemaphoreType.DMA((3,))],
        flops=5_000_000,
        moved=2 << 20,
        places=[HB, VM],
    )(coef, pe_got, pe_own, inner)
    (out,) = call(
        tail_po_kernel,
        [shape(*cells)],
        [VM] * 5 + [HB],
        [pltpu.VMEM((3, 16, 8, WIDE), F32), held, pltpu.SemaphoreType.DMA((6,))],
        flops=5_000_000,
        moved=2 << 20,
        places=[HB],
        aliases={5: 0},
    )(coef, po_got, po_own, base, half, out)
    return out


def solution(mesh):
    in_specs = (
        P(None, "story", "plan", None),
        P(None, "story", "plan", None),
        P("story", "plan", None),
        P("story", "plan", None),
        P(),
        P(),
        P(),
    )
    out_specs = P(None, "story", "plan", None)
    return jax.shard_map(local, mesh=mesh, in_specs=in_specs, out_specs=out_specs, check_vma=False)
```

```python
import functools

import jax
import jax.numpy as jnp
from jax import lax
from jax.experimental import pallas as pl
from jax.experimental.pallas import tpu as pltpu
from jax.sharding import PartitionSpec as P

BLOCK = 16
WIDE = 256
PAD = 24
F32 = jnp.float32


def swap(values, axis, first):
    pairs = []
    for low in range(first, lax.axis_size(axis) - 1, 2):
        pairs += [(low, low + 1), (low + 1, low)]
    return lax.ppermute(values, axis, pairs)


def row_shift(v):
    count = v.shape[0] // 8
    row = lax.broadcasted_iota(jnp.int32, (8, v.shape[1]), 0)
    tiles = [v[8 * k : 8 * k + 8] for k in range(count)]
    down, up = [pltpu.roll(t, 1, 0) for t in tiles], [pltpu.roll(t, 7, 0) for t in tiles]
    zero = jnp.zeros_like(tiles[0])
    around = v.shape[0] == PAD
    down, up = [down[-1] if around else zero] + down, up + [up[0] if around else zero]
    lower = [jnp.where(row == 0, down[k], down[k + 1]) for k in range(count)]
    upper = [jnp.where(row == 7, up[k + 1], up[k]) for k in range(count)]
    return jnp.concatenate(lower, 0), jnp.concatenate(upper, 0)


def lane_shift(v):
    half = WIDE // 2
    lane = lax.broadcasted_iota(jnp.int32, (v.shape[0], half), 1)
    first, second = v[:, :half], v[:, half:]
    first_down, second_down = pltpu.roll(first, 1, 1), pltpu.roll(second, 1, 1)
    first_up, second_up = pltpu.roll(first, half - 1, 1), pltpu.roll(second, half - 1, 1)
    lower = [jnp.where(lane == 0, 0.0, first_down), jnp.where(lane == 0, first_down, second_down)]
    upper = [jnp.where(lane == half - 1, second_up, first_up), jnp.where(lane == half - 1, 0.0, second_up)]
    return jnp.concatenate(lower, 1), jnp.concatenate(upper, 1)


def lane_smooth(v):
    lower, upper = lane_shift(v)
    return lower + upper + 4.0 * v


def lane_first(v):
    lower, upper = lane_shift(v)
    return upper - lower


def total(terms):
    terms = [t for t in terms if t is not None]
    return functools.reduce(lambda p, q: p + q, terms)


def stencil(below, here, above, sign=None):
    zs, zf = [], []
    for j in range(3):
        zs.append(total([below and below[j], above and above[j], here and 4.0 * here[j]]))
        if below and above:
            zf.append(above[j] - below[j])
        else:
            zf.append(above[j] if above else -below[j])
    if sign is not None:
        zf = [sign * v for v in zf]
    zs_sh = [row_shift(v) for v in zs]
    zf_sh = [row_shift(v) for v in zf]
    s_zs = [lo + up + 4.0 * v for (lo, up), v in zip(zs_sh, zs)]
    lap = []
    if here:
        s_mid = [lo + up + 4.0 * v for (lo, up), v in zip([row_shift(v) for v in here], here)]
        inner = [s_zs[j] - 2.0 * (s_mid[j] + zs[j]) for j in range(3)]
        curl = 2.0 * s_zs[0] - 12.0 * s_mid[0]
    else:
        inner = [s_zs[j] - 2.0 * zs[j] for j in range(3)]
        curl = 2.0 * s_zs[0]
    for j in range(3):
        lap.append(lane_smooth(inner[j]) - 2.0 * s_zs[j])
    f_zf0 = zf_sh[0][1] - zf_sh[0][0]
    f_zf1 = zf_sh[1][1] - zf_sh[1][0]
    s_zf0 = zf_sh[0][0] + zf_sh[0][1] + 4.0 * zf[0]
    s_zf2 = zf_sh[2][0] + zf_sh[2][1] + 4.0 * zf[2]
    f_zs1 = zs_sh[1][1] - zs_sh[1][0]
    f_zs2 = zs_sh[2][1] - zs_sh[2][0]
    c0 = lane_smooth(curl + 3.0 * f_zf1) + lane_first(3.0 * s_zf2)
    c1 = lane_smooth(2.0 * s_zs[1] - 12.0 * zs[1] + 3.0 * f_zf0) + lane_first(3.0 * f_zs2)
    c2 = lane_first(3.0 * (s_zf0 + f_zs1)) + 2.0 * lane_smooth(s_zs[2]) - 12.0 * s_zs[2]
    return lap, [c0, c1, c2]


def heights():
    row = lax.broadcasted_iota(jnp.int32, (PAD, WIDE), 0)
    return jnp.where(row > 20, row - PAD, row)


def coefficients(own, over, under, carried):
    z = heights()
    zf = z.astype(F32)

    def pick(k):
        return jnp.where(z < 0, under[k], jnp.where(z > 15, over[k], own[k]))

    a, b, g = pick(0), pick(1), pick(2)
    mass, mass_over, mass_under = own[3], over[3], under[3]
    upper = jnp.where(z > 15, carried - mass_over, carried + mass * (15.0 - zf))
    lower = jnp.where(z < 0, carried + 16.0 * mass + mass_under, carried + mass * (16.0 - zf))
    return a, b, g * upper, g * lower


def parity(axis):
    return lax.axis_index(axis) % 2 == 0


def slice_kernel(now, prev, occ_h, mat_h, shear_h, lame_h, dens_h, small, se, so, blocks, occ, mat, shear_t, lame_t, dens_t, held, held_blocks, sems, *, factor):
    even = parity("story")
    smalls = []
    for k, (source, target) in enumerate(((occ_h, occ), (mat_h, mat), (shear_h, shear_t), (lame_h, lame_t), (dens_h, dens_t))):
        smalls.append(pltpu.make_async_copy(source, target, sems.at[6 + k]))
    copies = []
    for k, out in enumerate((se, so)):
        top = jnp.logical_xor(even, k == 1)
        near, far = jnp.where(top, 15, 0), jnp.where(top, 14, 1)
        for j, (source, z) in enumerate(((now, near), (now, far), (prev, near))):
            copies.append(pltpu.make_async_copy(source.at[:, z], out.at[pl.ds(3 * j, 3)], sems.at[3 * k + j]))
            if k == 1:
                for h, x in enumerate((0, 14)):
                    rows = small.at[pl.ds(3 * j, 3), pl.ds(2 * h, 2), :]
                    copies.append(pltpu.make_async_copy(source.at[:, z, pl.ds(x, 2), :], rows, sems.at[12 + 2 * j + h]))
    for copy in smalls + copies:
        copy.start()
    for copy in smalls:
        copy.wait()
    segment = lax.broadcasted_iota(jnp.int32, (8, 128), 1) // BLOCK

    def repeat(ref):
        held[...] = jnp.zeros((8, 128), F32)
        held[0:1, 0:BLOCK] = ref[...].astype(F32)
        once = held[...]
        return once + sum(pltpu.roll(once, BLOCK * k, 1) for k in range(1, 5))

    occupied, which = repeat(occ), repeat(mat)
    found = []
    for table in (shear_t, lame_t, dens_t):
        value = jnp.zeros((8, 128), F32)
        for k in range(table.shape[1]):
            value = jnp.where(which == k, table[0:1, k : k + 1], value)
        found.append(value)
    shear, lame, dens = found
    scale = occupied * (0.1 / dens)
    parts = (scale * shear * (1.0 / 12.0), scale * (lame + shear) * (1.0 / 72.0), scale * factor, dens * occupied, occupied)
    row = jnp.zeros((8, 128), F32)
    for k, part in enumerate(parts):
        row = jnp.where(segment == k, part, row)
    held_blocks[...] = jnp.broadcast_to(row[0:1], held_blocks.shape)
    copies.append(pltpu.make_async_copy(held_blocks, blocks, sems.at[11]))
    copies[-1].start()
    for copy in copies:
        copy.wait()


def ghost_of(se, so, consts):
    even = parity("story")

    def ghost(over, plane, *where):
        take = even if over else jnp.logical_not(even)
        row = 9 if over else 14
        return jnp.where(take, se[(plane,) + where], so[(plane,) + where]) * consts[row : row + 1, :]

    return ghost


def edge_of(se, small, consts):
    even = parity("story")

    def edge(over, plane, x):
        take = even if over else jnp.logical_not(even)
        row = 9 if over else 14
        at = x % 12
        return jnp.where(take, se[plane, x : x + 1, :], small[plane, at : at + 1, :]) * consts[row : row + 1, :]

    return edge


def planes_kernel(now, prev, po, pe, token):
    even = parity("plan")
    token[...] = jnp.zeros(token.shape, F32)

    def load(out, near, far):
        for k, (source, x) in enumerate(((now, near), (now, far), (prev, near))):
            for c in range(3):
                base = (3 * k + c) * 16
                out[base : base + 16, :] = source[c, :, x, :]

    @pl.when(even)
    def _():
        load(pe, 15, 14)
        load(po, 0, 1)

    @pl.when(jnp.logical_not(even))
    def _():
        load(pe, 0, 1)
        load(po, 15, 14)


def fill(right, edge, consts, coef, layers, out, far_rows, prev_rows):
    occupied = consts[4:5, :]

    def load(near, far):
        for kind, (target, x, sides) in enumerate(((out, near, (0, 3)), (far_rows, far, (0, 3)), (prev_rows, near, (6,)))):
            for c in range(3):
                base = c * PAD
                at = (3 * kind + c) * 16
                target[base : base + 16, :] = layers[at : at + 16, :] * occupied
                for k, side in enumerate(sides):
                    target[base + 23 - k : base + 24 - k, :] = edge(False, side + c, x)
                    target[base + 16 + k : base + 17 + k, :] = edge(True, side + c, x)

    @pl.when(right)
    def _():
        load(15, 14)

    @pl.when(jnp.logical_not(right))
    def _():
        load(0, 1)

    order = (1, 0, 2)

    def planes(ref):
        return [ref[c * PAD : (c + 1) * PAD, :] for c in order]

    first = advance(planes(far_rows), planes(out), None, planes(prev_rows), [coef[k] for k in range(4)], jnp.where(right, 1.0, -1.0))
    lane = lax.broadcasted_iota(jnp.int32, (1, WIDE), 1)
    for k, c in enumerate(order):
        count = 16 if c < 2 else 15
        out[3 * PAD + 16 * c : 3 * PAD + 16 * c + count, :] = first[k][0:count]
        out[c * PAD + 18 : c * PAD + 19, :] = first[k][23:24]
        out[c * PAD + 19 : c * PAD + 20, :] = first[k][16:17]
    out[2 * PAD + 21 : 2 * PAD + 22, :] = first[order.index(2)][15:16]
    for k, row in enumerate((20, 21)):
        out[row : row + 1, :] = consts[k : k + 1, :]
        out[PAD + row : PAD + row + 1, :] = jnp.where(lane % 2 == 0, consts[5 + k : 6 + k, :], consts[10 + k : 11 + k, :])


def expand_kernel(blocks, token, coef, consts):
    place = lax.axis_index("story")
    step = lax.broadcasted_iota(jnp.int32, blocks.shape, 0)
    rows = [jnp.sum(jnp.where(step == place + k, blocks[...], 0.0), 0, keepdims=True) for k in (0, 1, -1)]
    rows.append(16.0 * jnp.sum(jnp.where(step > place, blocks[...], 0.0), 0, keepdims=True))
    stacked = jnp.concatenate(rows + [jnp.zeros((4, 128), F32)], 0)
    lane = lax.broadcasted_iota(jnp.int32, (8, 128), 1) // BLOCK

    def spread(k):
        halves = [jnp.take_along_axis(stacked, lane + (BLOCK * k + 8 * h), 1, mode="promise_in_bounds") for h in (0, 1)]
        return jnp.concatenate(halves, 1)

    sets = [[], [], []]
    for k in range(5):
        wide = spread(k)
        for j in range(3):
            sets[j].append(wide[j : j + 1])
            consts[5 * j + k : 5 * j + k + 1, :] = wide[j : j + 1]
        if k == 3:
            carried = wide[3:4]
    consts[15:16, :] = carried
    for k, value in enumerate(coefficients(sets[0], sets[1], sets[2], carried)):
        coef[k] = value


def pack_po_kernel(consts, coef, se, small, layers, po, far_rows, prev_rows):
    fill(jnp.logical_not(parity("plan")), edge_of(se, small, consts), consts, coef, layers, po, far_rows, prev_rows)


def advance(below, here, above, before, coefs, sign):
    a, b, gu, gd = coefs
    lap, coup = stencil(below, here, above, sign)
    news = []
    for c in range(3):
        lower, upper = row_shift(here[c])
        news.append(update(here[c], before[c], lap[c], coup[c], a, b, gu, gd, lower, upper))
    return news


def update(here, before, lap, coup, a, b, gu, gd, below, above):
    geometric = gu * (above - here) - gd * (here - below)
    return 2.0 * here - before + a * lap + b * coup - geometric


def both_steps(consts, coef, se, so, now, prev, out, u0, u1, before):
    ghost = ghost_of(se, so, consts)
    occupied = jnp.broadcast_to(consts[4:5, :], (16, WIDE))
    for c in range(3):
        u0[c, 0] = ghost(False, 3 + c)
        u0[c, 1] = ghost(False, c)
        u0[c, 18] = ghost(True, c)
        u0[c, 19] = ghost(True, 3 + c)
        before[c, 0] = ghost(False, 6 + c)
        before[c, 17] = ghost(True, 6 + c)

    @pl.loop(0, 16, unroll=4)
    def _(z):
        for c in range(3):
            u0[c, z + 2] = now[c, z] * occupied
            before[c, z + 1] = prev[c, z] * occupied

    def one(source, earlier, target, i, z):
        below, here, above = ([source[c, i + k] for c in range(3)] for k in range(3))
        lap, coup = stencil(below, here, above)
        a, b, gu, gd = (coef[k, pl.ds(z, 1), :] for k in range(4))
        for c in range(3):
            target[c, i] = update(here[c], earlier(c, i), lap[c], coup[c], a, b, gu, gd, below[c], above[c])

    @pl.loop(0, 18, unroll=6)
    def _(i):
        one(u0, lambda c, i: before[c, i], u1, i, jnp.where(i == 0, PAD - 1, i - 1))

    @pl.loop(0, 16, unroll=8)
    def _(i):
        one(u1, lambda c, i: u0[c, i + 2], out, i, i)


def pack_pe_kernel(consts, coef, se, small, layers, pe, far_rows, prev_rows):
    fill(parity("plan"), edge_of(se, small, consts), consts, coef, layers, pe, far_rows, prev_rows)


def planes_of(ref):
    return [ref[c * PAD : (c + 1) * PAD, :] for c in (1, 0, 2)]


def side_sign(right):
    return jnp.where(right, 1.0, -1.0)


def main_kernel(consts, coef, se, so, now, prev, pe_sent, po_sent, inner, base, pe_own, po_own, u0, u1, before):
    right = parity("plan")
    both_steps(consts, coef, se, so, now, prev, inner, u0, u1, before)
    for sent, own, sign in ((pe_sent, pe_own, side_sign(right)), (po_sent, po_own, -side_sign(right))):
        for k, v in enumerate(sum(stencil(planes_of(sent), None, None, sign), [])):
            own[k] = v

    def finish(near, far):
        for c in range(3):
            base[0, c] = inner[c, :, near, :]
            base[1, c] = inner[c, :, far, :]

    @pl.when(right)
    def _():
        finish(0, 1)

    @pl.when(jnp.logical_not(right))
    def _():
        finish(15, 14)


def rows_of(v):
    lower, upper = row_shift(v)
    return lower + upper + 4.0 * v, upper - lower


def outer_terms(layer, sign):
    (v0, s0, f0), (v1, s1, f1), (v2, s2, f2) = layer
    lap = [lane_smooth(s - 2.0 * v) - 2.0 * s for v, s, _ in layer]
    c0 = lane_smooth(2.0 * s0 + (3.0 * sign) * f1) + lane_first((3.0 * sign) * s2)
    c1 = lane_smooth(2.0 * s1 - 12.0 * v1 + (3.0 * sign) * f0) + lane_first(3.0 * f2)
    c2 = lane_first(3.0 * (sign * s0 + f1)) + 2.0 * lane_smooth(s2) - 12.0 * s2
    return lap, [c0, c1, c2]


def both_terms(here, outer, sign):
    zs = [o[0] + 4.0 * h[0] for h, o in zip(here, outer)]
    s_zs = [o[1] + 4.0 * h[1] for h, o in zip(here, outer)]
    f_zs = [o[2] + 4.0 * h[2] for h, o in zip(here, outer)]
    lap = [lane_smooth(s_zs[j] - 2.0 * (here[j][1] + zs[j])) - 2.0 * s_zs[j] for j in range(3)]
    c0 = lane_smooth(2.0 * s_zs[0] - 12.0 * here[0][1] + (3.0 * sign) * outer[1][2]) + lane_first((3.0 * sign) * outer[2][1])
    c1 = lane_smooth(2.0 * s_zs[1] - 12.0 * zs[1] + (3.0 * sign) * outer[0][2]) + lane_first(3.0 * f_zs[2])
    c2 = lane_first(3.0 * (sign * outer[0][1] + f_zs[1])) + 2.0 * lane_smooth(s_zs[2]) - 12.0 * s_zs[2]
    return lap, [c0, c1, c2]


def one_side(coef, got, held, own, sign):
    for c in range(3):
        base = c * PAD
        count = 16 if c < 2 else 15
        held[base : base + count, :] = got[3 * PAD + 16 * c : 3 * PAD + 16 * c + count, :]
        held[base + 16 : base + 17, :] = got[base + 19 : base + 20, :]
        held[base + 23 : base + 24, :] = got[base + 18 : base + 19, :]
    held[2 * PAD + 15 : 2 * PAD + 16, :] = got[2 * PAD + 21 : 2 * PAD + 22, :]
    a, b, gu, gd = (coef[k] for k in range(4))
    z = heights()
    even = lax.broadcasted_iota(jnp.int32, (8, WIDE), 1) % 2 == 0

    def pick(row):
        mixed = jnp.broadcast_to(got[PAD + row : PAD + row + 1, :], (8, WIDE))
        lower, upper = lane_shift(mixed)
        over = jnp.where(even, mixed, lower)[0:1]
        under = jnp.where(even, upper, mixed)[0:1]
        return jnp.where(z < 0, under, jnp.where(z > 15, over, got[row : row + 1, :]))

    got_a, got_b = pick(20), pick(21)
    lap, coup = outer_terms([(v,) + rows_of(v) for v in planes_of(got)], sign)
    delta = [a * lap[k] + b * coup[k] for k in range(3)]
    outer = [p + got_a * own[k] + got_b * own[3 + k] for k, p in enumerate(planes_of(held))]
    delta_rows = [tuple(p[0:16] for p in (v,) + rows_of(v)) for v in delta]
    outer_rows = [tuple(p[0:16] for p in (v,) + rows_of(v)) for v in outer]
    far_lap, far_coup = outer_terms(delta_rows, sign)
    near_lap, near_coup = both_terms(delta_rows, outer_rows, sign)
    a, b, gu, gd = (coef[k, 0:16] for k in range(4))
    near, far = [None] * 3, [None] * 3
    for k, c in enumerate((1, 0, 2)):
        lower, upper = (v[0:16] for v in row_shift(delta[k]))
        here = delta[k][0:16]
        geometric = gu * (upper - here) - gd * (here - lower)
        near[c] = 2.0 * here + a * near_lap[k] + b * near_coup[k] - geometric
        far[c] = a * far_lap[k] + b * far_coup[k]
    return near, far


def tail_pe_kernel(coef, got, own, inner, out, half, held, sems):
    right = parity("plan")
    start = pl.multiple_of(jnp.where(right, 0, 8), 8)
    copies = [pltpu.make_async_copy(inner.at[c, :, pl.ds(start, 8), :], out.at[c, :, pl.ds(start, 8), :], sems.at[c]) for c in range(3)]
    for copy in copies:
        copy.start()
    near, far = one_side(coef, got, held, own, side_sign(right))

    def finish(row, next_row, first):
        for c in range(3):
            half[c] = inner[c, :, first : first + 8, :]
            half[c, :, row - first, :] += near[c]
            half[c, :, next_row - first, :] += far[c]

    @pl.when(right)
    def _():
        finish(15, 14, 8)

    @pl.when(jnp.logical_not(right))
    def _():
        finish(0, 1, 0)

    for copy in copies:
        copy.wait()


def tail_po_kernel(coef, got, own, base, half, before, out, work, held, sems):
    right = jnp.logical_not(parity("plan"))
    start = pl.multiple_of(jnp.where(right, 0, 8), 8)
    copies = [pltpu.make_async_copy(half.at[c], out.at[c, :, pl.ds(start, 8), :], sems.at[c]) for c in range(3)]
    for copy in copies:
        copy.start()
    near, far = one_side(coef, got, held, own, side_sign(right))

    def finish(row, next_row, first):
        last = []
        for c in range(3):
            work[c, :, row, :] = base[0, c] + near[c]
            work[c, :, next_row, :] = base[1, c] + far[c]
            rows = pl.ds(min(row, next_row), 2)
            last.append(pltpu.make_async_copy(work.at[c, :, rows, :], out.at[c, :, pl.ds(first + min(row, next_row), 2), :], sems.at[3 + c]))
            last[-1].start()
        for copy in last:
            copy.wait()

    @pl.when(right)
    def _():
        finish(7, 6, 8)

    @pl.when(jnp.logical_not(right))
    def _():
        finish(0, 1, 0)

    for copy in copies:
        copy.wait()


VM = pl.BlockSpec(memory_space=pltpu.VMEM)
HB = pl.BlockSpec(memory_space=pltpu.HBM)


def shape(*dims):
    return jax.ShapeDtypeStruct(dims, F32)


def call(kernel, outs, ins, scratch=(), flops=0, moved=0, grant=24.0, places=None, aliases=None):
    return pl.pallas_call(
        kernel,
        out_shape=outs,
        in_specs=ins,
        out_specs=places or [VM] * len(outs),
        scratch_shapes=list(scratch),
        input_output_aliases=aliases or {},
        compiler_params=pltpu.CompilerParams(vmem_limit_bytes=int(grant * 2**20)),
        cost_estimate=pl.CostEstimate(flops=flops, bytes_accessed=moved, transcendentals=0),
    )


def local(u_now, u_prev, occupancy, materials, shear_table, lame_table, density_table):
    height = u_now.shape[1] * lax.axis_size("story")
    stories = lax.axis_size("story")
    face, table = shape(9, 16, WIDE), shape(4, PAD, WIDE)
    rows = 3 * PAD + 48
    planes = [pltpu.VMEM((3 * PAD, WIDE), F32)] * 2
    small = [v.reshape(1, -1) for v in (occupancy, materials, shear_table, lame_table, density_table)]
    small_so, se, so, blocks = call(
        functools.partial(slice_kernel, factor=0.8 / height),
        [shape(9, 4, WIDE), face, shape(10, 16, WIDE), shape(stories, 128)],
        [HB] * 7,
        [pltpu.VMEM(v.shape, v.dtype) for v in small] + [pltpu.VMEM((8, 128), F32), pltpu.VMEM((stories, 128), F32), pltpu.SemaphoreType.DMA((18,))],
        moved=1 << 20,
        places=[VM, VM, VM, HB],
    )(*(pltpu.with_memory_space_constraint(v, pltpu.HBM) for v in [u_now, u_prev] + small))
    small_got = swap(small_so, "story", 1)
    so_got = swap(so, "story", 1)
    se_got = swap(se, "story", 0)
    blocks = lax.all_to_all(blocks, "story", 0, 0, tiled=True)
    cells = u_now.shape
    layers = shape(9 * 16, WIDE)
    po_layers, pe_layers, token = call(planes_kernel, [layers, layers, shape(8, 128)], [VM] * 2, flops=1_000_000_000, moved=16 << 20)(u_now, u_prev)
    coef, consts = call(expand_kernel, [table, shape(16, WIDE)], [VM] * 2, flops=20_000_000_000, moved=1 << 30)(blocks, token)
    (po,) = call(pack_po_kernel, [shape(rows, WIDE)], [VM] * 5, planes, moved=1 << 20)(consts, coef, se_got, small_got, po_layers)
    po_got = swap(po, "plan", 1)
    levels = [
        pltpu.VMEM((3, 20, 16, WIDE), F32),
        pltpu.VMEM((3, 18, 16, WIDE), F32),
        pltpu.VMEM((3, 18, 16, WIDE), F32),
    ]
    (pe,) = call(pack_pe_kernel, [shape(rows - 1, WIDE)], [VM] * 5, planes, moved=1 << 20)(consts, coef, se_got, small_got, pe_layers)
    pe_got = swap(pe, "plan", 0)
    side = shape(6, PAD, WIDE)
    inner, base, pe_own, po_own = call(
        main_kernel, [shape(*cells), shape(2, 3, 16, WIDE), side, side], [VM] * 8, levels, flops=60_000_000, moved=4 << 20
    )(consts, coef, se_got, so_got, u_now, u_prev, pe, po)
    held = pltpu.VMEM((3 * PAD, WIDE), F32)
    out, half = call(
        tail_pe_kernel,
        [shape(*cells), shape(3, 16, 8, WIDE)],
        [VM] * 4,
        [held, pltpu.SemaphoreType.DMA((3,))],
        flops=5_000_000,
        moved=2 << 20,
        places=[HB, VM],
    )(coef, pe_got, pe_own, inner)
    (out,) = call(
        tail_po_kernel,
        [shape(*cells)],
        [VM] * 5 + [HB],
        [pltpu.VMEM((3, 16, 8, WIDE), F32), held, pltpu.SemaphoreType.DMA((6,))],
        flops=5_000_000,
        moved=2 << 20,
        places=[HB],
        aliases={5: 0},
    )(coef, po_got, po_own, base, half, out)
    return out


def solution(mesh):
    in_specs = (
        P(None, "story", "plan", None),
        P(None, "story", "plan", None),
        P("story", "plan", None),
        P("story", "plan", None),
        P(),
        P(),
        P(),
    )
    out_specs = P(None, "story", "plan", None)
    return jax.shard_map(local, mesh=mesh, in_specs=in_specs, out_specs=out_specs, check_vma=False)
```

```python
import functools

import jax
import jax.numpy as jnp
from jax import lax
from jax.experimental import pallas as pl
from jax.experimental.pallas import tpu as pltpu
from jax.sharding import PartitionSpec as P

BLOCK = 16
WIDE = 256
PAD = 24
F32 = jnp.float32


def swap(values, axis, first):
    pairs = []
    for low in range(first, lax.axis_size(axis) - 1, 2):
        pairs += [(low, low + 1), (low + 1, low)]
    return lax.ppermute(values, axis, pairs)


def row_shift(v):
    count = v.shape[0] // 8
    row = lax.broadcasted_iota(jnp.int32, (8, v.shape[1]), 0)
    tiles = [v[8 * k : 8 * k + 8] for k in range(count)]
    down, up = [pltpu.roll(t, 1, 0) for t in tiles], [pltpu.roll(t, 7, 0) for t in tiles]
    zero = jnp.zeros_like(tiles[0])
    around = v.shape[0] == PAD
    down, up = [down[-1] if around else zero] + down, up + [up[0] if around else zero]
    lower = [jnp.where(row == 0, down[k], down[k + 1]) for k in range(count)]
    upper = [jnp.where(row == 7, up[k + 1], up[k]) for k in range(count)]
    return jnp.concatenate(lower, 0), jnp.concatenate(upper, 0)


def lane_shift(v):
    half = WIDE // 2
    lane = lax.broadcasted_iota(jnp.int32, (v.shape[0], half), 1)
    first, second = v[:, :half], v[:, half:]
    first_down, second_down = pltpu.roll(first, 1, 1), pltpu.roll(second, 1, 1)
    first_up, second_up = pltpu.roll(first, half - 1, 1), pltpu.roll(second, half - 1, 1)
    lower = [jnp.where(lane == 0, 0.0, first_down), jnp.where(lane == 0, first_down, second_down)]
    upper = [jnp.where(lane == half - 1, second_up, first_up), jnp.where(lane == half - 1, 0.0, second_up)]
    return jnp.concatenate(lower, 1), jnp.concatenate(upper, 1)


def lane_smooth(v):
    lower, upper = lane_shift(v)
    return lower + upper + 4.0 * v


def lane_first(v):
    lower, upper = lane_shift(v)
    return upper - lower


def total(terms):
    terms = [t for t in terms if t is not None]
    return functools.reduce(lambda p, q: p + q, terms)


def stencil(below, here, above, sign=None):
    zs, zf = [], []
    for j in range(3):
        zs.append(total([below and below[j], above and above[j], here and 4.0 * here[j]]))
        if below and above:
            zf.append(above[j] - below[j])
        else:
            zf.append(above[j] if above else -below[j])
    if sign is not None:
        zf = [sign * v for v in zf]
    zs_sh = [row_shift(v) for v in zs]
    zf_sh = [row_shift(v) for v in zf]
    s_zs = [lo + up + 4.0 * v for (lo, up), v in zip(zs_sh, zs)]
    lap = []
    if here:
        s_mid = [lo + up + 4.0 * v for (lo, up), v in zip([row_shift(v) for v in here], here)]
        inner = [s_zs[j] - 2.0 * (s_mid[j] + zs[j]) for j in range(3)]
        curl = 2.0 * s_zs[0] - 12.0 * s_mid[0]
    else:
        inner = [s_zs[j] - 2.0 * zs[j] for j in range(3)]
        curl = 2.0 * s_zs[0]
    for j in range(3):
        lap.append(lane_smooth(inner[j]) - 2.0 * s_zs[j])
    f_zf0 = zf_sh[0][1] - zf_sh[0][0]
    f_zf1 = zf_sh[1][1] - zf_sh[1][0]
    s_zf0 = zf_sh[0][0] + zf_sh[0][1] + 4.0 * zf[0]
    s_zf2 = zf_sh[2][0] + zf_sh[2][1] + 4.0 * zf[2]
    f_zs1 = zs_sh[1][1] - zs_sh[1][0]
    f_zs2 = zs_sh[2][1] - zs_sh[2][0]
    c0 = lane_smooth(curl + 3.0 * f_zf1) + lane_first(3.0 * s_zf2)
    c1 = lane_smooth(2.0 * s_zs[1] - 12.0 * zs[1] + 3.0 * f_zf0) + lane_first(3.0 * f_zs2)
    c2 = lane_first(3.0 * (s_zf0 + f_zs1)) + 2.0 * lane_smooth(s_zs[2]) - 12.0 * s_zs[2]
    return lap, [c0, c1, c2]


def heights():
    row = lax.broadcasted_iota(jnp.int32, (PAD, WIDE), 0)
    return jnp.where(row > 20, row - PAD, row)


def coefficients(own, over, under, carried):
    z = heights()
    zf = z.astype(F32)

    def pick(k):
        return jnp.where(z < 0, under[k], jnp.where(z > 15, over[k], own[k]))

    a, b, g = pick(0), pick(1), pick(2)
    mass, mass_over, mass_under = own[3], over[3], under[3]
    upper = jnp.where(z > 15, carried - mass_over, carried + mass * (15.0 - zf))
    lower = jnp.where(z < 0, carried + 16.0 * mass + mass_under, carried + mass * (16.0 - zf))
    return a, b, g * upper, g * lower


def parity(axis):
    return lax.axis_index(axis) % 2 == 0


def slice_kernel(now, prev, occ_h, mat_h, shear_h, lame_h, dens_h, so, se, blocks, occ, mat, shear_t, lame_t, dens_t, held, held_blocks, sems, *, factor):
    even = parity("story")
    smalls = []
    for k, (source, target) in enumerate(((occ_h, occ), (mat_h, mat), (shear_h, shear_t), (lame_h, lame_t), (dens_h, dens_t))):
        smalls.append(pltpu.make_async_copy(source, target, sems.at[6 + k]))
    copies = []
    for k, out in enumerate((se, so)):
        top = jnp.logical_xor(even, k == 1)
        near, far = jnp.where(top, 15, 0), jnp.where(top, 14, 1)
        for j, (source, z) in enumerate(((now, near), (now, far), (prev, near))):
            copies.append(pltpu.make_async_copy(source.at[:, z], out.at[pl.ds(3 * j, 3)], sems.at[3 * k + j]))
    for copy in smalls + copies:
        copy.start()
    for copy in smalls:
        copy.wait()
    segment = lax.broadcasted_iota(jnp.int32, (8, 128), 1) // BLOCK

    def repeat(ref):
        held[...] = jnp.zeros((8, 128), F32)
        held[0:1, 0:BLOCK] = ref[...].astype(F32)
        once = held[...]
        return once + sum(pltpu.roll(once, BLOCK * k, 1) for k in range(1, 5))

    occupied, which = repeat(occ), repeat(mat)
    found = []
    for table in (shear_t, lame_t, dens_t):
        value = jnp.zeros((8, 128), F32)
        for k in range(table.shape[1]):
            value = jnp.where(which == k, table[0:1, k : k + 1], value)
        found.append(value)
    shear, lame, dens = found
    scale = occupied * (0.1 / dens)
    parts = (scale * shear * (1.0 / 12.0), scale * (lame + shear) * (1.0 / 72.0), scale * factor, dens * occupied, occupied)
    row = jnp.zeros((8, 128), F32)
    for k, part in enumerate(parts):
        row = jnp.where(segment == k, part, row)
    held_blocks[...] = jnp.broadcast_to(row[0:1], held_blocks.shape)
    copies.append(pltpu.make_async_copy(held_blocks, blocks, sems.at[11]))
    copies[-1].start()
    for copy in copies:
        copy.wait()


def ghost_of(se, so, consts):
    even = parity("story")

    def ghost(over, plane, *where):
        take = even if over else jnp.logical_not(even)
        row = 9 if over else 14
        return jnp.where(take, se[(plane,) + where], so[(plane,) + where]) * consts[row : row + 1, :]

    return ghost


def edge_of(se, so, consts):
    even = parity("story")

    def edge(over, plane, x):
        take = even if over else jnp.logical_not(even)
        row = 9 if over else 14
        return jnp.where(take, se[plane, x : x + 1, :], so[plane, x : x + 1, :]) * consts[row : row + 1, :]

    return edge


def planes_kernel(now, prev, po, pe, token):
    even = parity("plan")
    token[...] = jnp.zeros(token.shape, F32)

    def load(out, near, far):
        for k, (source, x) in enumerate(((now, near), (now, far), (prev, near))):
            for c in range(3):
                base = (3 * k + c) * 16
                out[base : base + 16, :] = source[c, :, x, :]

    @pl.when(even)
    def _():
        load(pe, 15, 14)
        load(po, 0, 1)

    @pl.when(jnp.logical_not(even))
    def _():
        load(pe, 0, 1)
        load(po, 15, 14)


def fill(right, edge, consts, coef, layers, out, far_rows, prev_rows):
    occupied = consts[4:5, :]

    def load(near, far):
        for kind, (target, x, sides) in enumerate(((out, near, (0, 3)), (far_rows, far, (0, 3)), (prev_rows, near, (6,)))):
            for c in range(3):
                base = c * PAD
                at = (3 * kind + c) * 16
                target[base : base + 16, :] = layers[at : at + 16, :] * occupied
                for k, side in enumerate(sides):
                    target[base + 23 - k : base + 24 - k, :] = edge(False, side + c, x)
                    target[base + 16 + k : base + 17 + k, :] = edge(True, side + c, x)

    @pl.when(right)
    def _():
        load(15, 14)

    @pl.when(jnp.logical_not(right))
    def _():
        load(0, 1)

    order = (1, 0, 2)

    def planes(ref):
        return [ref[c * PAD : (c + 1) * PAD, :] for c in order]

    first = advance(planes(far_rows), planes(out), None, planes(prev_rows), [coef[k] for k in range(4)], jnp.where(right, 1.0, -1.0))
    lane = lax.broadcasted_iota(jnp.int32, (1, WIDE), 1)
    for k, c in enumerate(order):
        count = 16 if c < 2 else 15
        out[3 * PAD + 16 * c : 3 * PAD + 16 * c + count, :] = first[k][0:count]
        out[c * PAD + 18 : c * PAD + 19, :] = first[k][23:24]
        out[c * PAD + 19 : c * PAD + 20, :] = first[k][16:17]
    out[2 * PAD + 21 : 2 * PAD + 22, :] = first[order.index(2)][15:16]
    for k, row in enumerate((20, 21)):
        out[row : row + 1, :] = consts[k : k + 1, :]
        out[PAD + row : PAD + row + 1, :] = jnp.where(lane % 2 == 0, consts[5 + k : 6 + k, :], consts[10 + k : 11 + k, :])


def expand_kernel(blocks, token, coef, consts):
    place = lax.axis_index("story")
    step = lax.broadcasted_iota(jnp.int32, blocks.shape, 0)
    rows = [jnp.sum(jnp.where(step == place + k, blocks[...], 0.0), 0, keepdims=True) for k in (0, 1, -1)]
    rows.append(16.0 * jnp.sum(jnp.where(step > place, blocks[...], 0.0), 0, keepdims=True))
    stacked = jnp.concatenate(rows + [jnp.zeros((4, 128), F32)], 0)
    lane = lax.broadcasted_iota(jnp.int32, (8, 128), 1) // BLOCK

    def spread(k):
        halves = [jnp.take_along_axis(stacked, lane + (BLOCK * k + 8 * h), 1, mode="promise_in_bounds") for h in (0, 1)]
        return jnp.concatenate(halves, 1)

    sets = [[], [], []]
    for k in range(5):
        wide = spread(k)
        for j in range(3):
            sets[j].append(wide[j : j + 1])
            consts[5 * j + k : 5 * j + k + 1, :] = wide[j : j + 1]
        if k == 3:
            carried = wide[3:4]
    consts[15:16, :] = carried
    for k, value in enumerate(coefficients(sets[0], sets[1], sets[2], carried)):
        coef[k] = value


def pack_po_kernel(consts, coef, se, so, layers, po, far_rows, prev_rows):
    fill(jnp.logical_not(parity("plan")), edge_of(se, so, consts), consts, coef, layers, po, far_rows, prev_rows)


def advance(below, here, above, before, coefs, sign):
    a, b, gu, gd = coefs
    lap, coup = stencil(below, here, above, sign)
    news = []
    for c in range(3):
        lower, upper = row_shift(here[c])
        news.append(update(here[c], before[c], lap[c], coup[c], a, b, gu, gd, lower, upper))
    return news


def update(here, before, lap, coup, a, b, gu, gd, below, above):
    geometric = gu * (above - here) - gd * (here - below)
    return 2.0 * here - before + a * lap + b * coup - geometric


def both_steps(consts, coef, se, so, now, prev, out, u0, u1, before):
    ghost = ghost_of(se, so, consts)
    occupied = jnp.broadcast_to(consts[4:5, :], (16, WIDE))
    for c in range(3):
        u0[c, 0] = ghost(False, 3 + c)
        u0[c, 1] = ghost(False, c)
        u0[c, 18] = ghost(True, c)
        u0[c, 19] = ghost(True, 3 + c)
        before[c, 0] = ghost(False, 6 + c)
        before[c, 17] = ghost(True, 6 + c)

    @pl.loop(0, 16, unroll=4)
    def _(z):
        for c in range(3):
            u0[c, z + 2] = now[c, z] * occupied
            before[c, z + 1] = prev[c, z] * occupied

    def one(source, earlier, target, i, z):
        below, here, above = ([source[c, i + k] for c in range(3)] for k in range(3))
        lap, coup = stencil(below, here, above)
        a, b, gu, gd = (coef[k, pl.ds(z, 1), :] for k in range(4))
        for c in range(3):
            target[c, i] = update(here[c], earlier(c, i), lap[c], coup[c], a, b, gu, gd, below[c], above[c])

    @pl.loop(0, 18, unroll=6)
    def _(i):
        one(u0, lambda c, i: before[c, i], u1, i, jnp.where(i == 0, PAD - 1, i - 1))

    @pl.loop(0, 16, unroll=8)
    def _(i):
        one(u1, lambda c, i: u0[c, i + 2], out, i, i)


def pack_pe_kernel(consts, coef, se, so, layers, pe, far_rows, prev_rows):
    fill(parity("plan"), edge_of(se, so, consts), consts, coef, layers, pe, far_rows, prev_rows)


def planes_of(ref):
    return [ref[c * PAD : (c + 1) * PAD, :] for c in (1, 0, 2)]


def side_sign(right):
    return jnp.where(right, 1.0, -1.0)


def main_kernel(consts, coef, se, so, now, prev, pe_sent, po_sent, inner, base, pe_own, po_own, u0, u1, before):
    right = parity("plan")
    both_steps(consts, coef, se, so, now, prev, inner, u0, u1, before)
    for sent, own, sign in ((pe_sent, pe_own, side_sign(right)), (po_sent, po_own, -side_sign(right))):
        for k, v in enumerate(sum(stencil(planes_of(sent), None, None, sign), [])):
            own[k] = v

    def finish(near, far):
        for c in range(3):
            base[0, c] = inner[c, :, near, :]
            base[1, c] = inner[c, :, far, :]

    @pl.when(right)
    def _():
        finish(0, 1)

    @pl.when(jnp.logical_not(right))
    def _():
        finish(15, 14)


def rows_of(v):
    lower, upper = row_shift(v)
    return lower + upper + 4.0 * v, upper - lower


def outer_terms(layer, sign):
    (v0, s0, f0), (v1, s1, f1), (v2, s2, f2) = layer
    lap = [lane_smooth(s - 2.0 * v) - 2.0 * s for v, s, _ in layer]
    c0 = lane_smooth(2.0 * s0 + (3.0 * sign) * f1) + lane_first((3.0 * sign) * s2)
    c1 = lane_smooth(2.0 * s1 - 12.0 * v1 + (3.0 * sign) * f0) + lane_first(3.0 * f2)
    c2 = lane_first(3.0 * (sign * s0 + f1)) + 2.0 * lane_smooth(s2) - 12.0 * s2
    return lap, [c0, c1, c2]


def both_terms(here, outer, sign):
    zs = [o[0] + 4.0 * h[0] for h, o in zip(here, outer)]
    s_zs = [o[1] + 4.0 * h[1] for h, o in zip(here, outer)]
    f_zs = [o[2] + 4.0 * h[2] for h, o in zip(here, outer)]
    lap = [lane_smooth(s_zs[j] - 2.0 * (here[j][1] + zs[j])) - 2.0 * s_zs[j] for j in range(3)]
    c0 = lane_smooth(2.0 * s_zs[0] - 12.0 * here[0][1] + (3.0 * sign) * outer[1][2]) + lane_first((3.0 * sign) * outer[2][1])
    c1 = lane_smooth(2.0 * s_zs[1] - 12.0 * zs[1] + (3.0 * sign) * outer[0][2]) + lane_first(3.0 * f_zs[2])
    c2 = lane_first(3.0 * (sign * outer[0][1] + f_zs[1])) + 2.0 * lane_smooth(s_zs[2]) - 12.0 * s_zs[2]
    return lap, [c0, c1, c2]


def one_side(coef, got, held, own, sign):
    for c in range(3):
        base = c * PAD
        count = 16 if c < 2 else 15
        held[base : base + count, :] = got[3 * PAD + 16 * c : 3 * PAD + 16 * c + count, :]
        held[base + 16 : base + 17, :] = got[base + 19 : base + 20, :]
        held[base + 23 : base + 24, :] = got[base + 18 : base + 19, :]
    held[2 * PAD + 15 : 2 * PAD + 16, :] = got[2 * PAD + 21 : 2 * PAD + 22, :]
    a, b, gu, gd = (coef[k] for k in range(4))
    z = heights()
    even = lax.broadcasted_iota(jnp.int32, (8, WIDE), 1) % 2 == 0

    def pick(row):
        mixed = jnp.broadcast_to(got[PAD + row : PAD + row + 1, :], (8, WIDE))
        lower, upper = lane_shift(mixed)
        over = jnp.where(even, mixed, lower)[0:1]
        under = jnp.where(even, upper, mixed)[0:1]
        return jnp.where(z < 0, under, jnp.where(z > 15, over, got[row : row + 1, :]))

    got_a, got_b = pick(20), pick(21)
    lap, coup = outer_terms([(v,) + rows_of(v) for v in planes_of(got)], sign)
    delta = [a * lap[k] + b * coup[k] for k in range(3)]
    outer = [p + got_a * own[k] + got_b * own[3 + k] for k, p in enumerate(planes_of(held))]
    delta_rows = [tuple(p[0:16] for p in (v,) + rows_of(v)) for v in delta]
    outer_rows = [tuple(p[0:16] for p in (v,) + rows_of(v)) for v in outer]
    far_lap, far_coup = outer_terms(delta_rows, sign)
    near_lap, near_coup = both_terms(delta_rows, outer_rows, sign)
    a, b, gu, gd = (coef[k, 0:16] for k in range(4))
    near, far = [None] * 3, [None] * 3
    for k, c in enumerate((1, 0, 2)):
        lower, upper = (v[0:16] for v in row_shift(delta[k]))
        here = delta[k][0:16]
        geometric = gu * (upper - here) - gd * (here - lower)
        near[c] = 2.0 * here + a * near_lap[k] + b * near_coup[k] - geometric
        far[c] = a * far_lap[k] + b * far_coup[k]
    return near, far


def tail_pe_kernel(coef, got, own, inner, out, half, held, sems):
    right = parity("plan")
    start = pl.multiple_of(jnp.where(right, 0, 8), 8)
    copies = [pltpu.make_async_copy(inner.at[c, :, pl.ds(start, 8), :], out.at[c, :, pl.ds(start, 8), :], sems.at[c]) for c in range(3)]
    for copy in copies:
        copy.start()
    near, far = one_side(coef, got, held, own, side_sign(right))

    def finish(row, next_row, first):
        for c in range(3):
            half[c] = inner[c, :, first : first + 8, :]
            half[c, :, row - first, :] += near[c]
            half[c, :, next_row - first, :] += far[c]

    @pl.when(right)
    def _():
        finish(15, 14, 8)

    @pl.when(jnp.logical_not(right))
    def _():
        finish(0, 1, 0)

    for copy in copies:
        copy.wait()


def tail_po_kernel(coef, got, own, base, half, before, out, work, held, sems):
    right = jnp.logical_not(parity("plan"))
    start = pl.multiple_of(jnp.where(right, 0, 8), 8)
    copies = [pltpu.make_async_copy(half.at[c], out.at[c, :, pl.ds(start, 8), :], sems.at[c]) for c in range(3)]
    for copy in copies:
        copy.start()
    near, far = one_side(coef, got, held, own, side_sign(right))

    def finish(row, next_row, first):
        last = []
        for c in range(3):
            work[c, :, row, :] = base[0, c] + near[c]
            work[c, :, next_row, :] = base[1, c] + far[c]
            rows = pl.ds(min(row, next_row), 2)
            last.append(pltpu.make_async_copy(work.at[c, :, rows, :], out.at[c, :, pl.ds(first + min(row, next_row), 2), :], sems.at[3 + c]))
            last[-1].start()
        for copy in last:
            copy.wait()

    @pl.when(right)
    def _():
        finish(7, 6, 8)

    @pl.when(jnp.logical_not(right))
    def _():
        finish(0, 1, 0)

    for copy in copies:
        copy.wait()


VM = pl.BlockSpec(memory_space=pltpu.VMEM)
HB = pl.BlockSpec(memory_space=pltpu.HBM)


def shape(*dims):
    return jax.ShapeDtypeStruct(dims, F32)


def call(kernel, outs, ins, scratch=(), flops=0, moved=0, grant=24.0, places=None, aliases=None):
    return pl.pallas_call(
        kernel,
        out_shape=outs,
        in_specs=ins,
        out_specs=places or [VM] * len(outs),
        scratch_shapes=list(scratch),
        input_output_aliases=aliases or {},
        compiler_params=pltpu.CompilerParams(vmem_limit_bytes=int(grant * 2**20)),
        cost_estimate=pl.CostEstimate(flops=flops, bytes_accessed=moved, transcendentals=0),
    )


def local(u_now, u_prev, occupancy, materials, shear_table, lame_table, density_table):
    height = u_now.shape[1] * lax.axis_size("story")
    stories = lax.axis_size("story")
    face, table = shape(9, 16, WIDE), shape(4, PAD, WIDE)
    rows = 3 * PAD + 48
    planes = [pltpu.VMEM((3 * PAD, WIDE), F32)] * 2
    small = [v.reshape(1, -1) for v in (occupancy, materials, shear_table, lame_table, density_table)]
    so, se, blocks = call(
        functools.partial(slice_kernel, factor=0.8 / height),
        [face, shape(10, 16, WIDE), shape(stories, 128)],
        [HB] * 7,
        [pltpu.VMEM(v.shape, v.dtype) for v in small] + [pltpu.VMEM((8, 128), F32), pltpu.VMEM((stories, 128), F32), pltpu.SemaphoreType.DMA((12,))],
        moved=1 << 20,
        places=[VM, VM, HB],
    )(*(pltpu.with_memory_space_constraint(v, pltpu.HBM) for v in [u_now, u_prev] + small))
    so_got = swap(so, "story", 1)
    se_got = swap(se, "story", 0)
    blocks = lax.all_to_all(blocks, "story", 0, 0, tiled=True)
    cells = u_now.shape
    layers = shape(9 * 16, WIDE)
    po_layers, pe_layers, token = call(planes_kernel, [layers, layers, shape(8, 128)], [VM] * 2, flops=1_000_000_000, moved=16 << 20)(u_now, u_prev)
    coef, consts = call(expand_kernel, [table, shape(16, WIDE)], [VM] * 2, flops=20_000_000_000, moved=1 << 30)(blocks, token)
    (po,) = call(pack_po_kernel, [shape(rows, WIDE)], [VM] * 5, planes, moved=1 << 20)(consts, coef, se_got, so_got, po_layers)
    po_got = swap(po, "plan", 1)
    levels = [
        pltpu.VMEM((3, 20, 16, WIDE), F32),
        pltpu.VMEM((3, 18, 16, WIDE), F32),
        pltpu.VMEM((3, 18, 16, WIDE), F32),
    ]
    (pe,) = call(pack_pe_kernel, [shape(rows - 1, WIDE)], [VM] * 5, planes, moved=1 << 20)(consts, coef, se_got, so_got, pe_layers)
    pe_got = swap(pe, "plan", 0)
    side = shape(6, PAD, WIDE)
    inner, base, pe_own, po_own = call(
        main_kernel, [shape(*cells), shape(2, 3, 16, WIDE), side, side], [VM] * 8, levels, flops=60_000_000, moved=4 << 20
    )(consts, coef, se_got, so_got, u_now, u_prev, pe, po)
    held = pltpu.VMEM((3 * PAD, WIDE), F32)
    out, half = call(
        tail_pe_kernel,
        [shape(*cells), shape(3, 16, 8, WIDE)],
        [VM] * 4,
        [held, pltpu.SemaphoreType.DMA((3,))],
        flops=5_000_000,
        moved=2 << 20,
        places=[HB, VM],
    )(coef, pe_got, pe_own, inner)
    (out,) = call(
        tail_po_kernel,
        [shape(*cells)],
        [VM] * 5 + [HB],
        [pltpu.VMEM((3, 16, 8, WIDE), F32), held, pltpu.SemaphoreType.DMA((6,))],
        flops=5_000_000,
        moved=2 << 20,
        places=[HB],
        aliases={5: 0},
    )(coef, po_got, po_own, base, half, out)
    return out


def solution(mesh):
    in_specs = (
        P(None, "story", "plan", None),
        P(None, "story", "plan", None),
        P("story", "plan", None),
        P("story", "plan", None),
        P(),
        P(),
        P(),
    )
    out_specs = P(None, "story", "plan", None)
    return jax.shard_map(local, mesh=mesh, in_specs=in_specs, out_specs=out_specs, check_vma=False)
```

```python
import functools

import jax
import jax.numpy as jnp
from jax import lax
from jax.experimental import pallas as pl
from jax.experimental.pallas import tpu as pltpu
from jax.sharding import PartitionSpec as P

BLOCK = 16
WIDE = 256
PAD = 24
F32 = jnp.float32


def swap(values, axis, first):
    pairs = []
    for low in range(first, lax.axis_size(axis) - 1, 2):
        pairs += [(low, low + 1), (low + 1, low)]
    return lax.ppermute(values, axis, pairs)


def row_shift(v):
    count = v.shape[0] // 8
    row = lax.broadcasted_iota(jnp.int32, (8, v.shape[1]), 0)
    tiles = [v[8 * k : 8 * k + 8] for k in range(count)]
    down, up = [pltpu.roll(t, 1, 0) for t in tiles], [pltpu.roll(t, 7, 0) for t in tiles]
    zero = jnp.zeros_like(tiles[0])
    around = v.shape[0] == PAD
    down, up = [down[-1] if around else zero] + down, up + [up[0] if around else zero]
    lower = [jnp.where(row == 0, down[k], down[k + 1]) for k in range(count)]
    upper = [jnp.where(row == 7, up[k + 1], up[k]) for k in range(count)]
    return jnp.concatenate(lower, 0), jnp.concatenate(upper, 0)


def lane_shift(v):
    half = WIDE // 2
    lane = lax.broadcasted_iota(jnp.int32, (v.shape[0], half), 1)
    first, second = v[:, :half], v[:, half:]
    first_down, second_down = pltpu.roll(first, 1, 1), pltpu.roll(second, 1, 1)
    first_up, second_up = pltpu.roll(first, half - 1, 1), pltpu.roll(second, half - 1, 1)
    lower = [jnp.where(lane == 0, 0.0, first_down), jnp.where(lane == 0, first_down, second_down)]
    upper = [jnp.where(lane == half - 1, second_up, first_up), jnp.where(lane == half - 1, 0.0, second_up)]
    return jnp.concatenate(lower, 1), jnp.concatenate(upper, 1)


def lane_smooth(v):
    lower, upper = lane_shift(v)
    return lower + upper + 4.0 * v


def lane_first(v):
    lower, upper = lane_shift(v)
    return upper - lower


def total(terms):
    terms = [t for t in terms if t is not None]
    return functools.reduce(lambda p, q: p + q, terms)


def stencil(below, here, above, sign=None):
    zs, zf = [], []
    for j in range(3):
        zs.append(total([below and below[j], above and above[j], here and 4.0 * here[j]]))
        if below and above:
            zf.append(above[j] - below[j])
        else:
            zf.append(above[j] if above else -below[j])
    if sign is not None:
        zf = [sign * v for v in zf]
    zs_sh = [row_shift(v) for v in zs]
    zf_sh = [row_shift(v) for v in zf]
    s_zs = [lo + up + 4.0 * v for (lo, up), v in zip(zs_sh, zs)]
    lap = []
    if here:
        s_mid = [lo + up + 4.0 * v for (lo, up), v in zip([row_shift(v) for v in here], here)]
        inner = [s_zs[j] - 2.0 * (s_mid[j] + zs[j]) for j in range(3)]
        curl = 2.0 * s_zs[0] - 12.0 * s_mid[0]
    else:
        inner = [s_zs[j] - 2.0 * zs[j] for j in range(3)]
        curl = 2.0 * s_zs[0]
    for j in range(3):
        lap.append(lane_smooth(inner[j]) - 2.0 * s_zs[j])
    f_zf0 = zf_sh[0][1] - zf_sh[0][0]
    f_zf1 = zf_sh[1][1] - zf_sh[1][0]
    s_zf0 = zf_sh[0][0] + zf_sh[0][1] + 4.0 * zf[0]
    s_zf2 = zf_sh[2][0] + zf_sh[2][1] + 4.0 * zf[2]
    f_zs1 = zs_sh[1][1] - zs_sh[1][0]
    f_zs2 = zs_sh[2][1] - zs_sh[2][0]
    c0 = lane_smooth(curl + 3.0 * f_zf1) + lane_first(3.0 * s_zf2)
    c1 = lane_smooth(2.0 * s_zs[1] - 12.0 * zs[1] + 3.0 * f_zf0) + lane_first(3.0 * f_zs2)
    c2 = lane_first(3.0 * (s_zf0 + f_zs1)) + 2.0 * lane_smooth(s_zs[2]) - 12.0 * s_zs[2]
    return lap, [c0, c1, c2]


def heights():
    row = lax.broadcasted_iota(jnp.int32, (PAD, WIDE), 0)
    return jnp.where(row > 20, row - PAD, row)


def coefficients(own, over, under, carried):
    z = heights()
    zf = z.astype(F32)

    def pick(k):
        return jnp.where(z < 0, under[k], jnp.where(z > 15, over[k], own[k]))

    a, b, g = pick(0), pick(1), pick(2)
    mass, mass_over, mass_under = own[3], over[3], under[3]
    upper = jnp.where(z > 15, carried - mass_over, carried + mass * (15.0 - zf))
    lower = jnp.where(z < 0, carried + 16.0 * mass + mass_under, carried + mass * (16.0 - zf))
    return a, b, g * upper, g * lower


def parity(axis):
    return lax.axis_index(axis) % 2 == 0


def slice_kernel(now, prev, occ_h, mat_h, shear_h, lame_h, dens_h, small, se, so, blocks, occ, mat, shear_t, lame_t, dens_t, held, held_blocks, sems, *, factor):
    even = parity("story")
    smalls = []
    for k, (source, target) in enumerate(((occ_h, occ), (mat_h, mat), (shear_h, shear_t), (lame_h, lame_t), (dens_h, dens_t))):
        smalls.append(pltpu.make_async_copy(source, target, sems.at[6 + k]))
    copies = []
    for k, out in enumerate((se, so)):
        top = jnp.logical_xor(even, k == 1)
        near, far = jnp.where(top, 15, 0), jnp.where(top, 14, 1)
        for j, (source, z) in enumerate(((now, near), (now, far), (prev, near))):
            copies.append(pltpu.make_async_copy(source.at[:, z], out.at[pl.ds(3 * j, 3)], sems.at[3 * k + j]))
            if k == 1:
                for h, x in enumerate((0, 14)):
                    rows = small.at[pl.ds(3 * j, 3), pl.ds(2 * h, 2), :]
                    copies.append(pltpu.make_async_copy(source.at[:, z, pl.ds(x, 2), :], rows, sems.at[12 + 2 * j + h]))
    for copy in smalls + copies:
        copy.start()
    for copy in smalls:
        copy.wait()
    segment = lax.broadcasted_iota(jnp.int32, (8, 128), 1) // BLOCK

    def repeat(ref):
        held[...] = jnp.zeros((8, 128), F32)
        held[0:1, 0:BLOCK] = ref[...].astype(F32)
        once = held[...]
        return once + sum(pltpu.roll(once, BLOCK * k, 1) for k in range(1, 5))

    occupied, which = repeat(occ), repeat(mat)
    found = []
    for table in (shear_t, lame_t, dens_t):
        value = jnp.zeros((8, 128), F32)
        for k in range(table.shape[1]):
            value = jnp.where(which == k, table[0:1, k : k + 1], value)
        found.append(value)
    shear, lame, dens = found
    scale = occupied * (0.1 / dens)
    parts = (scale * shear * (1.0 / 12.0), scale * (lame + shear) * (1.0 / 72.0), scale * factor, dens * occupied, occupied)
    row = jnp.zeros((8, 128), F32)
    for k, part in enumerate(parts):
        row = jnp.where(segment == k, part, row)
    held_blocks[...] = jnp.broadcast_to(row[0:1], held_blocks.shape)
    copies.append(pltpu.make_async_copy(held_blocks, blocks, sems.at[11]))
    copies[-1].start()
    for copy in copies:
        copy.wait()


def ghost_of(se, so, consts):
    even = parity("story")

    def ghost(over, plane, *where):
        take = even if over else jnp.logical_not(even)
        row = 9 if over else 14
        return jnp.where(take, se[(plane,) + where], so[(plane,) + where]) * consts[row : row + 1, :]

    return ghost


def edge_of(se, small, consts):
    even = parity("story")

    def edge(over, plane, x):
        take = even if over else jnp.logical_not(even)
        row = 9 if over else 14
        at = x % 12
        return jnp.where(take, se[plane, x : x + 1, :], small[plane, at : at + 1, :]) * consts[row : row + 1, :]

    return edge


def planes_kernel(now, prev, po, pe, token):
    even = parity("plan")
    token[...] = jnp.zeros(token.shape, F32)

    def load(out, near, far):
        for k, (source, x) in enumerate(((now, near), (now, far), (prev, near))):
            for c in range(3):
                base = (3 * k + c) * 16
                out[base : base + 16, :] = source[c, :, x, :]

    @pl.when(even)
    def _():
        load(pe, 15, 14)
        load(po, 0, 1)

    @pl.when(jnp.logical_not(even))
    def _():
        load(pe, 0, 1)
        load(po, 15, 14)


def fill(right, edge, consts, coef, layers, out, far_rows, prev_rows):
    occupied = consts[4:5, :]

    def load(near, far):
        for kind, (target, x, sides) in enumerate(((out, near, (0, 3)), (far_rows, far, (0, 3)), (prev_rows, near, (6,)))):
            for c in range(3):
                base = c * PAD
                at = (3 * kind + c) * 16
                target[base : base + 16, :] = layers[at : at + 16, :] * occupied
                for k, side in enumerate(sides):
                    target[base + 23 - k : base + 24 - k, :] = edge(False, side + c, x)
                    target[base + 16 + k : base + 17 + k, :] = edge(True, side + c, x)

    @pl.when(right)
    def _():
        load(15, 14)

    @pl.when(jnp.logical_not(right))
    def _():
        load(0, 1)

    order = (1, 0, 2)

    def planes(ref):
        return [ref[c * PAD : (c + 1) * PAD, :] for c in order]

    first = advance(planes(far_rows), planes(out), None, planes(prev_rows), [coef[k] for k in range(4)], jnp.where(right, 1.0, -1.0))
    lane = lax.broadcasted_iota(jnp.int32, (1, WIDE), 1)
    for k, c in enumerate(order):
        count = 16 if c < 2 else 15
        out[3 * PAD + 16 * c : 3 * PAD + 16 * c + count, :] = first[k][0:count]
        out[c * PAD + 18 : c * PAD + 19, :] = first[k][23:24]
        out[c * PAD + 19 : c * PAD + 20, :] = first[k][16:17]
    out[2 * PAD + 21 : 2 * PAD + 22, :] = first[order.index(2)][15:16]
    for k, row in enumerate((20, 21)):
        out[row : row + 1, :] = consts[k : k + 1, :]
        out[PAD + row : PAD + row + 1, :] = jnp.where(lane % 2 == 0, consts[5 + k : 6 + k, :], consts[10 + k : 11 + k, :])


def expand_kernel(blocks, token, coef, consts):
    place = lax.axis_index("story")
    step = lax.broadcasted_iota(jnp.int32, blocks.shape, 0)
    rows = [jnp.sum(jnp.where(step == place + k, blocks[...], 0.0), 0, keepdims=True) for k in (0, 1, -1)]
    rows.append(16.0 * jnp.sum(jnp.where(step > place, blocks[...], 0.0), 0, keepdims=True))
    stacked = jnp.concatenate(rows + [jnp.zeros((4, 128), F32)], 0)
    lane = lax.broadcasted_iota(jnp.int32, (8, 128), 1) // BLOCK

    def spread(k):
        halves = [jnp.take_along_axis(stacked, lane + (BLOCK * k + 8 * h), 1, mode="promise_in_bounds") for h in (0, 1)]
        return jnp.concatenate(halves, 1)

    sets = [[], [], []]
    for k in range(5):
        wide = spread(k)
        for j in range(3):
            sets[j].append(wide[j : j + 1])
            consts[5 * j + k : 5 * j + k + 1, :] = wide[j : j + 1]
        if k == 3:
            carried = wide[3:4]
    consts[15:16, :] = carried
    for k, value in enumerate(coefficients(sets[0], sets[1], sets[2], carried)):
        coef[k] = value


def pack_po_kernel(consts, coef, se, small, layers, po, far_rows, prev_rows):
    fill(jnp.logical_not(parity("plan")), edge_of(se, small, consts), consts, coef, layers, po, far_rows, prev_rows)


def advance(below, here, above, before, coefs, sign):
    a, b, gu, gd = coefs
    lap, coup = stencil(below, here, above, sign)
    news = []
    for c in range(3):
        lower, upper = row_shift(here[c])
        news.append(update(here[c], before[c], lap[c], coup[c], a, b, gu, gd, lower, upper))
    return news


def update(here, before, lap, coup, a, b, gu, gd, below, above):
    geometric = gu * (above - here) - gd * (here - below)
    return 2.0 * here - before + a * lap + b * coup - geometric


def both_steps(consts, coef, se, so, now, prev, out, u0, u1, before):
    ghost = ghost_of(se, so, consts)
    occupied = jnp.broadcast_to(consts[4:5, :], (16, WIDE))
    for c in range(3):
        u0[c, 0] = ghost(False, 3 + c)
        u0[c, 1] = ghost(False, c)
        u0[c, 18] = ghost(True, c)
        u0[c, 19] = ghost(True, 3 + c)
        before[c, 0] = ghost(False, 6 + c)
        before[c, 17] = ghost(True, 6 + c)

    @pl.loop(0, 16, unroll=4)
    def _(z):
        for c in range(3):
            u0[c, z + 2] = now[c, z] * occupied
            before[c, z + 1] = prev[c, z] * occupied

    def one(source, earlier, target, i, z):
        below, here, above = ([source[c, i + k] for c in range(3)] for k in range(3))
        lap, coup = stencil(below, here, above)
        a, b, gu, gd = (coef[k, pl.ds(z, 1), :] for k in range(4))
        for c in range(3):
            target[c, i] = update(here[c], earlier(c, i), lap[c], coup[c], a, b, gu, gd, below[c], above[c])

    @pl.loop(0, 18, unroll=6)
    def _(i):
        one(u0, lambda c, i: before[c, i], u1, i, jnp.where(i == 0, PAD - 1, i - 1))

    @pl.loop(0, 16, unroll=8)
    def _(i):
        one(u1, lambda c, i: u0[c, i + 2], out, i, i)


def pack_pe_kernel(consts, coef, se, small, layers, pe, far_rows, prev_rows):
    fill(parity("plan"), edge_of(se, small, consts), consts, coef, layers, pe, far_rows, prev_rows)


def planes_of(ref):
    return [ref[c * PAD : (c + 1) * PAD, :] for c in (1, 0, 2)]


def side_sign(right):
    return jnp.where(right, 1.0, -1.0)


def main_kernel(consts, coef, se, so, now, prev, pe_sent, po_sent, inner, base, pe_own, po_own, u0, u1, before):
    right = parity("plan")
    both_steps(consts, coef, se, so, now, prev, inner, u0, u1, before)
    for sent, own, sign in ((pe_sent, pe_own, side_sign(right)), (po_sent, po_own, -side_sign(right))):
        for k, v in enumerate(sum(stencil(planes_of(sent), None, None, sign), [])):
            own[k] = v

    def finish(near, far):
        for c in range(3):
            base[0, c] = inner[c, :, near, :]
            base[1, c] = inner[c, :, far, :]

    @pl.when(right)
    def _():
        finish(0, 1)

    @pl.when(jnp.logical_not(right))
    def _():
        finish(15, 14)


def rows_of(v):
    lower, upper = row_shift(v)
    return lower + upper + 4.0 * v, upper - lower


def outer_terms(layer, sign):
    (v0, s0, f0), (v1, s1, f1), (v2, s2, f2) = layer
    lap = [lane_smooth(s - 2.0 * v) - 2.0 * s for v, s, _ in layer]
    c0 = lane_smooth(2.0 * s0 + (3.0 * sign) * f1) + lane_first((3.0 * sign) * s2)
    c1 = lane_smooth(2.0 * s1 - 12.0 * v1 + (3.0 * sign) * f0) + lane_first(3.0 * f2)
    c2 = lane_first(3.0 * (sign * s0 + f1)) + 2.0 * lane_smooth(s2) - 12.0 * s2
    return lap, [c0, c1, c2]


def both_terms(here, outer, sign):
    zs = [o[0] + 4.0 * h[0] for h, o in zip(here, outer)]
    s_zs = [o[1] + 4.0 * h[1] for h, o in zip(here, outer)]
    f_zs = [o[2] + 4.0 * h[2] for h, o in zip(here, outer)]
    lap = [lane_smooth(s_zs[j] - 2.0 * (here[j][1] + zs[j])) - 2.0 * s_zs[j] for j in range(3)]
    c0 = lane_smooth(2.0 * s_zs[0] - 12.0 * here[0][1] + (3.0 * sign) * outer[1][2]) + lane_first((3.0 * sign) * outer[2][1])
    c1 = lane_smooth(2.0 * s_zs[1] - 12.0 * zs[1] + (3.0 * sign) * outer[0][2]) + lane_first(3.0 * f_zs[2])
    c2 = lane_first(3.0 * (sign * outer[0][1] + f_zs[1])) + 2.0 * lane_smooth(s_zs[2]) - 12.0 * s_zs[2]
    return lap, [c0, c1, c2]


def one_side(coef, got, held, own, sign):
    for c in range(3):
        base = c * PAD
        count = 16 if c < 2 else 15
        held[base : base + count, :] = got[3 * PAD + 16 * c : 3 * PAD + 16 * c + count, :]
        held[base + 16 : base + 17, :] = got[base + 19 : base + 20, :]
        held[base + 23 : base + 24, :] = got[base + 18 : base + 19, :]
    held[2 * PAD + 15 : 2 * PAD + 16, :] = got[2 * PAD + 21 : 2 * PAD + 22, :]
    a, b, gu, gd = (coef[k] for k in range(4))
    z = heights()
    even = lax.broadcasted_iota(jnp.int32, (8, WIDE), 1) % 2 == 0

    def pick(row):
        mixed = jnp.broadcast_to(got[PAD + row : PAD + row + 1, :], (8, WIDE))
        lower, upper = lane_shift(mixed)
        over = jnp.where(even, mixed, lower)[0:1]
        under = jnp.where(even, upper, mixed)[0:1]
        return jnp.where(z < 0, under, jnp.where(z > 15, over, got[row : row + 1, :]))

    got_a, got_b = pick(20), pick(21)
    lap, coup = outer_terms([(v,) + rows_of(v) for v in planes_of(got)], sign)
    delta = [a * lap[k] + b * coup[k] for k in range(3)]
    outer = [p + got_a * own[k] + got_b * own[3 + k] for k, p in enumerate(planes_of(held))]
    delta_rows = [tuple(p[0:16] for p in (v,) + rows_of(v)) for v in delta]
    outer_rows = [tuple(p[0:16] for p in (v,) + rows_of(v)) for v in outer]
    far_lap, far_coup = outer_terms(delta_rows, sign)
    near_lap, near_coup = both_terms(delta_rows, outer_rows, sign)
    a, b, gu, gd = (coef[k, 0:16] for k in range(4))
    near, far = [None] * 3, [None] * 3
    for k, c in enumerate((1, 0, 2)):
        lower, upper = (v[0:16] for v in row_shift(delta[k]))
        here = delta[k][0:16]
        geometric = gu * (upper - here) - gd * (here - lower)
        near[c] = 2.0 * here + a * near_lap[k] + b * near_coup[k] - geometric
        far[c] = a * far_lap[k] + b * far_coup[k]
    return near, far


def tail_pe_kernel(coef, got, own, inner, out, half, held, sems):
    right = parity("plan")
    start = pl.multiple_of(jnp.where(right, 0, 8), 8)
    copies = [pltpu.make_async_copy(inner.at[c, :, pl.ds(start, 8), :], out.at[c, :, pl.ds(start, 8), :], sems.at[c]) for c in range(3)]
    for copy in copies:
        copy.start()
    near, far = one_side(coef, got, held, own, side_sign(right))

    def finish(row, next_row, first):
        mine = list(copies)
        for c in range(3):
            half[c] = inner[c, :, first : first + 8, :]
            half[c, :, row - first, :] += near[c]
            half[c, :, next_row - first, :] += far[c]
            mine.append(pltpu.make_async_copy(half.at[c], out.at[c, :, pl.ds(first, 8), :], sems.at[3 + c]))
            mine[-1].start()
        for copy in mine:
            copy.wait()

    @pl.when(right)
    def _():
        finish(15, 14, 8)

    @pl.when(jnp.logical_not(right))
    def _():
        finish(0, 1, 0)


def tail_po_kernel(coef, got, own, base, before, out, work, held, sems):
    right = jnp.logical_not(parity("plan"))
    near, far = one_side(coef, got, held, own, side_sign(right))

    def finish(row, next_row, first):
        last = []
        for c in range(3):
            work[c, :, row, :] = base[0, c] + near[c]
            work[c, :, next_row, :] = base[1, c] + far[c]
            rows = pl.ds(min(row, next_row), 2)
            last.append(pltpu.make_async_copy(work.at[c, :, rows, :], out.at[c, :, pl.ds(first + min(row, next_row), 2), :], sems.at[3 + c]))
            last[-1].start()
        for copy in last:
            copy.wait()

    @pl.when(right)
    def _():
        finish(7, 6, 8)

    @pl.when(jnp.logical_not(right))
    def _():
        finish(0, 1, 0)


VM = pl.BlockSpec(memory_space=pltpu.VMEM)
HB = pl.BlockSpec(memory_space=pltpu.HBM)


def shape(*dims):
    return jax.ShapeDtypeStruct(dims, F32)


def call(kernel, outs, ins, scratch=(), flops=0, moved=0, grant=24.0, places=None, aliases=None):
    return pl.pallas_call(
        kernel,
        out_shape=outs,
        in_specs=ins,
        out_specs=places or [VM] * len(outs),
        scratch_shapes=list(scratch),
        input_output_aliases=aliases or {},
        compiler_params=pltpu.CompilerParams(vmem_limit_bytes=int(grant * 2**20)),
        cost_estimate=pl.CostEstimate(flops=flops, bytes_accessed=moved, transcendentals=0),
    )


def local(u_now, u_prev, occupancy, materials, shear_table, lame_table, density_table):
    height = u_now.shape[1] * lax.axis_size("story")
    stories = lax.axis_size("story")
    face, table = shape(9, 16, WIDE), shape(4, PAD, WIDE)
    rows = 3 * PAD + 48
    planes = [pltpu.VMEM((3 * PAD, WIDE), F32)] * 2
    small = [v.reshape(1, -1) for v in (occupancy, materials, shear_table, lame_table, density_table)]
    small_so, se, so, blocks = call(
        functools.partial(slice_kernel, factor=0.8 / height),
        [shape(9, 4, WIDE), face, shape(10, 16, WIDE), shape(stories, 128)],
        [HB] * 7,
        [pltpu.VMEM(v.shape, v.dtype) for v in small] + [pltpu.VMEM((8, 128), F32), pltpu.VMEM((stories, 128), F32), pltpu.SemaphoreType.DMA((18,))],
        moved=1 << 20,
        places=[VM, VM, VM, HB],
    )(*(pltpu.with_memory_space_constraint(v, pltpu.HBM) for v in [u_now, u_prev] + small))
    small_got = swap(small_so, "story", 1)
    so_got = swap(so, "story", 1)
    se_got = swap(se, "story", 0)
    blocks = lax.all_to_all(blocks, "story", 0, 0, tiled=True)
    cells = u_now.shape
    layers = shape(9 * 16, WIDE)
    po_layers, pe_layers, token = call(planes_kernel, [layers, layers, shape(8, 128)], [VM] * 2, flops=1_000_000_000, moved=16 << 20)(u_now, u_prev)
    coef, consts = call(expand_kernel, [table, shape(16, WIDE)], [VM] * 2, flops=20_000_000_000, moved=1 << 30)(blocks, token)
    (po,) = call(pack_po_kernel, [shape(rows, WIDE)], [VM] * 5, planes, moved=1 << 20)(consts, coef, se_got, small_got, po_layers)
    po_got = swap(po, "plan", 1)
    levels = [
        pltpu.VMEM((3, 20, 16, WIDE), F32),
        pltpu.VMEM((3, 18, 16, WIDE), F32),
        pltpu.VMEM((3, 18, 16, WIDE), F32),
    ]
    (pe,) = call(pack_pe_kernel, [shape(rows - 1, WIDE)], [VM] * 5, planes, moved=1 << 20)(consts, coef, se_got, small_got, pe_layers)
    pe_got = swap(pe, "plan", 0)
    side = shape(6, PAD, WIDE)
    inner, base, pe_own, po_own = call(
        main_kernel, [shape(*cells), shape(2, 3, 16, WIDE), side, side], [VM] * 8, levels, flops=60_000_000, moved=4 << 20
    )(consts, coef, se_got, so_got, u_now, u_prev, pe, po)
    held = pltpu.VMEM((3 * PAD, WIDE), F32)
    half = pltpu.VMEM((3, 16, 8, WIDE), F32)
    (out,) = call(
        tail_pe_kernel,
        [shape(*cells)],
        [VM] * 4,
        [half, held, pltpu.SemaphoreType.DMA((6,))],
        flops=5_000_000,
        moved=2 << 20,
        places=[HB],
    )(coef, pe_got, pe_own, inner)
    (out,) = call(
        tail_po_kernel,
        [shape(*cells)],
        [VM] * 4 + [HB],
        [half, held, pltpu.SemaphoreType.DMA((6,))],
        flops=5_000_000,
        moved=2 << 20,
        places=[HB],
        aliases={4: 0},
    )(coef, po_got, po_own, base, out)
    return out


def solution(mesh):
    in_specs = (
        P(None, "story", "plan", None),
        P(None, "story", "plan", None),
        P("story", "plan", None),
        P("story", "plan", None),
        P(),
        P(),
        P(),
    )
    out_specs = P(None, "story", "plan", None)
    return jax.shard_map(local, mesh=mesh, in_specs=in_specs, out_specs=out_specs, check_vma=False)
```

```python
import functools

import jax
import jax.numpy as jnp
from jax import lax
from jax.experimental import pallas as pl
from jax.experimental.pallas import tpu as pltpu
from jax.sharding import PartitionSpec as P

BLOCK = 16
WIDE = 256
PAD = 24
F32 = jnp.float32


def swap(values, axis, first):
    pairs = []
    for low in range(first, lax.axis_size(axis) - 1, 2):
        pairs += [(low, low + 1), (low + 1, low)]
    return lax.ppermute(values, axis, pairs)


def row_shift(v):
    count = v.shape[0] // 8
    row = lax.broadcasted_iota(jnp.int32, (8, v.shape[1]), 0)
    tiles = [v[8 * k : 8 * k + 8] for k in range(count)]
    down, up = [pltpu.roll(t, 1, 0) for t in tiles], [pltpu.roll(t, 7, 0) for t in tiles]
    zero = jnp.zeros_like(tiles[0])
    around = v.shape[0] == PAD
    down, up = [down[-1] if around else zero] + down, up + [up[0] if around else zero]
    lower = [jnp.where(row == 0, down[k], down[k + 1]) for k in range(count)]
    upper = [jnp.where(row == 7, up[k + 1], up[k]) for k in range(count)]
    return jnp.concatenate(lower, 0), jnp.concatenate(upper, 0)


def lane_shift(v):
    half = WIDE // 2
    lane = lax.broadcasted_iota(jnp.int32, (v.shape[0], half), 1)
    first, second = v[:, :half], v[:, half:]
    first_down, second_down = pltpu.roll(first, 1, 1), pltpu.roll(second, 1, 1)
    first_up, second_up = pltpu.roll(first, half - 1, 1), pltpu.roll(second, half - 1, 1)
    lower = [jnp.where(lane == 0, 0.0, first_down), jnp.where(lane == 0, first_down, second_down)]
    upper = [jnp.where(lane == half - 1, second_up, first_up), jnp.where(lane == half - 1, 0.0, second_up)]
    return jnp.concatenate(lower, 1), jnp.concatenate(upper, 1)


def lane_smooth(v):
    lower, upper = lane_shift(v)
    return lower + upper + 4.0 * v


def lane_first(v):
    lower, upper = lane_shift(v)
    return upper - lower


def total(terms):
    terms = [t for t in terms if t is not None]
    return functools.reduce(lambda p, q: p + q, terms)


def stencil(below, here, above, sign=None):
    zs, zf = [], []
    for j in range(3):
        zs.append(total([below and below[j], above and above[j], here and 4.0 * here[j]]))
        if below and above:
            zf.append(above[j] - below[j])
        else:
            zf.append(above[j] if above else -below[j])
    if sign is not None:
        zf = [sign * v for v in zf]
    zs_sh = [row_shift(v) for v in zs]
    zf_sh = [row_shift(v) for v in zf]
    s_zs = [lo + up + 4.0 * v for (lo, up), v in zip(zs_sh, zs)]
    lap = []
    if here:
        s_mid = [lo + up + 4.0 * v for (lo, up), v in zip([row_shift(v) for v in here], here)]
        inner = [s_zs[j] - 2.0 * (s_mid[j] + zs[j]) for j in range(3)]
        curl = 2.0 * s_zs[0] - 12.0 * s_mid[0]
    else:
        inner = [s_zs[j] - 2.0 * zs[j] for j in range(3)]
        curl = 2.0 * s_zs[0]
    for j in range(3):
        lap.append(lane_smooth(inner[j]) - 2.0 * s_zs[j])
    f_zf0 = zf_sh[0][1] - zf_sh[0][0]
    f_zf1 = zf_sh[1][1] - zf_sh[1][0]
    s_zf0 = zf_sh[0][0] + zf_sh[0][1] + 4.0 * zf[0]
    s_zf2 = zf_sh[2][0] + zf_sh[2][1] + 4.0 * zf[2]
    f_zs1 = zs_sh[1][1] - zs_sh[1][0]
    f_zs2 = zs_sh[2][1] - zs_sh[2][0]
    c0 = lane_smooth(curl + 3.0 * f_zf1) + lane_first(3.0 * s_zf2)
    c1 = lane_smooth(2.0 * s_zs[1] - 12.0 * zs[1] + 3.0 * f_zf0) + lane_first(3.0 * f_zs2)
    c2 = lane_first(3.0 * (s_zf0 + f_zs1)) + 2.0 * lane_smooth(s_zs[2]) - 12.0 * s_zs[2]
    return lap, [c0, c1, c2]


def heights():
    row = lax.broadcasted_iota(jnp.int32, (PAD, WIDE), 0)
    return jnp.where(row > 20, row - PAD, row)


def coefficients(own, over, under, carried):
    z = heights()
    zf = z.astype(F32)

    def pick(k):
        return jnp.where(z < 0, under[k], jnp.where(z > 15, over[k], own[k]))

    a, b, g = pick(0), pick(1), pick(2)
    mass, mass_over, mass_under = own[3], over[3], under[3]
    upper = jnp.where(z > 15, carried - mass_over, carried + mass * (15.0 - zf))
    lower = jnp.where(z < 0, carried + 16.0 * mass + mass_under, carried + mass * (16.0 - zf))
    return a, b, g * upper, g * lower


def parity(axis):
    return lax.axis_index(axis) % 2 == 0


def slice_kernel(now, prev, occ_h, mat_h, shear_h, lame_h, dens_h, small, se, so, blocks, occ, mat, shear_t, lame_t, dens_t, held, held_blocks, sems, *, factor):
    even = parity("story")
    smalls = []
    for k, (source, target) in enumerate(((occ_h, occ), (mat_h, mat), (shear_h, shear_t), (lame_h, lame_t), (dens_h, dens_t))):
        smalls.append(pltpu.make_async_copy(source, target, sems.at[6 + k]))
    copies = []
    for k, out in enumerate((se, so)):
        top = jnp.logical_xor(even, k == 1)
        near, far = jnp.where(top, 15, 0), jnp.where(top, 14, 1)
        for j, (source, z) in enumerate(((now, near), (now, far), (prev, near))):
            copies.append(pltpu.make_async_copy(source.at[:, z], out.at[pl.ds(3 * j, 3)], sems.at[3 * k + j]))
            if k == 1:
                for h, x in enumerate((0, 14)):
                    rows = small.at[pl.ds(3 * j, 3), pl.ds(2 * h, 2), :]
                    copies.append(pltpu.make_async_copy(source.at[:, z, pl.ds(x, 2), :], rows, sems.at[12 + 2 * j + h]))
    for copy in smalls + copies:
        copy.start()
    for copy in smalls:
        copy.wait()
    segment = lax.broadcasted_iota(jnp.int32, (8, 128), 1) // BLOCK

    def repeat(ref):
        held[...] = jnp.zeros((8, 128), F32)
        held[0:1, 0:BLOCK] = ref[...].astype(F32)
        once = held[...]
        return once + sum(pltpu.roll(once, BLOCK * k, 1) for k in range(1, 5))

    occupied, which = repeat(occ), repeat(mat)
    found = []
    for table in (shear_t, lame_t, dens_t):
        value = jnp.zeros((8, 128), F32)
        for k in range(table.shape[1]):
            value = jnp.where(which == k, table[0:1, k : k + 1], value)
        found.append(value)
    shear, lame, dens = found
    scale = occupied * (0.1 / dens)
    parts = (scale * shear * (1.0 / 12.0), scale * (lame + shear) * (1.0 / 72.0), scale * factor, dens * occupied, occupied)
    row = jnp.zeros((8, 128), F32)
    for k, part in enumerate(parts):
        row = jnp.where(segment == k, part, row)
    held_blocks[...] = jnp.broadcast_to(row[0:1], held_blocks.shape)
    copies.append(pltpu.make_async_copy(held_blocks, blocks, sems.at[11]))
    copies[-1].start()
    for copy in copies:
        copy.wait()


def ghost_of(se, so, consts):
    even = parity("story")

    def ghost(over, plane, *where):
        take = even if over else jnp.logical_not(even)
        row = 9 if over else 14
        return jnp.where(take, se[(plane,) + where], so[(plane,) + where]) * consts[row : row + 1, :]

    return ghost


def edge_of(se, small, consts):
    even = parity("story")

    def edge(over, plane, x):
        take = even if over else jnp.logical_not(even)
        row = 9 if over else 14
        at = x % 12
        return jnp.where(take, se[plane, x : x + 1, :], small[plane, at : at + 1, :]) * consts[row : row + 1, :]

    return edge


def planes_kernel(now, prev, po, pe, token):
    even = parity("plan")
    token[...] = jnp.zeros(token.shape, F32)

    def load(out, near, far):
        for k, (source, x) in enumerate(((now, near), (now, far), (prev, near))):
            for c in range(3):
                base = (3 * k + c) * 16
                out[base : base + 16, :] = source[c, :, x, :]

    @pl.when(even)
    def _():
        load(pe, 15, 14)
        load(po, 0, 1)

    @pl.when(jnp.logical_not(even))
    def _():
        load(pe, 0, 1)
        load(po, 15, 14)


def fill(right, edge, consts, coef, layers, out, far_rows, prev_rows):
    occupied = consts[4:5, :]

    def load(near, far):
        for kind, (target, x, sides) in enumerate(((out, near, (0, 3)), (far_rows, far, (0, 3)), (prev_rows, near, (6,)))):
            for c in range(3):
                base = c * PAD
                at = (3 * kind + c) * 16
                target[base : base + 16, :] = layers[at : at + 16, :] * occupied
                for k, side in enumerate(sides):
                    target[base + 23 - k : base + 24 - k, :] = edge(False, side + c, x)
                    target[base + 16 + k : base + 17 + k, :] = edge(True, side + c, x)

    @pl.when(right)
    def _():
        load(15, 14)

    @pl.when(jnp.logical_not(right))
    def _():
        load(0, 1)

    order = (1, 0, 2)

    def planes(ref):
        return [ref[c * PAD : (c + 1) * PAD, :] for c in order]

    first = advance(planes(far_rows), planes(out), None, planes(prev_rows), [coef[k] for k in range(4)], jnp.where(right, 1.0, -1.0))
    lane = lax.broadcasted_iota(jnp.int32, (1, WIDE), 1)
    for k, c in enumerate(order):
        count = 16 if c < 2 else 15
        out[3 * PAD + 16 * c : 3 * PAD + 16 * c + count, :] = first[k][0:count]
        out[c * PAD + 18 : c * PAD + 19, :] = first[k][23:24]
        out[c * PAD + 19 : c * PAD + 20, :] = first[k][16:17]
    out[2 * PAD + 21 : 2 * PAD + 22, :] = first[order.index(2)][15:16]
    for k, row in enumerate((20, 21)):
        out[row : row + 1, :] = consts[k : k + 1, :]
        out[PAD + row : PAD + row + 1, :] = jnp.where(lane % 2 == 0, consts[5 + k : 6 + k, :], consts[10 + k : 11 + k, :])


def expand_kernel(blocks, token, coef, consts):
    place = lax.axis_index("story")
    step = lax.broadcasted_iota(jnp.int32, blocks.shape, 0)
    rows = [jnp.sum(jnp.where(step == place + k, blocks[...], 0.0), 0, keepdims=True) for k in (0, 1, -1)]
    rows.append(16.0 * jnp.sum(jnp.where(step > place, blocks[...], 0.0), 0, keepdims=True))
    stacked = jnp.concatenate(rows + [jnp.zeros((4, 128), F32)], 0)
    lane = lax.broadcasted_iota(jnp.int32, (8, 128), 1) // BLOCK

    def spread(k):
        halves = [jnp.take_along_axis(stacked, lane + (BLOCK * k + 8 * h), 1, mode="promise_in_bounds") for h in (0, 1)]
        return jnp.concatenate(halves, 1)

    sets = [[], [], []]
    for k in range(5):
        wide = spread(k)
        for j in range(3):
            sets[j].append(wide[j : j + 1])
            consts[5 * j + k : 5 * j + k + 1, :] = wide[j : j + 1]
        if k == 3:
            carried = wide[3:4]
    consts[15:16, :] = carried
    for k, value in enumerate(coefficients(sets[0], sets[1], sets[2], carried)):
        coef[k] = value


def pack_po_kernel(consts, coef, se, small, layers, po, far_rows, prev_rows):
    fill(jnp.logical_not(parity("plan")), edge_of(se, small, consts), consts, coef, layers, po, far_rows, prev_rows)


def advance(below, here, above, before, coefs, sign):
    a, b, gu, gd = coefs
    lap, coup = stencil(below, here, above, sign)
    news = []
    for c in range(3):
        lower, upper = row_shift(here[c])
        news.append(update(here[c], before[c], lap[c], coup[c], a, b, gu, gd, lower, upper))
    return news


def update(here, before, lap, coup, a, b, gu, gd, below, above):
    geometric = gu * (above - here) - gd * (here - below)
    return 2.0 * here - before + a * lap + b * coup - geometric


def both_steps(consts, coef, se, so, now, prev, out, u0, u1, before):
    ghost = ghost_of(se, so, consts)
    occupied = jnp.broadcast_to(consts[4:5, :], (16, WIDE))
    for c in range(3):
        u0[c, 0] = ghost(False, 3 + c)
        u0[c, 1] = ghost(False, c)
        u0[c, 18] = ghost(True, c)
        u0[c, 19] = ghost(True, 3 + c)
        before[c, 0] = ghost(False, 6 + c)
        before[c, 17] = ghost(True, 6 + c)

    @pl.loop(0, 16, unroll=4)
    def _(z):
        for c in range(3):
            u0[c, z + 2] = now[c, z] * occupied
            before[c, z + 1] = prev[c, z] * occupied

    def one(source, earlier, target, i, z):
        below, here, above = ([source[c, i + k] for c in range(3)] for k in range(3))
        lap, coup = stencil(below, here, above)
        a, b, gu, gd = (coef[k, pl.ds(z, 1), :] for k in range(4))
        for c in range(3):
            target[c, i] = update(here[c], earlier(c, i), lap[c], coup[c], a, b, gu, gd, below[c], above[c])

    @pl.loop(0, 18, unroll=6)
    def _(i):
        one(u0, lambda c, i: before[c, i], u1, i, jnp.where(i == 0, PAD - 1, i - 1))

    @pl.loop(0, 16, unroll=8)
    def _(i):
        one(u1, lambda c, i: u0[c, i + 2], out, i, i)


def pack_pe_kernel(consts, coef, se, small, layers, pe, far_rows, prev_rows):
    fill(parity("plan"), edge_of(se, small, consts), consts, coef, layers, pe, far_rows, prev_rows)


def planes_of(ref):
    return [ref[c * PAD : (c + 1) * PAD, :] for c in (1, 0, 2)]


def side_sign(right):
    return jnp.where(right, 1.0, -1.0)


def main_kernel(consts, coef, se, so, now, prev, pe_sent, po_sent, inner, base, pe_own, po_own, u0, u1, before):
    right = parity("plan")
    both_steps(consts, coef, se, so, now, prev, inner, u0, u1, before)
    for sent, own, sign in ((pe_sent, pe_own, side_sign(right)), (po_sent, po_own, -side_sign(right))):
        for k, v in enumerate(sum(stencil(planes_of(sent), None, None, sign), [])):
            own[k] = v

    def finish(near, far):
        for c in range(3):
            base[0, c] = inner[c, :, near, :]
            base[1, c] = inner[c, :, far, :]

    @pl.when(right)
    def _():
        finish(0, 1)

    @pl.when(jnp.logical_not(right))
    def _():
        finish(15, 14)


def rows_of(v):
    lower, upper = row_shift(v)
    return lower + upper + 4.0 * v, upper - lower


def outer_terms(layer, sign):
    (v0, s0, f0), (v1, s1, f1), (v2, s2, f2) = layer
    lap = [lane_smooth(s - 2.0 * v) - 2.0 * s for v, s, _ in layer]
    c0 = lane_smooth(2.0 * s0 + (3.0 * sign) * f1) + lane_first((3.0 * sign) * s2)
    c1 = lane_smooth(2.0 * s1 - 12.0 * v1 + (3.0 * sign) * f0) + lane_first(3.0 * f2)
    c2 = lane_first(3.0 * (sign * s0 + f1)) + 2.0 * lane_smooth(s2) - 12.0 * s2
    return lap, [c0, c1, c2]


def both_terms(here, outer, sign):
    zs = [o[0] + 4.0 * h[0] for h, o in zip(here, outer)]
    s_zs = [o[1] + 4.0 * h[1] for h, o in zip(here, outer)]
    f_zs = [o[2] + 4.0 * h[2] for h, o in zip(here, outer)]
    lap = [lane_smooth(s_zs[j] - 2.0 * (here[j][1] + zs[j])) - 2.0 * s_zs[j] for j in range(3)]
    c0 = lane_smooth(2.0 * s_zs[0] - 12.0 * here[0][1] + (3.0 * sign) * outer[1][2]) + lane_first((3.0 * sign) * outer[2][1])
    c1 = lane_smooth(2.0 * s_zs[1] - 12.0 * zs[1] + (3.0 * sign) * outer[0][2]) + lane_first(3.0 * f_zs[2])
    c2 = lane_first(3.0 * (sign * outer[0][1] + f_zs[1])) + 2.0 * lane_smooth(s_zs[2]) - 12.0 * s_zs[2]
    return lap, [c0, c1, c2]


def one_side(coef, got, held, own, sign):
    for c in range(3):
        base = c * PAD
        count = 16 if c < 2 else 15
        held[base : base + count, :] = got[3 * PAD + 16 * c : 3 * PAD + 16 * c + count, :]
        held[base + 16 : base + 17, :] = got[base + 19 : base + 20, :]
        held[base + 23 : base + 24, :] = got[base + 18 : base + 19, :]
    held[2 * PAD + 15 : 2 * PAD + 16, :] = got[2 * PAD + 21 : 2 * PAD + 22, :]
    a, b, gu, gd = (coef[k] for k in range(4))
    z = heights()
    even = lax.broadcasted_iota(jnp.int32, (8, WIDE), 1) % 2 == 0

    def pick(row):
        mixed = jnp.broadcast_to(got[PAD + row : PAD + row + 1, :], (8, WIDE))
        lower, upper = lane_shift(mixed)
        over = jnp.where(even, mixed, lower)[0:1]
        under = jnp.where(even, upper, mixed)[0:1]
        return jnp.where(z < 0, under, jnp.where(z > 15, over, got[row : row + 1, :]))

    got_a, got_b = pick(20), pick(21)
    lap, coup = outer_terms([(v,) + rows_of(v) for v in planes_of(got)], sign)
    delta = [a * lap[k] + b * coup[k] for k in range(3)]
    outer = [p + got_a * own[k] + got_b * own[3 + k] for k, p in enumerate(planes_of(held))]
    delta_rows = [tuple(p[0:16] for p in (v,) + rows_of(v)) for v in delta]
    outer_rows = [tuple(p[0:16] for p in (v,) + rows_of(v)) for v in outer]
    far_lap, far_coup = outer_terms(delta_rows, sign)
    near_lap, near_coup = both_terms(delta_rows, outer_rows, sign)
    a, b, gu, gd = (coef[k, 0:16] for k in range(4))
    near, far = [None] * 3, [None] * 3
    for k, c in enumerate((1, 0, 2)):
        lower, upper = (v[0:16] for v in row_shift(delta[k]))
        here = delta[k][0:16]
        geometric = gu * (upper - here) - gd * (here - lower)
        near[c] = 2.0 * here + a * near_lap[k] + b * near_coup[k] - geometric
        far[c] = a * far_lap[k] + b * far_coup[k]
    return near, far


def tail_pe_kernel(coef, got, own, inner, out, half, held, sems):
    right = parity("plan")
    start = pl.multiple_of(jnp.where(right, 0, 8), 8)
    copies = [pltpu.make_async_copy(inner.at[c, :, pl.ds(start, 8), :], out.at[c, :, pl.ds(start, 8), :], sems.at[c]) for c in range(3)]
    for copy in copies:
        copy.start()
    near, far = one_side(coef, got, held, own, side_sign(right))

    def finish(row, next_row, first):
        mine = list(copies)
        for c in range(3):
            half[c] = inner[c, :, first : first + 8, :]
            half[c, :, row - first, :] += near[c]
            half[c, :, next_row - first, :] += far[c]
            mine.append(pltpu.make_async_copy(half.at[c], out.at[c, :, pl.ds(first, 8), :], sems.at[3 + c]))
            mine[-1].start()
        for copy in mine:
            copy.wait()

    @pl.when(right)
    def _():
        finish(15, 14, 8)

    @pl.when(jnp.logical_not(right))
    def _():
        finish(0, 1, 0)


def tail_po_kernel(coef, got, own, base, before, out, work, held, sems):
    right = jnp.logical_not(parity("plan"))
    near, far = one_side(coef, got, held, own, side_sign(right))

    def finish(row, next_row, first):
        last = []
        for c in range(3):
            work[c, :, row, :] = base[0, c] + near[c]
            work[c, :, next_row, :] = base[1, c] + far[c]
            rows = pl.ds(min(row, next_row), 2)
            last.append(pltpu.make_async_copy(work.at[c, :, rows, :], out.at[c, :, pl.ds(first + min(row, next_row), 2), :], sems.at[3 + c]))
            last[-1].start()
        for copy in last:
            copy.wait()

    @pl.when(right)
    def _():
        finish(7, 6, 8)

    @pl.when(jnp.logical_not(right))
    def _():
        finish(0, 1, 0)


VM = pl.BlockSpec(memory_space=pltpu.VMEM)
HB = pl.BlockSpec(memory_space=pltpu.HBM)


def shape(*dims):
    return jax.ShapeDtypeStruct(dims, F32)


def call(kernel, outs, ins, scratch=(), flops=0, moved=0, grant=24.0, places=None, aliases=None):
    return pl.pallas_call(
        kernel,
        out_shape=outs,
        in_specs=ins,
        out_specs=places or [VM] * len(outs),
        scratch_shapes=list(scratch),
        input_output_aliases=aliases or {},
        compiler_params=pltpu.CompilerParams(vmem_limit_bytes=int(grant * 2**20)),
        cost_estimate=pl.CostEstimate(flops=flops, bytes_accessed=moved, transcendentals=0),
    )


def local(u_now, u_prev, occupancy, materials, shear_table, lame_table, density_table):
    height = u_now.shape[1] * lax.axis_size("story")
    stories = lax.axis_size("story")
    face, table = shape(9, 16, WIDE), shape(4, PAD, WIDE)
    rows = 3 * PAD + 48
    planes = [pltpu.VMEM((3 * PAD, WIDE), F32)] * 2
    small = [v.reshape(1, -1) for v in (occupancy, materials, shear_table, lame_table, density_table)]
    small_so, se, so, blocks = call(
        functools.partial(slice_kernel, factor=0.8 / height),
        [shape(9, 4, WIDE), shape(10, 16, WIDE), face, shape(stories, 128)],
        [HB] * 7,
        [pltpu.VMEM(v.shape, v.dtype) for v in small] + [pltpu.VMEM((8, 128), F32), pltpu.VMEM((stories, 128), F32), pltpu.SemaphoreType.DMA((18,))],
        moved=1 << 20,
        places=[VM, VM, VM, HB],
    )(*(pltpu.with_memory_space_constraint(v, pltpu.HBM) for v in [u_now, u_prev] + small))
    small_got = swap(small_so, "story", 1)
    so_got = swap(so, "story", 1)
    se_got = swap(se, "story", 0)
    blocks = lax.all_to_all(blocks, "story", 0, 0, tiled=True)
    cells = u_now.shape
    layers = shape(9 * 16, WIDE)
    po_layers, pe_layers, token = call(planes_kernel, [layers, layers, shape(8, 128)], [VM] * 2, flops=1_000_000_000, moved=16 << 20)(u_now, u_prev)
    coef, consts = call(expand_kernel, [table, shape(16, WIDE)], [VM] * 2, flops=20_000_000_000, moved=1 << 30)(blocks, token)
    (po,) = call(pack_po_kernel, [shape(rows, WIDE)], [VM] * 5, planes, moved=1 << 20)(consts, coef, se_got, small_got, po_layers)
    po_got = swap(po, "plan", 1)
    levels = [
        pltpu.VMEM((3, 20, 16, WIDE), F32),
        pltpu.VMEM((3, 18, 16, WIDE), F32),
        pltpu.VMEM((3, 18, 16, WIDE), F32),
    ]
    (pe,) = call(pack_pe_kernel, [shape(rows - 1, WIDE)], [VM] * 5, planes, moved=1 << 20)(consts, coef, se_got, small_got, pe_layers)
    pe_got = swap(pe, "plan", 0)
    side = shape(6, PAD, WIDE)
    inner, base, pe_own, po_own = call(
        main_kernel, [shape(*cells), shape(2, 3, 16, WIDE), side, side], [VM] * 8, levels, flops=60_000_000, moved=4 << 20
    )(consts, coef, se_got, so_got, u_now, u_prev, pe, po)
    held = pltpu.VMEM((3 * PAD, WIDE), F32)
    half = pltpu.VMEM((3, 16, 8, WIDE), F32)
    (out,) = call(
        tail_pe_kernel,
        [shape(*cells)],
        [VM] * 4,
        [half, held, pltpu.SemaphoreType.DMA((6,))],
        flops=5_000_000,
        moved=2 << 20,
        places=[HB],
    )(coef, pe_got, pe_own, inner)
    (out,) = call(
        tail_po_kernel,
        [shape(*cells)],
        [VM] * 4 + [HB],
        [half, held, pltpu.SemaphoreType.DMA((6,))],
        flops=5_000_000,
        moved=2 << 20,
        places=[HB],
        aliases={4: 0},
    )(coef, po_got, po_own, base, out)
    return out


def solution(mesh):
    in_specs = (
        P(None, "story", "plan", None),
        P(None, "story", "plan", None),
        P("story", "plan", None),
        P("story", "plan", None),
        P(),
        P(),
        P(),
    )
    out_specs = P(None, "story", "plan", None)
    return jax.shard_map(local, mesh=mesh, in_specs=in_specs, out_specs=out_specs, check_vma=False)
```
